32 devices in a mesh: ens: 8 (over z, core), pen: 4 (over y, x).
Axes of the slice: x: 2, y: 2, z: 4, core: 2. Of those that a mesh axis runs over, the one named last changes fastest.
Arguments:
- state: float32 [2, 8, 4, 256, 512], P(None, 'ens', None, 'pen'), may hold values from -8 to 8, as said below
- accum: float32 [2, 8, 4, 256, 512], P(None, 'ens', None, 'pen'), may hold values from -8 to 8, as said below
- base_flow: float32 [6, 4, 256, 256], P(None, None, 'pen', 'ens'), may hold values from -6 to 6
Outputs:
- state_next: float32 [2, 8, 4, 256, 512], P(None, 'ens', None, 'pen')
- accum_next: float32 [2, 8, 4, 256, 512], P(None, 'ens', None, 'pen')
The draws below stay inside these ranges and needn't reach their ends.
Inputs may be any that keep to these rules, and one draw needn't show every extreme that they name: `state`: each field of each perturbation and level is the spectrum of a real field: the entry at ((256 - ky) mod 256, (256 - kx) mod 256) is the complex conjugate of the entry at (ky, kx). `accum`: each field of each perturbation and level is the spectrum of a real field: the entry at ((256 - ky) mod 256, (256 - kx) mod 256) is the complex conjugate of the entry at (ky, kx).
All inputs are finite; a program needn't handle non-finite values.
Results may differ from the reference program's by a relative error of at most 0.0003.
Values sent between devices are 32-bit elements; how exact they have to be, the bound alone decides.
No kernel may reach another device: no remote copies, remote signals or barrier semaphores. Data moves between devices by JAX's collectives and lax.ppermute only.
A program may use at most 64 MiB of HBM per device.

```python
import math
import jax
import jax.numpy as jnp
from jax import lax

GRID = 256
LEVELS = 4
PERTS = 8


def reflect(values):
    return jnp.roll(jnp.flip(values, axis=(-1, -2)), 1, axis=(-1, -2))


def hermitian(key):
    full_shape = (2, PERTS, LEVELS, GRID, GRID)
    key_real, key_imag = jax.random.split(key)
    real_part = 1.4142 * jax.random.truncated_normal(key_real, -5.0, 5.0, full_shape, jnp.float32)
    imag_part = 1.4142 * jax.random.truncated_normal(key_imag, -5.0, 5.0, full_shape, jnp.float32)
    real_part = 0.5 * (real_part + reflect(real_part))
    imag_part = 0.5 * (imag_part - reflect(imag_part))
    return jnp.concatenate([real_part, imag_part], axis=-1)


def draw_state(key, part):
    return hermitian(jax.random.fold_in(key, 11))


def draw_accum(key, part):
    return hermitian(jax.random.fold_in(key, 23))


def levels(rng, extent, cuts, least, largest):
    def one(dim, shards_of):
        heights = jax.random.uniform(jax.random.fold_in(jax.random.fold_in(rng, 6), dim), (shards_of,), jnp.float32, least / len(cuts), largest / len(cuts))
        return jnp.repeat(jnp.exp(heights), extent[dim] // shards_of).reshape((-1,) + (1,) * (len(extent) - dim - 1))

    level = one(*cuts[0])
    for cut in cuts[1:]:
        level = level * one(*cut)
    return level


def noise(key, extent, width, bound, cuts=(), held_as=jnp.bfloat16):
    values = jax.random.normal(key, extent, jnp.float32) * width
    if len(cuts) > 0:
        values = levels(key, extent, cuts, -0.22, 0.18) * values
    return jnp.clip(values, min=-bound, max=bound).astype(held_as)


def setup_inputs(seed: int = 0) -> dict:
    seeds = jax.random.split(jax.random.key(seed), 4)
    state = draw_state(jax.random.fold_in(seeds[3], 71), 0)
    accum = draw_accum(jax.random.fold_in(seeds[3], 71), 0)
    base_flow = noise(seeds[2], (6, LEVELS, GRID, GRID), 1.0, 6.0, ((2, 4), (3, 8)), jnp.float32)
    return dict(state=state, accum=accum, base_flow=base_flow)


viscosity = 0.05
diffusivity = 0.05
vertical_mixing = 0.5
buoyancy_gain = 0.5
stratification = 0.5
memory_factor = -5.0 / 9.0
weight_factor = 15.0 / 16.0
time_step = 0.4


def wave_numbers(amount, offset, length):
    position = offset + jnp.arange(amount, dtype=jnp.int32)
    half_length = length // 2
    signed = jnp.where(position <= half_length, position, position - length)
    derivative = jnp.where(position == half_length, 0, signed)
    return (2.0 * math.pi / length) * derivative.astype(jnp.float32), signed


def times_i(real_part, imag_part, factor):
    return -factor * imag_part, factor * real_part


def vertical(quantity, level_axis):
    depth = quantity.shape[level_axis]
    lower = lax.slice_in_dim(quantity, 0, 1, axis=level_axis)
    upper = lax.slice_in_dim(quantity, depth - 1, depth, axis=level_axis)
    padded = jnp.concatenate([lower, quantity, upper], axis=level_axis)
    above = lax.slice_in_dim(padded, 2, depth + 2, axis=level_axis)
    below = lax.slice_in_dim(padded, 0, depth, axis=level_axis)
    return above + below - 2.0 * quantity


def tendency(vort, buoy, advect, across, kappa_x, square, level_axis):
    tend_vort_re = (-advect[0] + buoyancy_gain * (-kappa_x * buoy[1]) - viscosity * square * vort[0]
                    + vertical_mixing * vertical(vort[0], level_axis))
    tend_vort_im = (-advect[1] + buoyancy_gain * (kappa_x * buoy[0]) - viscosity * square * vort[1]
                    + vertical_mixing * vertical(vort[1], level_axis))
    tend_buoy_re = (-advect[2] - stratification * across[0] - diffusivity * square * buoy[0]
                    + vertical_mixing * vertical(buoy[0], level_axis))
    tend_buoy_im = (-advect[3] - stratification * across[1] - diffusivity * square * buoy[1]
                    + vertical_mixing * vertical(buoy[1], level_axis))
    return jnp.stack([jnp.concatenate([tend_vort_re, tend_vort_im], axis=-1),
                      jnp.concatenate([tend_buoy_re, tend_buoy_im], axis=-1)])


def physical(spectral_pair):
    joined = spectral_pair[0] + 1j * spectral_pair[1]
    return jnp.real(jnp.fft.ifft2(jnp.swapaxes(joined, -1, -2), norm="ortho"))


def spectrum(quantity):
    result = jnp.swapaxes(jnp.fft.fft2(quantity, norm="ortho"), -1, -2)
    return jnp.real(result), jnp.imag(result)


def reference(state, accum, base_flow):
    def one_member(member_pair):
        member, memory = member_pair
        kappa, signed = wave_numbers(GRID, 0, GRID)
        kappa_y = kappa[:, None]
        kappa_x = kappa[None, :]
        wave_square = signed[:, None] ** 2 + signed[None, :] ** 2
        factor = (2.0 * math.pi / GRID) ** 2
        square = factor * wave_square.astype(jnp.float32)
        inverse = jnp.where(wave_square > 0, 1.0 / (factor * jnp.maximum(wave_square, 1).astype(jnp.float32)), 0.0)
        vort = (member[0][..., :GRID], member[0][..., GRID:])
        buoy = (member[1][..., :GRID], member[1][..., GRID:])
        potential_re = -vort[0] * inverse
        potential_im = -vort[1] * inverse
        flow_x = times_i(potential_re, potential_im, -kappa_y)
        flow_y = times_i(potential_re, potential_im, kappa_x)
        vort_x = times_i(vort[0], vort[1], kappa_x)
        vort_y = times_i(vort[0], vort[1], kappa_y)
        buoy_x = times_i(buoy[0], buoy[1], kappa_x)
        buoy_y = times_i(buoy[0], buoy[1], kappa_y)
        flow_x_p = physical(flow_x)
        flow_y_p = physical(flow_y)
        vort_x_p = physical(vort_x)
        vort_y_p = physical(vort_y)
        buoy_x_p = physical(buoy_x)
        buoy_y_p = physical(buoy_y)
        advect_vort = (base_flow[0] * vort_x_p + base_flow[1] * vort_y_p
                       + flow_x_p * base_flow[2] + flow_y_p * base_flow[3])
        advect_buoy = (base_flow[0] * buoy_x_p + base_flow[1] * buoy_y_p
                       + flow_x_p * base_flow[4] + flow_y_p * base_flow[5])
        vort_hat = spectrum(advect_vort)
        buoy_hat = spectrum(advect_buoy)
        advect = (vort_hat[0], vort_hat[1], buoy_hat[0], buoy_hat[1])
        tend = tendency(vort, buoy, advect, flow_y, kappa_x, square, 0)
        memory_next = memory_factor * memory + tend
        return member + weight_factor * time_step * memory_next, memory_next

    members = (jnp.moveaxis(state, 1, 0), jnp.moveaxis(accum, 1, 0))
    state_next, accum_next = lax.map(one_member, members)
    return jnp.moveaxis(state_next, 0, 1), jnp.moveaxis(accum_next, 0, 1)
```

```python
import functools
import math

import jax
import jax.numpy as jnp
import ml_dtypes
import numpy as np
from jax import lax
from jax.experimental import pallas as pl
from jax.experimental.pallas import tpu as pltpu
from jax.sharding import PartitionSpec as P

viscosity = 0.05
diffusivity = 0.05
vertical_mixing = 0.5
buoyancy_gain = 0.5
stratification = 0.5
memory_factor = -5.0 / 9.0
weight_factor = 15.0 / 16.0
time_step = 0.4


def wave_numbers(amount, offset, length):
    position = offset + jnp.arange(amount, dtype=jnp.int32)
    half_length = length // 2
    signed = jnp.where(position <= half_length, position, position - length)
    derivative = jnp.where(position == half_length, 0, signed)
    return (2.0 * math.pi / length * derivative.astype(jnp.float32), signed)


def times_i(real_part, imag_part, factor):
    return (-factor * imag_part, factor * real_part)


def vertical(quantity, level_axis):
    depth = quantity.shape[level_axis]
    lower = lax.slice_in_dim(quantity, 0, 1, axis=level_axis)
    upper = lax.slice_in_dim(quantity, depth - 1, depth, axis=level_axis)
    padded = jnp.concatenate([lower, quantity, upper], axis=level_axis)
    above = lax.slice_in_dim(padded, 2, depth + 2, axis=level_axis)
    below = lax.slice_in_dim(padded, 0, depth, axis=level_axis)
    return above + below - 2.0 * quantity


def tendency(vort, buoy, advect, across, kappa_x, square, level_axis):
    tend_vort_re = (
        -advect[0]
        + buoyancy_gain * (-kappa_x * buoy[1])
        - viscosity * square * vort[0]
        + vertical_mixing * vertical(vort[0], level_axis)
    )
    tend_vort_im = (
        -advect[1]
        + buoyancy_gain * (kappa_x * buoy[0])
        - viscosity * square * vort[1]
        + vertical_mixing * vertical(vort[1], level_axis)
    )
    tend_buoy_re = (
        -advect[2]
        - stratification * across[0]
        - diffusivity * square * buoy[0]
        + vertical_mixing * vertical(buoy[0], level_axis)
    )
    tend_buoy_im = (
        -advect[3]
        - stratification * across[1]
        - diffusivity * square * buoy[1]
        + vertical_mixing * vertical(buoy[1], level_axis)
    )
    return jnp.stack(
        [
            jnp.concatenate([tend_vort_re, tend_vort_im], axis=-1),
            jnp.concatenate([tend_buoy_re, tend_buoy_im], axis=-1),
        ]
    )


def dft_tables(length):
    position = jnp.arange(length, dtype=jnp.int32)
    product = position[:, None] * position[None, :] % length
    angle = 2.0 * math.pi / length * product.astype(jnp.float32)
    scale = 1.0 / math.sqrt(length)
    return (scale * jnp.cos(angle), scale * jnp.sin(angle))


def to_physical(spectral, x_table, y_table):
    mixed_space = jnp.einsum(
        "fplkj,jcx->fplcxk", spectral, x_table, precision=lax.Precision.HIGHEST
    )
    return jnp.einsum(
        "fplcxk,ckm->fplxm",
        lax.all_to_all(mixed_space, "pen", split_axis=4, concat_axis=5, tiled=True),
        y_table,
        precision=lax.Precision.HIGHEST,
    )


def on_device_general(state, accum, base_flow):
    grid_size = state.shape[-1] // 2
    row_count = state.shape[3]
    base_all = lax.all_gather(base_flow, "ens", axis=3, tiled=True)
    kappa_rows, signed_y = wave_numbers(row_count, lax.axis_index("pen") * row_count, grid_size)
    kappa_cols, signed_x = wave_numbers(grid_size, 0, grid_size)
    kappa_y = kappa_rows[:, None]
    kappa_x = kappa_cols[None, :]
    wave_square = signed_y[:, None] ** 2 + signed_x[None, :] ** 2
    factor = (2.0 * math.pi / grid_size) ** 2
    square = factor * wave_square.astype(jnp.float32)
    inverse = jnp.where(
        wave_square > 0, 1.0 / (factor * jnp.maximum(wave_square, 1).astype(jnp.float32)), 0.0
    )
    vort = (state[0][..., :grid_size], state[0][..., grid_size:])
    buoy = (state[1][..., :grid_size], state[1][..., grid_size:])
    potential_re = -vort[0] * inverse
    potential_im = -vort[1] * inverse
    flow_x = times_i(potential_re, potential_im, -kappa_y)
    flow_y = times_i(potential_re, potential_im, kappa_x)
    vort_x = times_i(vort[0], vort[1], kappa_x)
    vort_y = times_i(vort[0], vort[1], kappa_y)
    buoy_x = times_i(buoy[0], buoy[1], kappa_x)
    buoy_y = times_i(buoy[0], buoy[1], kappa_y)
    cosine_table, sine_table = dft_tables(grid_size)
    x_table = jnp.concatenate(
        [
            jnp.stack([cosine_table, sine_table], axis=1),
            jnp.stack([-sine_table, cosine_table], axis=1),
        ],
        axis=0,
    )
    y_table = jnp.stack([cosine_table, -sine_table])
    components = [flow_x, flow_y, vort_x, vort_y, buoy_x, buoy_y]
    spectral = jnp.stack([jnp.concatenate(component, axis=-1) for component in components])
    physical = to_physical(spectral, x_table, y_table)
    flow_x_p, flow_y_p = (physical[0], physical[1])
    vort_x_p, vort_y_p = (physical[2], physical[3])
    buoy_x_p, buoy_y_p = (physical[4], physical[5])
    advect_vort = (
        base_all[0] * vort_x_p
        + base_all[1] * vort_y_p
        + flow_x_p * base_all[2]
        + flow_y_p * base_all[3]
    )
    advect_buoy = (
        base_all[0] * buoy_x_p
        + base_all[1] * buoy_y_p
        + flow_x_p * base_all[4]
        + flow_y_p * base_all[5]
    )
    advect_both = jnp.stack([advect_vort, advect_buoy])
    y_forward = jnp.stack([cosine_table, -sine_table], axis=1)
    x_forward = jnp.stack(
        [
            jnp.concatenate([cosine_table, -sine_table], axis=1),
            jnp.concatenate([sine_table, cosine_table], axis=1),
        ]
    )
    spread = jnp.einsum(
        "fplxy,yck->fplckx", advect_both, y_forward, precision=lax.Precision.HIGHEST
    )
    spectra = jnp.einsum(
        "fplckx,cxm->fplkm",
        lax.all_to_all(spread, "pen", split_axis=4, concat_axis=5, tiled=True),
        x_forward,
        precision=lax.Precision.HIGHEST,
    )
    advect = (
        spectra[0][..., :grid_size],
        spectra[0][..., grid_size:],
        spectra[1][..., :grid_size],
        spectra[1][..., grid_size:],
    )
    tend = tendency(vort, buoy, advect, flow_y, kappa_x, square, 1)
    accum_next = memory_factor * accum + tend
    state_next = state + weight_factor * time_step * accum_next
    return (state_next, accum_next)


PEN = 4
EXTRA = 8


def split(values):
    high = values.astype(jnp.bfloat16)
    return high, (values - high.astype(jnp.float32)).astype(jnp.bfloat16)


def split_table(values):
    high = values.astype(ml_dtypes.bfloat16)
    low = (values - high.astype(np.float64)).astype(ml_dtypes.bfloat16)
    return np.stack([high, low])


def x_table(grid):
    angle = 2.0 * np.pi / grid * (np.outer(np.arange(grid), np.arange(grid)) % grid)
    return split_table(np.concatenate([np.cos(angle), np.sin(angle)], axis=1) / math.sqrt(grid))


def y_inverse_table(grid):
    rows = grid // PEN
    y = np.arange(grid)[:, None]
    halves = []
    for half in range(2):
        columns = []
        for slot in range(2):
            ky = (half * 2 + slot) * rows + np.arange(rows)[None, :]
            angle = 2.0 * np.pi / grid * (y * ky % grid)
            real = np.where(ky % (grid // 2) == 0, 1.0, 2.0) * np.cos(angle)
            imag = -2.0 * np.sin(angle)
            if slot == 0:
                other = (1 - half) * (grid // 2)
                imag[:, 0] = np.cos(2.0 * np.pi / grid * (y[:, 0] * other % grid))
            columns += [real, imag]
        halves.append(np.concatenate(columns, axis=1))
    return split_table(np.stack(halves) / math.sqrt(grid))


def y_forward_table(grid):
    rows = grid // PEN
    parts = []
    for device in range(PEN):
        ky = device * rows + np.arange(rows)[:, None]
        angle = 2.0 * np.pi / grid * (ky * np.arange(grid)[None, :] % grid)
        parts += [np.cos(angle), -np.sin(angle)]
    return split_table(np.concatenate(parts, axis=0) / math.sqrt(grid))


def dot(left, right):
    return jnp.dot(left, right, preferred_element_type=jnp.float32)


def dot_table(values, table_ref):
    high, low = split(values)
    return dot(high, table_ref[0]) + (dot(low, table_ref[0]) + dot(high, table_ref[1]))


def waves(position, grid):
    signed = jnp.where(position <= grid // 2, position, position - grid)
    derivative = jnp.where(position == grid // 2, 0, signed)
    return (2.0 * math.pi / grid) * derivative.astype(jnp.float32), signed


def wave_arrays(row_position, grid):
    kappa_y, signed_y = waves(row_position, grid)
    kappa_x, signed_x = waves(lax.broadcasted_iota(jnp.int32, (1, grid), 1), grid)
    wave_square = signed_y * signed_y + signed_x * signed_x
    factor = (2.0 * math.pi / grid) ** 2
    square = factor * wave_square.astype(jnp.float32)
    inverse = jnp.where(wave_square > 0, 1.0 / jnp.where(wave_square > 0, square, 1.0), 0.0)
    return kappa_y, kappa_x, square, inverse


def relayout_kernel(base_ref, first_ref, second_ref):
    cut = first_ref.shape[1]
    turned = base_ref[...].T
    first_ref[...] = turned[:, :cut]
    second_ref[...] = turned[:, cut:]


def x_inverse_kernel(grid, state_ref, table_ref, *refs):
    first, second, scratch = refs[:PEN], refs[PEN : 2 * PEN], refs[2 * PEN]
    rows = state_ref.shape[3]
    pen = lax.axis_index("pen")
    half = pen // 2
    row = lax.broadcasted_iota(jnp.int32, (rows + EXTRA, 1), 0)
    kappa_y, kappa_x, _, inverse = wave_arrays(
        pen * rows + jnp.where(row < rows, row, row - rows), grid
    )
    low_lanes = lax.broadcasted_iota(jnp.int32, (1, 128), 1) < 64

    def part(field, level, columns):
        return jnp.concatenate(
            [
                state_ref[field, 0, 2 * half + level, :, columns],
                state_ref[field, 0, 2 * (1 - half) + level, :EXTRA, columns],
            ],
            axis=0,
        )

    real, imag = slice(0, grid), slice(grid, 2 * grid)
    fields = [
        (0, inverse, kappa_y),
        (0, -kappa_x * inverse, None),
        (0, kappa_x, None),
        (0, None, kappa_y),
        (1, kappa_x, None),
        (1, None, kappa_y),
    ]
    count = rows + EXTRA
    for index, (field, before, after) in enumerate(fields):
        stacked = []
        for level in range(2):
            for columns in (real, imag):
                values = part(field, level, columns)
                stacked.append(values if before is None else values * before)
        product = dot_table(jnp.concatenate(stacked, axis=0), table_ref)
        for level in range(2):
            top = product[2 * level * count : (2 * level + 1) * count]
            bottom = product[(2 * level + 1) * count : (2 * level + 2) * count]
            out_real = -(bottom[:, :grid] + top[:, grid:])
            out_imag = top[:, :grid] - bottom[:, grid:]
            if after is not None:
                out_real, out_imag = after * out_real, after * out_imag
            scratch[level, :count, :] = out_real
            scratch[level, count:, :] = out_imag[:rows]
        for step in range(PEN):
            target = pen ^ step
            columns = pl.ds(pl.multiple_of((target // 2) * 128, 128), 128)
            odd = target % 2 == 1
            left, right = scratch[0, :, columns], scratch[1, :, columns]
            message = jnp.where(
                low_lanes,
                jnp.where(odd, pltpu.roll(left, 64, 1), left),
                jnp.where(odd, right, pltpu.roll(right, 64, 1)),
            )
            if index < 4:
                first[step][:, 128 * index : 128 * (index + 1)] = message
            else:
                second[step][:, 128 * (index - 4) : 128 * (index - 3)] = message


def fill_spectrum(messages, extra_ref, high_ref, low_ref, rows):
    pen = lax.axis_index("pen")
    for step in range(PEN):
        extra_ref[pen ^ step] = messages[step][rows : rows + EXTRA, :]
    first_row = lax.broadcasted_iota(jnp.int32, (rows, 1), 0) == 0
    for step in range(PEN):
        source = pen ^ step
        real = messages[step][:rows, :]
        imag = messages[step][rows + EXTRA :, :]
        other = extra_ref[source ^ 2][0:1, :]
        imag = jnp.where(jnp.logical_and(first_row, source % 2 == 0), other, imag)
        high, low = split(jnp.concatenate([real, imag], axis=0))
        place = pl.ds(pl.multiple_of((source % 2) * 2 * rows, 2 * rows), 2 * rows)
        high_ref[source // 2, place, :] = high
        low_ref[source // 2, place, :] = low


def y_inverse(table_ref, high_ref, low_ref, half):
    return dot(table_ref[0, half], high_ref[half]) + (
        dot(table_ref[0, half], low_ref[half]) + dot(table_ref[1, half], high_ref[half])
    )


def y_forward(table_ref, adv_high, adv_low, outs, rows):
    pen = lax.axis_index("pen")
    for step in range(PEN):
        place = pl.ds(pl.multiple_of((pen ^ step) * 2 * rows, 2 * rows), 2 * rows)
        high, low = table_ref[0, place, :], table_ref[1, place, :]
        outs[step][...] = dot(high, adv_high[...]) + (
            dot(high, adv_low[...]) + dot(low, adv_high[...])
        )


def vorticity_kernel(masks, rows, *refs):
    refs = list(refs)
    messages, blocks = refs[:PEN], refs[PEN : PEN + len(masks)]
    inverse_ref, forward_ref = refs[PEN + len(masks) : PEN + len(masks) + 2]
    outs = refs[PEN + len(masks) + 2 :]
    flow_ref, outs = outs[0], outs[1:]
    results, (extra_ref, high_ref, low_ref, field_ref, adv_high, adv_low) = outs[:PEN], outs[PEN:]
    fill_spectrum(messages, extra_ref, high_ref, low_ref, rows)
    for half in range(2):
        field_ref[half] = y_inverse(inverse_ref, high_ref, low_ref, half)
    ens = lax.axis_index("ens")
    tall = blocks[0].shape[0]
    for mask, block in zip(masks, blocks, strict=True):
        place = pl.ds(pl.multiple_of((ens ^ mask) * tall, tall), tall)
        for half in range(2):

            def base(index, half=half, block=block):
                return block[:, 256 * index + 128 * half : 256 * index + 128 * half + 128]

            def field(index, half=half, place=place):
                return field_ref[half, place, 128 * index : 128 * index + 128]

            flow_x, flow_y = field(0), field(1)
            total = (
                base(0) * field(2) + base(1) * field(3) + flow_x * base(2) + flow_y * base(3)
            )
            high, low = split(total)
            adv_high[place, 128 * half : 128 * half + 128] = high
            adv_low[place, 128 * half : 128 * half + 128] = low
            flow_ref[half, place, :128] = flow_x
            flow_ref[half, place, 128:] = flow_y
    y_forward(forward_ref, adv_high, adv_low, results, rows)


def buoyancy_kernel(masks, rows, *refs):
    refs = list(refs)
    count = len(masks)
    messages, blocks, more_blocks = refs[:PEN], refs[PEN : PEN + count], refs[PEN + count : PEN + 2 * count]
    flow_ref, inverse_ref, forward_ref = refs[PEN + 2 * count : PEN + 2 * count + 3]
    outs = refs[PEN + 2 * count + 3 :]
    results, (extra_ref, high_ref, low_ref, field_ref, adv_high, adv_low) = outs[:PEN], outs[PEN:]
    fill_spectrum(messages, extra_ref, high_ref, low_ref, rows)
    for half in range(2):
        field_ref[half] = y_inverse(inverse_ref, high_ref, low_ref, half)
    ens = lax.axis_index("ens")
    tall = blocks[0].shape[0]
    for mask, block, more in zip(masks, blocks, more_blocks, strict=True):
        place = pl.ds(pl.multiple_of((ens ^ mask) * tall, tall), tall)
        for half in range(2):

            def base(ref, index, half=half):
                return ref[:, 256 * index + 128 * half : 256 * index + 128 * half + 128]

            total = (
                base(block, 0) * field_ref[half, place, :128]
                + base(block, 1) * field_ref[half, place, 128:]
                + flow_ref[half, place, :128] * base(more, 0)
                + flow_ref[half, place, 128:] * base(more, 1)
            )
            high, low = split(total)
            adv_high[place, 128 * half : 128 * half + 128] = high
            adv_low[place, 128 * half : 128 * half + 128] = low
    y_forward(forward_ref, adv_high, adv_low, results, rows)


def x_forward(messages, gathered, left, table_ref, rows):
    pen = lax.axis_index("pen")
    for step in range(PEN):
        gathered[pen ^ step] = messages[step][...]
    low_lanes = lax.broadcasted_iota(jnp.int32, (1, 128), 1) < 64
    for half in range(2):
        lanes = slice(128 * half, 128 * half + 128)
        for pair in range(2):
            even, odd = gathered[2 * pair, :, lanes], gathered[2 * pair + 1, :, lanes]
            columns = slice(128 * pair, 128 * pair + 128)
            left[2 * half, :, columns] = jnp.where(low_lanes, even, pltpu.roll(odd, 64, 1))
            left[2 * half + 1, :, columns] = jnp.where(low_lanes, pltpu.roll(even, 64, 1), odd)
    levels = left.shape[0]
    product = dot_table(left[...].reshape(levels * 2 * rows, left.shape[2]), table_ref)
    grid = left.shape[2]
    spectra = []
    for level in range(levels):
        top = product[2 * level * rows : (2 * level + 1) * rows]
        bottom = product[(2 * level + 1) * rows : (2 * level + 2) * rows]
        spectra.append(
            (top[:, :grid] + bottom[:, grid:], bottom[:, :grid] - top[:, grid:])
        )
    return spectra


def final_kernel(grid, *refs):
    vort_messages, buoy_messages = refs[:PEN], refs[PEN : 2 * PEN]
    state_ref, accum_ref, table_ref, state_out, accum_out, gathered, left = refs[2 * PEN :]
    rows = state_ref.shape[3]
    levels = state_ref.shape[2]
    pen = lax.axis_index("pen")
    row = lax.broadcasted_iota(jnp.int32, (rows, 1), 0)
    _, kappa_x, square, inverse = wave_arrays(pen * rows + row, grid)
    real, imag = slice(0, grid), slice(grid, 2 * grid)

    def mixing(field, level, columns):
        here = state_ref[field, 0, level, :, columns]
        above = state_ref[field, 0, min(level + 1, levels - 1), :, columns]
        below = state_ref[field, 0, max(level - 1, 0), :, columns]
        return above + below - 2.0 * here

    def store(field, level, columns, tend):
        memory = memory_factor * accum_ref[field, 0, level, :, columns] + tend
        accum_out[field, 0, level, :, columns] = memory
        state_out[field, 0, level, :, columns] = (
            state_ref[field, 0, level, :, columns] + weight_factor * time_step * memory
        )

    for field, messages in enumerate((vort_messages, buoy_messages)):
        spectra = x_forward(messages, gathered, left, table_ref, rows)
        for level in range(levels):
            for columns, other, sign, advect in (
                (real, imag, 1.0, spectra[level][0]),
                (imag, real, -1.0, spectra[level][1]),
            ):
                cross = state_ref[1 - field, 0, level, :, other]
                if field == 0:
                    coupling = (-sign * buoyancy_gain) * (kappa_x * cross)
                else:
                    coupling = (-sign * stratification) * (kappa_x * inverse * cross)
                damping = viscosity if field == 0 else diffusivity
                tend = (
                    -advect
                    + coupling
                    - damping * square * state_ref[field, 0, level, :, columns]
                    + vertical_mixing * mixing(field, level, columns)
                )
                store(field, level, columns, tend)


def exchange(values, axis, size, mask):
    return lax.ppermute(values, axis, [(index, index ^ mask) for index in range(size)])


def gather_blocks(block, size):
    held = {0: block}
    bit = size // 2
    while bit >= 1:
        mask = 2 * bit - 1 if bit > 1 else 1
        mask = mask & ~1 if bit > 1 else 1
        for offset in list(held):
            held[offset ^ mask] = exchange(held[offset], "ens", size, mask)
        bit //= 2
    return held


def call(kernel, outs, scratch, flops, args, limit=40):
    total = sum(math.prod(a.shape) * a.dtype.itemsize for a in list(args) + list(outs))
    return pl.pallas_call(
        kernel,
        out_shape=outs,
        in_specs=[pl.BlockSpec(memory_space=pltpu.VMEM)] * len(args),
        out_specs=[pl.BlockSpec(memory_space=pltpu.VMEM)] * len(outs),
        scratch_shapes=scratch,
        compiler_params=pltpu.CompilerParams(vmem_limit_bytes=limit * 1024 * 1024),
        cost_estimate=pl.CostEstimate(flops=flops, bytes_accessed=total, transcendentals=0),
    )(*args)


def on_device(axes, state, accum, base_flow):
    grid, rows, levels = state.shape[-1] // 2, state.shape[3], state.shape[2]
    if axes["pen"] != PEN or levels != 4 or grid != 256 or axes["ens"] & (axes["ens"] - 1):
        return on_device_general(state, accum, base_flow)
    f32 = jnp.float32
    shape = functools.partial(jax.ShapeDtypeStruct, dtype=f32)
    fields, _, wide, tall = base_flow.shape
    lanes = levels * wide
    table = jnp.asarray(x_table(grid))
    inverse = jnp.asarray(y_inverse_table(grid))
    forward = jnp.asarray(y_forward_table(grid))

    first, second = call(
        relayout_kernel,
        [shape((tall, 4 * lanes)), shape((tall, 2 * lanes))],
        [],
        0,
        [base_flow.reshape(fields * lanes, tall)],
    )
    message_rows = 2 * rows + EXTRA
    spectra = call(
        functools.partial(x_inverse_kernel, grid),
        [shape((message_rows, 512))] * PEN + [shape((message_rows, 256))] * PEN,
        [pltpu.VMEM((2, message_rows, grid), f32)],
        6 * 6 * 2 * 2 * 2 * (rows + EXTRA) * grid * grid,
        [state, table],
    )
    first_blocks = gather_blocks(first, axes["ens"])
    vort_in = [spectra[0]] + [exchange(spectra[step], "pen", PEN, step) for step in range(1, PEN)]
    second_blocks = gather_blocks(second, axes["ens"])
    buoy_in = [spectra[PEN]] + [
        exchange(spectra[PEN + step], "pen", PEN, step) for step in range(1, PEN)
    ]
    masks = tuple(first_blocks)

    def scratch(width):
        return [
            pltpu.VMEM((PEN, EXTRA, width), f32),
            pltpu.VMEM((2, grid, width), jnp.bfloat16),
            pltpu.VMEM((2, grid, width), jnp.bfloat16),
            pltpu.VMEM((2, grid, width), f32),
            pltpu.VMEM((grid, lanes), jnp.bfloat16),
            pltpu.VMEM((grid, lanes), jnp.bfloat16),
        ]

    flow, *vort_out = call(
        functools.partial(vorticity_kernel, masks, rows),
        [shape((2, grid, 256))] + [shape((2 * rows, lanes))] * PEN,
        scratch(512),
        6 * 2 * grid * grid * 512 + 6 * 2 * grid * grid * lanes,
        vort_in + [first_blocks[mask] for mask in masks] + [inverse, forward],
    )
    vort_back = [vort_out[0]] + [
        exchange(vort_out[step], "pen", PEN, step) for step in range(1, PEN)
    ]
    buoy_out = call(
        functools.partial(buoyancy_kernel, masks, rows),
        [shape((2 * rows, lanes))] * PEN,
        scratch(256),
        6 * 2 * grid * grid * 256 + 6 * 2 * grid * grid * lanes,
        buoy_in
        + [first_blocks[mask] for mask in masks]
        + [second_blocks[mask] for mask in masks]
        + [flow, inverse, forward],
    )
    buoy_back = [buoy_out[0]] + [
        exchange(buoy_out[step], "pen", PEN, step) for step in range(1, PEN)
    ]
    state_next, accum_next = call(
        functools.partial(final_kernel, grid),
        [shape(state.shape), shape(accum.shape)],
        [pltpu.VMEM((PEN, 2 * rows, lanes), f32), pltpu.VMEM((levels, 2 * rows, grid), f32)],
        6 * 2 * levels * 2 * rows * grid * 2 * grid,
        vort_back + buoy_back + [state, accum, table],
    )
    return state_next, accum_next


def solution(mesh):
    return jax.shard_map(
        functools.partial(on_device, dict(mesh.shape)),
        mesh=mesh,
        in_specs=(
            P(None, "ens", None, "pen", None),
            P(None, "ens", None, "pen", None),
            P(None, None, "pen", "ens"),
        ),
        out_specs=(P(None, "ens", None, "pen", None), P(None, "ens", None, "pen", None)),
        check_vma=False,
    )
```

```python
import functools
import math

import jax
import jax.numpy as jnp
import ml_dtypes
import numpy as np
from jax import lax
from jax.experimental import pallas as pl
from jax.experimental.pallas import tpu as pltpu
from jax.sharding import PartitionSpec as P

viscosity = 0.05
diffusivity = 0.05
vertical_mixing = 0.5
buoyancy_gain = 0.5
stratification = 0.5
memory_factor = -5.0 / 9.0
weight_factor = 15.0 / 16.0
time_step = 0.4


def wave_numbers(amount, offset, length):
    position = offset + jnp.arange(amount, dtype=jnp.int32)
    half_length = length // 2
    signed = jnp.where(position <= half_length, position, position - length)
    derivative = jnp.where(position == half_length, 0, signed)
    return (2.0 * math.pi / length * derivative.astype(jnp.float32), signed)


def times_i(real_part, imag_part, factor):
    return (-factor * imag_part, factor * real_part)


def vertical(quantity, level_axis):
    depth = quantity.shape[level_axis]
    lower = lax.slice_in_dim(quantity, 0, 1, axis=level_axis)
    upper = lax.slice_in_dim(quantity, depth - 1, depth, axis=level_axis)
    padded = jnp.concatenate([lower, quantity, upper], axis=level_axis)
    above = lax.slice_in_dim(padded, 2, depth + 2, axis=level_axis)
    below = lax.slice_in_dim(padded, 0, depth, axis=level_axis)
    return above + below - 2.0 * quantity


def tendency(vort, buoy, advect, across, kappa_x, square, level_axis):
    tend_vort_re = (
        -advect[0]
        + buoyancy_gain * (-kappa_x * buoy[1])
        - viscosity * square * vort[0]
        + vertical_mixing * vertical(vort[0], level_axis)
    )
    tend_vort_im = (
        -advect[1]
        + buoyancy_gain * (kappa_x * buoy[0])
        - viscosity * square * vort[1]
        + vertical_mixing * vertical(vort[1], level_axis)
    )
    tend_buoy_re = (
        -advect[2]
        - stratification * across[0]
        - diffusivity * square * buoy[0]
        + vertical_mixing * vertical(buoy[0], level_axis)
    )
    tend_buoy_im = (
        -advect[3]
        - stratification * across[1]
        - diffusivity * square * buoy[1]
        + vertical_mixing * vertical(buoy[1], level_axis)
    )
    return jnp.stack(
        [
            jnp.concatenate([tend_vort_re, tend_vort_im], axis=-1),
            jnp.concatenate([tend_buoy_re, tend_buoy_im], axis=-1),
        ]
    )


def dft_tables(length):
    position = jnp.arange(length, dtype=jnp.int32)
    product = position[:, None] * position[None, :] % length
    angle = 2.0 * math.pi / length * product.astype(jnp.float32)
    scale = 1.0 / math.sqrt(length)
    return (scale * jnp.cos(angle), scale * jnp.sin(angle))


def to_physical(spectral, x_table, y_table):
    mixed_space = jnp.einsum(
        "fplkj,jcx->fplcxk", spectral, x_table, precision=lax.Precision.HIGHEST
    )
    return jnp.einsum(
        "fplcxk,ckm->fplxm",
        lax.all_to_all(mixed_space, "pen", split_axis=4, concat_axis=5, tiled=True),
        y_table,
        precision=lax.Precision.HIGHEST,
    )


def on_device_general(state, accum, base_flow):
    grid_size = state.shape[-1] // 2
    row_count = state.shape[3]
    base_all = lax.all_gather(base_flow, "ens", axis=3, tiled=True)
    kappa_rows, signed_y = wave_numbers(row_count, lax.axis_index("pen") * row_count, grid_size)
    kappa_cols, signed_x = wave_numbers(grid_size, 0, grid_size)
    kappa_y = kappa_rows[:, None]
    kappa_x = kappa_cols[None, :]
    wave_square = signed_y[:, None] ** 2 + signed_x[None, :] ** 2
    factor = (2.0 * math.pi / grid_size) ** 2
    square = factor * wave_square.astype(jnp.float32)
    inverse = jnp.where(
        wave_square > 0, 1.0 / (factor * jnp.maximum(wave_square, 1).astype(jnp.float32)), 0.0
    )
    vort = (state[0][..., :grid_size], state[0][..., grid_size:])
    buoy = (state[1][..., :grid_size], state[1][..., grid_size:])
    potential_re = -vort[0] * inverse
    potential_im = -vort[1] * inverse
    flow_x = times_i(potential_re, potential_im, -kappa_y)
    flow_y = times_i(potential_re, potential_im, kappa_x)
    vort_x = times_i(vort[0], vort[1], kappa_x)
    vort_y = times_i(vort[0], vort[1], kappa_y)
    buoy_x = times_i(buoy[0], buoy[1], kappa_x)
    buoy_y = times_i(buoy[0], buoy[1], kappa_y)
    cosine_table, sine_table = dft_tables(grid_size)
    x_table = jnp.concatenate(
        [
            jnp.stack([cosine_table, sine_table], axis=1),
            jnp.stack([-sine_table, cosine_table], axis=1),
        ],
        axis=0,
    )
    y_table = jnp.stack([cosine_table, -sine_table])
    components = [flow_x, flow_y, vort_x, vort_y, buoy_x, buoy_y]
    spectral = jnp.stack([jnp.concatenate(component, axis=-1) for component in components])
    physical = to_physical(spectral, x_table, y_table)
    flow_x_p, flow_y_p = (physical[0], physical[1])
    vort_x_p, vort_y_p = (physical[2], physical[3])
    buoy_x_p, buoy_y_p = (physical[4], physical[5])
    advect_vort = (
        base_all[0] * vort_x_p
        + base_all[1] * vort_y_p
        + flow_x_p * base_all[2]
        + flow_y_p * base_all[3]
    )
    advect_buoy = (
        base_all[0] * buoy_x_p
        + base_all[1] * buoy_y_p
        + flow_x_p * base_all[4]
        + flow_y_p * base_all[5]
    )
    advect_both = jnp.stack([advect_vort, advect_buoy])
    y_forward = jnp.stack([cosine_table, -sine_table], axis=1)
    x_forward = jnp.stack(
        [
            jnp.concatenate([cosine_table, -sine_table], axis=1),
            jnp.concatenate([sine_table, cosine_table], axis=1),
        ]
    )
    spread = jnp.einsum(
        "fplxy,yck->fplckx", advect_both, y_forward, precision=lax.Precision.HIGHEST
    )
    spectra = jnp.einsum(
        "fplckx,cxm->fplkm",
        lax.all_to_all(spread, "pen", split_axis=4, concat_axis=5, tiled=True),
        x_forward,
        precision=lax.Precision.HIGHEST,
    )
    advect = (
        spectra[0][..., :grid_size],
        spectra[0][..., grid_size:],
        spectra[1][..., :grid_size],
        spectra[1][..., grid_size:],
    )
    tend = tendency(vort, buoy, advect, flow_y, kappa_x, square, 1)
    accum_next = memory_factor * accum + tend
    state_next = state + weight_factor * time_step * accum_next
    return (state_next, accum_next)


PEN = 4
HALF_ROWS = 32
EXTRA = 8


def split(values):
    high = values.astype(jnp.bfloat16)
    return high, (values - high.astype(jnp.float32)).astype(jnp.bfloat16)


def split_table(values):
    high = values.astype(ml_dtypes.bfloat16)
    low = (values - high.astype(np.float64)).astype(ml_dtypes.bfloat16)
    return np.stack([high, low], axis=-3)


def cosine(grid, left, right):
    return np.cos(2.0 * np.pi / grid * (left * right % grid)) / math.sqrt(grid)


def sine(grid, left, right):
    return np.sin(2.0 * np.pi / grid * (left * right % grid)) / math.sqrt(grid)


def x_forward_table(grid):
    kx = np.arange(grid)
    x = kx[:, None]
    return split_table(np.concatenate([cosine(grid, x, kx), sine(grid, x, kx)], axis=1))


def x_inverse_table(grid):
    rows = grid // PEN
    kx = np.arange(grid)[:, None]
    tables = []
    for device in range(PEN):
        x = np.concatenate([block * rows + np.arange(rows) for block in (device, device ^ 2)])
        tables.append(np.concatenate([cosine(grid, kx, x), sine(grid, kx, x)], axis=1))
    return split_table(np.stack(tables))


def row_numbers(device, rows):
    own = device * rows + np.arange(rows)
    near = [(device ^ step) * rows + np.arange(HALF_ROWS) for step in (1, 2)]
    return np.concatenate([own] + near)


def y_inverse_table(grid):
    rows = grid // PEN
    y = np.arange(grid)[:, None]
    tables = []
    for device in range(PEN):
        ky = row_numbers(device, rows)
        real = np.where(ky % (grid // 2) == 0, 1.0, 2.0) * cosine(grid, y, ky)
        imag = -2.0 * sine(grid, y, ky)
        extra = (device ^ 2) * rows + HALF_ROWS
        far = (device ^ 3) * rows
        from_y = rows + HALF_ROWS
        extra_real, extra_imag = 2.0 * cosine(grid, y[:, 0], extra), -2.0 * sine(grid, y[:, 0], extra)
        imag[:, from_y] = extra_imag
        if device % 2 == 0:
            imag[:, 0] = extra_real
        else:
            real[:, from_y] = extra_real
            imag[:, rows] = cosine(grid, y[:, 0], far)
        tables.append(np.concatenate([real, imag], axis=1))
    return split_table(np.stack(tables))


def y_forward_table(grid):
    rows = grid // PEN
    parts = []
    for device in range(PEN):
        ky = device * rows + np.arange(rows)[:, None]
        y = np.arange(grid)[None, :]
        parts += [cosine(grid, ky, y), -sine(grid, ky, y)]
    return split_table(np.concatenate(parts, axis=0))


def dot(left, right):
    return jnp.dot(left, right, preferred_element_type=jnp.float32)


def dot_split(left, right):
    return dot(left[0], right[0]) + (dot(left[1], right[0]) + dot(left[0], right[1]))


def waves(position, grid):
    signed = jnp.where(position <= grid // 2, position, position - grid)
    derivative = jnp.where(position == grid // 2, 0, signed)
    return (2.0 * math.pi / grid) * derivative.astype(jnp.float32), signed


def wave_arrays(row_position, grid):
    kappa_y, signed_y = waves(row_position, grid)
    kappa_x, signed_x = waves(lax.broadcasted_iota(jnp.int32, (1, grid), 1), grid)
    wave_square = signed_y * signed_y + signed_x * signed_x
    factor = (2.0 * math.pi / grid) ** 2
    square = factor * wave_square.astype(jnp.float32)
    inverse = jnp.where(wave_square > 0, 1.0 / jnp.where(wave_square > 0, square, 1.0), 0.0)
    return kappa_y, kappa_x, square, inverse


def interleave(even, odd):
    low_lanes = lax.broadcasted_iota(jnp.int32, (1, 128), 1) < 64
    return (
        jnp.where(low_lanes, even, pltpu.roll(odd, 64, 1)),
        jnp.where(low_lanes, pltpu.roll(even, 64, 1), odd),
    )


def base_kernel(base_ref, own_ref, swap_ref):
    mine = (lax.axis_index("pen") // 2) * 2
    for out_ref, first in ((own_ref, mine), (swap_ref, 2 - mine)):
        for field in range(base_ref.shape[0]):
            out_ref[:, 128 * field : 128 * field + 128] = jnp.concatenate(
                [base_ref[field, first], base_ref[field, first + 1]], axis=1
            )


def state_kernel(state_ref, near_x_ref, near_y_ref, far_ref):
    mine = (lax.axis_index("pen") // 2) * 2
    far_ref[...] = jnp.zeros_like(far_ref)
    near_y_ref[4 * HALF_ROWS :, :] = jnp.zeros((EXTRA, near_y_ref.shape[1]), jnp.float32)
    for field in range(2):
        for level in range(2):
            index = 2 * field + level
            place = slice(HALF_ROWS * index, HALF_ROWS * (index + 1))
            near_x_ref[place, :] = state_ref[field, 0, mine + level, :HALF_ROWS, :]
            other = 2 - mine + level
            near_y_ref[place, :] = state_ref[field, 0, other, :HALF_ROWS, :]
            line = slice(4 * HALF_ROWS + index, 4 * HALF_ROWS + index + 1)
            near_y_ref[line, :] = state_ref[field, 0, other, HALF_ROWS : HALF_ROWS + 1, :]
            far_ref[index : index + 1, :] = state_ref[field, 0, other, 0:1, :]


def inverse_kernel(
    grid, state_ref, near_x_ref, near_y_ref, far_ref, x_ref, y_ref, own_ref, swap_ref, held, mixed, high_ref, low_ref
):
    rows = state_ref.shape[3]
    pen = lax.axis_index("pen")
    mine = (pen // 2) * 2
    odd = pen % 2 == 1
    count = 2 * rows + EXTRA
    for field in range(2):
        for level in range(2):
            index = 2 * field + level
            place = slice(HALF_ROWS * index, HALF_ROWS * (index + 1))
            held[index, :rows, :] = state_ref[field, 0, mine + level]
            held[index, rows : rows + HALF_ROWS, :] = near_x_ref[place, :]
            held[index, rows + HALF_ROWS : 2 * rows, :] = near_y_ref[place, :]
            held[index, 2 * rows :, :] = jnp.zeros((EXTRA, 2 * grid), jnp.float32)
            line = slice(4 * HALF_ROWS + index, 4 * HALF_ROWS + index + 1)
            held[index, 2 * rows : 2 * rows + 1, :] = near_y_ref[line, :]
            held[index, 2 * rows + 1 : 2 * rows + 2, :] = far_ref[index : index + 1, :]
    row = lax.broadcasted_iota(jnp.int32, (count, 1), 0)
    ky = jnp.where(
        row < rows,
        pen * rows + row,
        jnp.where(
            row < rows + HALF_ROWS,
            (pen ^ 1) * rows + row - rows,
            jnp.where(
                row <= 2 * rows, (pen ^ 2) * rows + row - rows - HALF_ROWS, (pen ^ 3) * rows
            ),
        ),
    )
    kappa_y, kappa_x, _, inverse = wave_arrays(ky, grid)
    table = (x_ref[pen, 0], x_ref[pen, 1])
    fields = [
        (0, inverse, kappa_y),
        (0, -kappa_x * inverse, None),
        (0, kappa_x, None),
        (0, None, kappa_y),
        (1, kappa_x, None),
        (1, None, kappa_y),
    ]
    for number, (field, before, after) in enumerate(fields):
        stacked = []
        for level in range(2):
            for columns in (slice(0, grid), slice(grid, 2 * grid)):
                values = held[2 * field + level, :, columns]
                stacked.append(values if before is None else values * before)
        product = dot_split(split(jnp.concatenate(stacked, axis=0)), table)
        for level in range(2):
            top = product[2 * level * count : (2 * level + 1) * count]
            bottom = product[(2 * level + 1) * count : (2 * level + 2) * count]
            real = -(bottom[:, :128] + top[:, 128:])
            imag = top[:, :128] - bottom[:, 128:]
            if after is not None:
                real, imag = after * real, after * imag
            mixed[level, : 2 * rows, :] = real[: 2 * rows]
            mixed[level, 2 * rows :, :] = imag[: 2 * rows]
            extra_real, extra_imag = real[2 * rows : 2 * rows + 1], imag[2 * rows : 2 * rows + 1]
            far_real = real[2 * rows + 1 : 2 * rows + 2]
            from_y = rows + HALF_ROWS
            mixed[level, from_y : from_y + 1, :] = jnp.where(
                odd, extra_real, real[from_y : from_y + 1]
            )
            mixed[level, 2 * rows : 2 * rows + 1, :] = jnp.where(odd, imag[0:1], extra_real)
            mixed[level, 3 * rows : 3 * rows + 1, :] = jnp.where(
                odd, far_real, imag[rows : rows + 1]
            )
            mixed[level, 2 * rows + from_y : 2 * rows + from_y + 1, :] = extra_imag
        for block, values in enumerate(interleave(mixed[0], mixed[1])):
            high, low = split(values)
            high_ref[block, :, 128 * number : 128 * number + 128] = high
            low_ref[block, :, 128 * number : 128 * number + 128] = low
    left = (y_ref[pen, 0], y_ref[pen, 1])
    own_ref[...] = dot_split(left, (high_ref[0], low_ref[0]))
    swap_ref[...] = dot_split(left, (high_ref[1], low_ref[1]))


def advection_kernel(masks, rows, field_ref, *refs):
    blocks, forward_ref = refs[: len(masks)], refs[len(masks)]
    outs, (high_ref, low_ref) = refs[len(masks) + 1 : len(masks) + 1 + PEN], refs[-2:]
    ens = lax.axis_index("ens")
    for (mask, slot), block in zip(masks, blocks, strict=True):
        tall = block.shape[-2]
        place = pl.ds(pl.multiple_of((ens ^ mask) * tall, tall), tall)

        def base(index, block=block, slot=slot):
            lanes = slice(128 * index, 128 * index + 128)
            return block[:, lanes] if slot is None else block[slot, :, lanes]

        def field(index, place=place):
            return field_ref[place, 128 * index : 128 * index + 128]

        for output, first in ((0, 2), (1, 4)):
            total = (
                base(0) * field(first)
                + base(1) * field(first + 1)
                + field(0) * base(first)
                + field(1) * base(first + 1)
            )
            high, low = split(total)
            high_ref[place, 128 * output : 128 * output + 128] = high
            low_ref[place, 128 * output : 128 * output + 128] = low
    pen = lax.axis_index("pen")
    for step in range(PEN):
        place = pl.ds(pl.multiple_of((pen ^ step) * 2 * rows, 2 * rows), 2 * rows)
        outs[step][...] = dot_split(
            (forward_ref[0, place, :], forward_ref[1, place, :]), (high_ref[...], low_ref[...])
        )


def x_forward(chunk, messages, gathered, table_ref, rows):
    pen = lax.axis_index("pen")
    for step in range(PEN):
        gathered[pen ^ step] = messages[step][...]
    grid = table_ref.shape[1]
    for pair in range(2):
        block = pair if chunk == 0 else 1 - pair
        lines = slice(2 * rows * block, 2 * rows * (block + 1))
        stacked = []
        for field in range(2):
            lanes = slice(128 * field, 128 * field + 128)
            stacked += interleave(gathered[2 * pair, :, lanes], gathered[2 * pair + 1, :, lanes])
        product = dot_split(
            split(jnp.concatenate(stacked, axis=0)), (table_ref[0, lines, :], table_ref[1, lines, :])
        )
        for index in range(4):
            top = product[2 * index * rows : (2 * index + 1) * rows]
            bottom = product[(2 * index + 1) * rows : (2 * index + 2) * rows]
            yield (
                index // 2,
                2 * pair + index % 2,
                top[:, :grid] + bottom[:, grid:],
                bottom[:, :grid] - top[:, grid:],
            )


def first_kernel(grid, *refs):
    messages, (state_ref, accum_ref, table_ref, out_ref, gathered) = refs[:PEN], refs[PEN:]
    rows, levels = state_ref.shape[3], state_ref.shape[2]
    row = lax.broadcasted_iota(jnp.int32, (rows, 1), 0)
    _, kappa_x, square, inverse = wave_arrays(lax.axis_index("pen") * rows + row, grid)
    real, imag = slice(0, grid), slice(grid, 2 * grid)
    for field, level, advect_real, advect_imag in x_forward(0, messages, gathered, table_ref, rows):
        for columns, other, sign, advect in (
            (real, imag, 1.0, advect_real),
            (imag, real, -1.0, advect_imag),
        ):
            here = state_ref[field, 0, level, :, columns]
            above = state_ref[field, 0, min(level + 1, levels - 1), :, columns]
            below = state_ref[field, 0, max(level - 1, 0), :, columns]
            cross = state_ref[1 - field, 0, level, :, other]
            if field == 0:
                coupling = (-sign * buoyancy_gain) * (kappa_x * cross)
            else:
                coupling = (-sign * stratification) * (kappa_x * inverse * cross)
            damping = viscosity if field == 0 else diffusivity
            out_ref[field, 0, level, :, columns] = (
                memory_factor * accum_ref[field, 0, level, :, columns]
                - advect
                + coupling
                - damping * square * here
                + vertical_mixing * (above + below - 2.0 * here)
            )


def second_kernel(grid, *refs):
    messages, (state_ref, part_ref, table_ref, state_out, accum_out, gathered) = refs[:PEN], refs[PEN:]
    rows = state_ref.shape[3]
    for field, level, *advect in x_forward(1, messages, gathered, table_ref, rows):
        for columns, values in zip((slice(0, grid), slice(grid, 2 * grid)), advect, strict=True):
            memory = part_ref[field, 0, level, :, columns] - values
            accum_out[field, 0, level, :, columns] = memory
            state_out[field, 0, level, :, columns] = (
                state_ref[field, 0, level, :, columns] + weight_factor * time_step * memory
            )


def pack_kernel(*refs):
    for index, ref in enumerate(refs[:-1]):
        refs[-1][index] = ref[...]


def call(kernel, outs, scratch, flops, args, limit=40):
    total = sum(math.prod(a.shape) * a.dtype.itemsize for a in list(args) + list(outs))
    return pl.pallas_call(
        kernel,
        out_shape=outs,
        in_specs=[pl.BlockSpec(memory_space=pltpu.VMEM)] * len(args),
        out_specs=[pl.BlockSpec(memory_space=pltpu.VMEM)] * len(outs),
        scratch_shapes=scratch,
        compiler_params=pltpu.CompilerParams(vmem_limit_bytes=limit * 1024 * 1024),
        cost_estimate=pl.CostEstimate(flops=flops, bytes_accessed=total, transcendentals=0),
    )(*args)


def exchange(values, axis, size, mask):
    return lax.ppermute(values, axis, [(index, index ^ mask) for index in range(size)])


def gather_blocks(block, size):
    held = {0: block}
    bit = size // 2
    while bit > 1:
        for offset in list(held):
            mask = 2 * bit - 2
            held[offset ^ mask] = exchange(held[offset], "ens", size, mask)
        bit //= 2
    offsets = list(held)
    early, last = offsets[:-1], offsets[-1]
    shape = jax.ShapeDtypeStruct((len(early),) + block.shape, block.dtype)
    (packed,) = call(pack_kernel, [shape], [], 0, [held[offset] for offset in early])
    packed = exchange(packed, "ens", size, 1)
    final = exchange(held[last], "ens", size, 1)
    found = [((offset, None), held[offset]) for offset in offsets]
    found += [((offset ^ 1, slot), packed) for slot, offset in enumerate(early)]
    found.append(((last ^ 1, None), final))
    return found


def on_device(axes, state, accum, base_flow):
    grid, rows, levels = state.shape[-1] // 2, state.shape[3], state.shape[2]
    size = axes["ens"]
    if axes["pen"] != PEN or levels != 4 or grid != 256 or size & (size - 1):
        return on_device_general(state, accum, base_flow)
    f32, bf16 = jnp.float32, jnp.bfloat16
    shape = functools.partial(jax.ShapeDtypeStruct, dtype=f32)
    fields, _, wide, tall = base_flow.shape
    lanes = 2 * wide
    x_forward_parts = jnp.asarray(x_forward_table(grid))

    own_base, swap_base = call(
        base_kernel,
        [shape((tall, fields * lanes))] * 2,
        [],
        0,
        [jnp.swapaxes(base_flow, 2, 3)],
    )
    own_blocks = gather_blocks(own_base, size)
    swap_blocks = gather_blocks(exchange(swap_base, "pen", PEN, 2), size)
    near_x, near_y, far = call(
        state_kernel,
        [
            shape((4 * HALF_ROWS, 2 * grid)),
            shape((4 * HALF_ROWS + EXTRA, 2 * grid)),
            shape((EXTRA, 2 * grid)),
        ],
        [],
        0,
        [state],
    )
    near_x = exchange(near_x, "pen", PEN, 1)
    near_y = exchange(near_y, "pen", PEN, 2)
    far = exchange(far, "pen", PEN, 3)
    count = 2 * rows + EXTRA
    own_fields, swap_fields = call(
        functools.partial(inverse_kernel, grid),
        [shape((grid, fields * lanes))] * 2,
        [
            pltpu.VMEM((4, count, 2 * grid), f32),
            pltpu.VMEM((2, 4 * rows, lanes), f32),
            pltpu.VMEM((2, grid, fields * lanes), bf16),
            pltpu.VMEM((2, grid, fields * lanes), bf16),
        ],
        6 * fields * 4 * count * grid * 256 + 12 * grid * grid * fields * lanes,
        [
            state,
            near_x,
            near_y,
            far,
            jnp.asarray(x_inverse_table(grid)),
            jnp.asarray(y_inverse_table(grid)),
        ],
    )
    back = []
    forward = jnp.asarray(y_forward_table(grid))
    for physical, blocks in ((own_fields, own_blocks), (swap_fields, swap_blocks)):
        masks = tuple(key for key, _ in blocks)
        parts = call(
            functools.partial(advection_kernel, masks, rows),
            [shape((2 * rows, 2 * lanes))] * PEN,
            [pltpu.VMEM((grid, 2 * lanes), bf16)] * 2,
            6 * 2 * grid * grid * 2 * lanes,
            [physical] + [block for _, block in blocks] + [forward],
        )
        back.append([parts[0]] + [exchange(parts[step], "pen", PEN, step) for step in range(1, PEN)])
    gathered = [pltpu.VMEM((PEN, 2 * rows, 2 * lanes), f32)]
    flops = 6 * 8 * 2 * rows * 2 * rows * 2 * grid
    (part,) = call(
        functools.partial(first_kernel, grid),
        [shape(state.shape)],
        gathered,
        flops,
        back[0] + [state, accum, x_forward_parts],
    )
    state_next, accum_next = call(
        functools.partial(second_kernel, grid),
        [shape(state.shape), shape(state.shape)],
        gathered,
        flops,
        back[1] + [state, part, x_forward_parts],
    )
    return state_next, accum_next


def solution(mesh):
    return jax.shard_map(
        functools.partial(on_device, dict(mesh.shape)),
        mesh=mesh,
        in_specs=(
            P(None, "ens", None, "pen", None),
            P(None, "ens", None, "pen", None),
            P(None, None, "pen", "ens"),
        ),
        out_specs=(P(None, "ens", None, "pen", None), P(None, "ens", None, "pen", None)),
        check_vma=False,
    )
```

```python
import functools
import math

import jax
import jax.numpy as jnp
import ml_dtypes
import numpy as np
from jax import lax
from jax.experimental import pallas as pl
from jax.experimental.pallas import tpu as pltpu
from jax.sharding import PartitionSpec as P

viscosity = 0.05
diffusivity = 0.05
vertical_mixing = 0.5
buoyancy_gain = 0.5
stratification = 0.5
memory_factor = -5.0 / 9.0
weight_factor = 15.0 / 16.0
time_step = 0.4


def wave_numbers(amount, offset, length):
    position = offset + jnp.arange(amount, dtype=jnp.int32)
    half_length = length // 2
    signed = jnp.where(position <= half_length, position, position - length)
    derivative = jnp.where(position == half_length, 0, signed)
    return (2.0 * math.pi / length * derivative.astype(jnp.float32), signed)


def times_i(real_part, imag_part, factor):
    return (-factor * imag_part, factor * real_part)


def vertical(quantity, level_axis):
    depth = quantity.shape[level_axis]
    lower = lax.slice_in_dim(quantity, 0, 1, axis=level_axis)
    upper = lax.slice_in_dim(quantity, depth - 1, depth, axis=level_axis)
    padded = jnp.concatenate([lower, quantity, upper], axis=level_axis)
    above = lax.slice_in_dim(padded, 2, depth + 2, axis=level_axis)
    below = lax.slice_in_dim(padded, 0, depth, axis=level_axis)
    return above + below - 2.0 * quantity


def tendency(vort, buoy, advect, across, kappa_x, square, level_axis):
    tend_vort_re = (
        -advect[0]
        + buoyancy_gain * (-kappa_x * buoy[1])
        - viscosity * square * vort[0]
        + vertical_mixing * vertical(vort[0], level_axis)
    )
    tend_vort_im = (
        -advect[1]
        + buoyancy_gain * (kappa_x * buoy[0])
        - viscosity * square * vort[1]
        + vertical_mixing * vertical(vort[1], level_axis)
    )
    tend_buoy_re = (
        -advect[2]
        - stratification * across[0]
        - diffusivity * square * buoy[0]
        + vertical_mixing * vertical(buoy[0], level_axis)
    )
    tend_buoy_im = (
        -advect[3]
        - stratification * across[1]
        - diffusivity * square * buoy[1]
        + vertical_mixing * vertical(buoy[1], level_axis)
    )
    return jnp.stack(
        [
            jnp.concatenate([tend_vort_re, tend_vort_im], axis=-1),
            jnp.concatenate([tend_buoy_re, tend_buoy_im], axis=-1),
        ]
    )


def dft_tables(length):
    position = jnp.arange(length, dtype=jnp.int32)
    product = position[:, None] * position[None, :] % length
    angle = 2.0 * math.pi / length * product.astype(jnp.float32)
    scale = 1.0 / math.sqrt(length)
    return (scale * jnp.cos(angle), scale * jnp.sin(angle))


def to_physical(spectral, x_table, y_table):
    mixed_space = jnp.einsum(
        "fplkj,jcx->fplcxk", spectral, x_table, precision=lax.Precision.HIGHEST
    )
    return jnp.einsum(
        "fplcxk,ckm->fplxm",
        lax.all_to_all(mixed_space, "pen", split_axis=4, concat_axis=5, tiled=True),
        y_table,
        precision=lax.Precision.HIGHEST,
    )


def on_device_general(state, accum, base_flow):
    grid_size = state.shape[-1] // 2
    row_count = state.shape[3]
    base_all = lax.all_gather(base_flow, "ens", axis=3, tiled=True)
    kappa_rows, signed_y = wave_numbers(row_count, lax.axis_index("pen") * row_count, grid_size)
    kappa_cols, signed_x = wave_numbers(grid_size, 0, grid_size)
    kappa_y = kappa_rows[:, None]
    kappa_x = kappa_cols[None, :]
    wave_square = signed_y[:, None] ** 2 + signed_x[None, :] ** 2
    factor = (2.0 * math.pi / grid_size) ** 2
    square = factor * wave_square.astype(jnp.float32)
    inverse = jnp.where(
        wave_square > 0, 1.0 / (factor * jnp.maximum(wave_square, 1).astype(jnp.float32)), 0.0
    )
    vort = (state[0][..., :grid_size], state[0][..., grid_size:])
    buoy = (state[1][..., :grid_size], state[1][..., grid_size:])
    potential_re = -vort[0] * inverse
    potential_im = -vort[1] * inverse
    flow_x = times_i(potential_re, potential_im, -kappa_y)
    flow_y = times_i(potential_re, potential_im, kappa_x)
    vort_x = times_i(vort[0], vort[1], kappa_x)
    vort_y = times_i(vort[0], vort[1], kappa_y)
    buoy_x = times_i(buoy[0], buoy[1], kappa_x)
    buoy_y = times_i(buoy[0], buoy[1], kappa_y)
    cosine_table, sine_table = dft_tables(grid_size)
    x_table = jnp.concatenate(
        [
            jnp.stack([cosine_table, sine_table], axis=1),
            jnp.stack([-sine_table, cosine_table], axis=1),
        ],
        axis=0,
    )
    y_table = jnp.stack([cosine_table, -sine_table])
    components = [flow_x, flow_y, vort_x, vort_y, buoy_x, buoy_y]
    spectral = jnp.stack([jnp.concatenate(component, axis=-1) for component in components])
    physical = to_physical(spectral, x_table, y_table)
    flow_x_p, flow_y_p = (physical[0], physical[1])
    vort_x_p, vort_y_p = (physical[2], physical[3])
    buoy_x_p, buoy_y_p = (physical[4], physical[5])
    advect_vort = (
        base_all[0] * vort_x_p
        + base_all[1] * vort_y_p
        + flow_x_p * base_all[2]
        + flow_y_p * base_all[3]
    )
    advect_buoy = (
        base_all[0] * buoy_x_p
        + base_all[1] * buoy_y_p
        + flow_x_p * base_all[4]
        + flow_y_p * base_all[5]
    )
    advect_both = jnp.stack([advect_vort, advect_buoy])
    y_forward = jnp.stack([cosine_table, -sine_table], axis=1)
    x_forward = jnp.stack(
        [
            jnp.concatenate([cosine_table, -sine_table], axis=1),
            jnp.concatenate([sine_table, cosine_table], axis=1),
        ]
    )
    spread = jnp.einsum(
        "fplxy,yck->fplckx", advect_both, y_forward, precision=lax.Precision.HIGHEST
    )
    spectra = jnp.einsum(
        "fplckx,cxm->fplkm",
        lax.all_to_all(spread, "pen", split_axis=4, concat_axis=5, tiled=True),
        x_forward,
        precision=lax.Precision.HIGHEST,
    )
    advect = (
        spectra[0][..., :grid_size],
        spectra[0][..., grid_size:],
        spectra[1][..., :grid_size],
        spectra[1][..., grid_size:],
    )
    tend = tendency(vort, buoy, advect, flow_y, kappa_x, square, 1)
    accum_next = memory_factor * accum + tend
    state_next = state + weight_factor * time_step * accum_next
    return (state_next, accum_next)


PEN = 4
INV = 1
PACK = (10**10, 0)
HALF_ROWS = 32
EXTRA = 8


def split(values):
    high = values.astype(jnp.bfloat16)
    return high, (values - high.astype(jnp.float32)).astype(jnp.bfloat16)


def split_table(values):
    high = values.astype(ml_dtypes.bfloat16)
    low = (values - high.astype(np.float64)).astype(ml_dtypes.bfloat16)
    return np.stack([high, low], axis=-3)


def cosine(grid, left, right):
    return np.cos(2.0 * np.pi / grid * (left * right % grid)) / math.sqrt(grid)


def sine(grid, left, right):
    return np.sin(2.0 * np.pi / grid * (left * right % grid)) / math.sqrt(grid)


def x_table(grid):
    kx = np.arange(grid)
    x = kx[:, None]
    return split_table(np.concatenate([cosine(grid, x, kx), sine(grid, x, kx)], axis=1))


def row_numbers(device, rows):
    own = device * rows + np.arange(rows)
    near = [(device ^ step) * rows + np.arange(HALF_ROWS) for step in (1, 2)]
    return np.concatenate([own] + near)


def y_inverse_table(grid):
    rows = grid // PEN
    y = np.arange(grid)[:, None]
    tables = []
    for device in range(PEN):
        ky = row_numbers(device, rows)
        real = np.where(ky % (grid // 2) == 0, 1.0, 2.0) * cosine(grid, y, ky)
        imag = -2.0 * sine(grid, y, ky)
        extra = (device ^ 1) * rows + HALF_ROWS
        far = (device ^ 3) * rows
        from_y = rows + HALF_ROWS
        extra_real, extra_imag = 2.0 * cosine(grid, y[:, 0], extra), -2.0 * sine(grid, y[:, 0], extra)
        imag[:, from_y] = extra_imag
        if device % 2 == 0:
            imag[:, 0] = extra_real
        else:
            real[:, from_y] = extra_real
            imag[:, rows] = cosine(grid, y[:, 0], far)
        tables.append(np.concatenate([real, imag], axis=1))
    return split_table(np.stack(tables))


def y_forward_table(grid):
    rows = grid // PEN
    parts = []
    for device in range(PEN):
        ky = device * rows + np.arange(rows)[:, None]
        y = np.arange(grid)[None, :]
        parts += [cosine(grid, ky, y), -sine(grid, ky, y)]
    return split_table(np.concatenate([np.concatenate(parts[:4]), np.concatenate(parts[4:])], axis=1))


def dot(left, right):
    return jnp.dot(left, right, preferred_element_type=jnp.float32)


def dot_split(left, right):
    return dot(left[0], right[0]) + (dot(left[1], right[0]) + dot(left[0], right[1]))


def waves(position, grid):
    signed = jnp.where(position <= grid // 2, position, position - grid)
    derivative = jnp.where(position == grid // 2, 0, signed)
    return (2.0 * math.pi / grid) * derivative.astype(jnp.float32), signed


def wave_arrays(row_position, grid):
    kappa_y, signed_y = waves(row_position, grid)
    kappa_x, signed_x = waves(lax.broadcasted_iota(jnp.int32, (1, grid), 1), grid)
    wave_square = signed_y * signed_y + signed_x * signed_x
    factor = (2.0 * math.pi / grid) ** 2
    square = factor * wave_square.astype(jnp.float32)
    inverse = jnp.where(wave_square > 0, 1.0 / jnp.where(wave_square > 0, square, 1.0), 0.0)
    return kappa_y, kappa_x, square, inverse


def interleave(even, odd):
    low_lanes = lax.broadcasted_iota(jnp.int32, (1, 128), 1) < 64
    return (
        jnp.where(low_lanes, even, pltpu.roll(odd, 64, 1)),
        jnp.where(low_lanes, pltpu.roll(even, 64, 1), odd),
    )


def base_kernel(base_ref, own_ref, swap_ref):
    mine = (lax.axis_index("pen") % 2) * 2
    for out_ref, first in ((own_ref, mine), (swap_ref, 2 - mine)):
        for field in range(base_ref.shape[0]):
            out_ref[:, 128 * field : 128 * field + 128] = jnp.concatenate(
                [base_ref[field, first], base_ref[field, first + 1]], axis=1
            )


def lines_kernel(block_ref, state_ref, out_ref):
    other = 2 - (lax.axis_index("pen") % 2) * 2
    tall = block_ref.shape[0]
    out_ref[:tall, :] = block_ref[...]
    out_ref[tall:, :] = jnp.zeros((EXTRA, out_ref.shape[1]), jnp.float32)
    for index in range(4):
        out_ref[tall + index : tall + index + 1, : state_ref.shape[4]] = state_ref[
            index // 2, 0, other + index % 2, 0:1, :
        ]


def near_x_kernel(state_ref, near_ref):
    other = 2 - (lax.axis_index("pen") % 2) * 2
    near_ref[4 * HALF_ROWS :, :] = jnp.zeros((EXTRA, near_ref.shape[1]), jnp.float32)
    for index in range(4):
        rows = state_ref[index // 2, 0, other + index % 2, : HALF_ROWS + EXTRA, :]
        near_ref[HALF_ROWS * index : HALF_ROWS * (index + 1), :] = rows[:HALF_ROWS]
        line = 4 * HALF_ROWS + index
        near_ref[line : line + 1, :] = rows[HALF_ROWS : HALF_ROWS + 1]


def relay_kernel(came_ref, state_ref, swap_ref, near_ref):
    mine = (lax.axis_index("pen") % 2) * 2
    tall = swap_ref.shape[0]
    swap_ref[...] = came_ref[:tall, :]
    near_ref[4 * HALF_ROWS :, :] = came_ref[tall:, : near_ref.shape[1]]
    for index in range(4):
        near_ref[HALF_ROWS * index : HALF_ROWS * (index + 1), :] = state_ref[
            index // 2, 0, mine + index % 2, :HALF_ROWS, :
        ]


def x_stage(grid, table, ky, held):
    count = held[0].shape[0]
    kappa_y, kappa_x, _, inverse = wave_arrays(ky, grid)
    fields = [
        (0, inverse, kappa_y),
        (0, -kappa_x * inverse, None),
        (0, kappa_x, None),
        (0, None, kappa_y),
        (1, kappa_x, None),
        (1, None, kappa_y),
    ]
    for field, before, after in fields:
        stacked = []
        for level in range(2):
            for columns in (slice(0, grid), slice(grid, 2 * grid)):
                values = held[2 * field + level][:, columns]
                stacked.append(values if before is None else values * before)
        product = dot_split(split(jnp.concatenate(stacked, axis=0)), table)
        results = []
        for level in range(2):
            top = product[2 * level * count : (2 * level + 1) * count]
            bottom = product[(2 * level + 1) * count : (2 * level + 2) * count]
            real = -(bottom[:, :128] + top[:, 128:])
            imag = top[:, :128] - bottom[:, 128:]
            results.append((real, imag) if after is None else (after * real, after * imag))
        yield results


def x_columns(grid, x_ref):
    start = pl.multiple_of((lax.axis_index("pen") // 2) * 128, 128)
    return [
        jnp.concatenate(
            [x_ref[part, :, pl.ds(start, 128)], x_ref[part, :, pl.ds(grid + start, 128)]], axis=1
        )
        for part in range(2)
    ]


def own_rows_kernel(grid, state_ref, x_ref, real_ref, imag_ref):
    rows = state_ref.shape[3]
    pen = lax.axis_index("pen")
    mine = (pen % 2) * 2
    held = [state_ref[field, 0, mine + level] for field in range(2) for level in range(2)]
    ky = pen * rows + lax.broadcasted_iota(jnp.int32, (rows, 1), 0)
    for number, results in enumerate(x_stage(grid, x_columns(grid, x_ref), ky, held)):
        for level, (real, imag) in enumerate(results):
            real_ref[level, number] = real
            imag_ref[level, number] = imag


def inverse_kernel(
    grid, near_x_ref, near_y_ref, own_real, own_imag, x_ref, y_ref, own_ref, swap_ref, mixed, high_ref, low_ref, y_held, sem
):
    y_copy = pltpu.make_async_copy(y_ref.at[lax.axis_index("pen")], y_held, sem)
    y_copy.start()
    rows = own_real.shape[2]
    pen = lax.axis_index("pen")
    odd = pen % 2 == 1
    count = rows + EXTRA
    held = []
    for index in range(4):
        place = slice(HALF_ROWS * index, HALF_ROWS * (index + 1))
        line = slice(4 * HALF_ROWS + index, 4 * HALF_ROWS + index + 1)
        held.append(
            jnp.concatenate(
                [
                    near_x_ref[place, :],
                    near_y_ref[place, :],
                    near_x_ref[line, :],
                    near_y_ref[line, :],
                    jnp.zeros((EXTRA - 2, 2 * grid), jnp.float32),
                ],
                axis=0,
            )
        )
    row = lax.broadcasted_iota(jnp.int32, (count, 1), 0)
    ky = jnp.where(row < HALF_ROWS, (pen ^ 1) * rows + row, (pen ^ 2) * rows + row - HALF_ROWS)
    ky = jnp.where(row == rows, (pen ^ 1) * rows + HALF_ROWS, ky)
    ky = jnp.where(row > rows, (pen ^ 3) * rows, ky)
    from_y = rows + HALF_ROWS
    for number, results in enumerate(x_stage(grid, x_columns(grid, x_ref), ky, held)):
        for level, (real, imag) in enumerate(results):
            first_imag = own_imag[level, number, 0:1, :]
            mixed[level, :rows, :] = own_real[level, number]
            mixed[level, rows : 2 * rows, :] = real[:rows]
            mixed[level, 2 * rows : 3 * rows, :] = own_imag[level, number]
            mixed[level, 3 * rows :, :] = imag[:rows]
            extra_real, extra_imag = real[rows : rows + 1], imag[rows : rows + 1]
            far_real = real[rows + 1 : rows + 2]
            mixed[level, from_y : from_y + 1, :] = jnp.where(
                odd, extra_real, real[HALF_ROWS : HALF_ROWS + 1]
            )
            mixed[level, 2 * rows : 2 * rows + 1, :] = jnp.where(odd, first_imag, extra_real)
            mixed[level, 3 * rows : 3 * rows + 1, :] = jnp.where(odd, far_real, imag[0:1])
            mixed[level, 2 * rows + from_y : 2 * rows + from_y + 1, :] = extra_imag
        for block, values in enumerate(interleave(mixed[0], mixed[1])):
            high, low = split(values)
            high_ref[block ^ (pen % 2), :, 128 * number : 128 * number + 128] = high
            low_ref[block ^ (pen % 2), :, 128 * number : 128 * number + 128] = low
    y_copy.wait()
    left = (y_held[0], y_held[1])
    own_ref[...] = dot_split(left, (high_ref[0], low_ref[0]))
    swap_ref[...] = dot_split(left, (high_ref[1], low_ref[1]))


def advection_kernel(offsets, rows, field_ref, *refs):
    packs, table_ref = refs[:2], refs[2]
    outs, (high_ref, low_ref) = refs[3 : 3 + PEN], refs[-2:]
    ens = lax.axis_index("ens")
    tall = packs[0].shape[0] // len(offsets)
    for which, slot in [(which, slot) for which in range(2) for slot in range(len(offsets))]:
        mask = offsets[slot] ^ which
        place = pl.ds(pl.multiple_of((ens ^ mask) * tall, tall), tall)

        def base(index, which=which, slot=slot):
            return packs[which][tall * slot : tall * (slot + 1), 128 * index : 128 * index + 128]

        def field(index, place=place):
            return field_ref[place, 128 * index : 128 * index + 128]

        for output, first in ((0, 2), (1, 4)):
            total = (
                base(0) * field(first)
                + base(1) * field(first + 1)
                + field(0) * base(first)
                + field(1) * base(first + 1)
            )
            high, low = split(total)
            high_ref[place, 128 * output : 128 * output + 128] = high
            low_ref[place, 128 * output : 128 * output + 128] = low
    pen = lax.axis_index("pen")
    grid = table_ref.shape[1]
    for step in range(PEN):
        target = pen ^ step
        place = pl.ds(pl.multiple_of((target % 2) * 2 * rows, 2 * rows), 2 * rows)
        lanes = pl.ds(pl.multiple_of((target // 2) * grid, grid), grid)
        outs[step][...] = dot_split(
            (table_ref[2, place, lanes], table_ref[3, place, lanes]), (high_ref[...], low_ref[...])
        )


def x_forward(chunk, messages, gathered, table_ref, rows):
    pen = lax.axis_index("pen")
    for step in range(PEN):
        gathered[pen ^ step] = messages[step][...]
    grid = table_ref.shape[1]
    for pair in range(2):
        first = (pair if chunk == 0 else 1 - pair) * rows
        table = [
            jnp.concatenate(
                [table_ref[part, first : first + rows, :], table_ref[part, first + 2 * rows : first + 3 * rows, :]],
                axis=0,
            )
            for part in range(2)
        ]
        stacked = []
        for field in range(2):
            lanes = slice(128 * field, 128 * field + 128)
            stacked += interleave(gathered[pair, :, lanes], gathered[pair + 2, :, lanes])
        product = dot_split(split(jnp.concatenate(stacked, axis=0)), table)
        for index in range(4):
            top = product[2 * index * rows : (2 * index + 1) * rows]
            bottom = product[(2 * index + 1) * rows : (2 * index + 2) * rows]
            yield (
                index // 2,
                2 * pair + index % 2,
                top[:, :grid] + bottom[:, grid:],
                bottom[:, :grid] - top[:, grid:],
            )


def first_kernel(grid, *refs):
    messages, (state_ref, accum_ref, table_ref, out_ref, gathered) = refs[:PEN], refs[PEN:]
    rows, levels = state_ref.shape[3], state_ref.shape[2]
    row = lax.broadcasted_iota(jnp.int32, (rows, 1), 0)
    _, kappa_x, square, inverse = wave_arrays(lax.axis_index("pen") * rows + row, grid)
    real, imag = slice(0, grid), slice(grid, 2 * grid)
    for field, level, advect_real, advect_imag in x_forward(0, messages, gathered, table_ref, rows):
        for columns, other, sign, advect in (
            (real, imag, 1.0, advect_real),
            (imag, real, -1.0, advect_imag),
        ):
            here = state_ref[field, 0, level, :, columns]
            above = state_ref[field, 0, min(level + 1, levels - 1), :, columns]
            below = state_ref[field, 0, max(level - 1, 0), :, columns]
            cross = state_ref[1 - field, 0, level, :, other]
            if field == 0:
                coupling = (-sign * buoyancy_gain) * (kappa_x * cross)
            else:
                coupling = (-sign * stratification) * (kappa_x * inverse * cross)
            damping = viscosity if field == 0 else diffusivity
            out_ref[field, 0, level, :, columns] = (
                memory_factor * accum_ref[field, 0, level, :, columns]
                - advect
                + coupling
                - damping * square * here
                + vertical_mixing * (above + below - 2.0 * here)
            )


def second_kernel(grid, *refs):
    messages = refs[:PEN]
    state_ref, part_ref, table_ref, state_out, accum_out, gathered, state_next, accum_next, sems = refs[PEN:]
    rows = state_ref.shape[3]
    copies = []
    for field, level, *advect in x_forward(1, messages, gathered, table_ref, rows):
        for columns, values in zip((slice(0, grid), slice(grid, 2 * grid)), advect, strict=True):
            memory = part_ref[field, 0, level, :, columns] - values
            accum_next[field, 0, level, :, columns] = memory
            state_next[field, 0, level, :, columns] = (
                state_ref[field, 0, level, :, columns] + weight_factor * time_step * memory
            )
        for which, (held, out) in enumerate(((state_next, state_out), (accum_next, accum_out))):
            copy = pltpu.make_async_copy(
                held.at[field, 0, level], out.at[field, 0, level], sems.at[which, field, level]
            )
            copy.start()
            copies.append(copy)
    for copy in copies:
        copy.wait()


def pack_kernel(*refs):
    tall = refs[0].shape[0]
    for slot, ref in enumerate(refs[:-1]):
        refs[-1][tall * slot : tall * (slot + 1), :] = ref[...]


def call(kernel, outs, scratch, cost, args, outside=(), outs_outside=False, after=(), limit=24):
    args, after = list(args), list(after)
    spaces = [pltpu.HBM if index in outside else pltpu.VMEM for index in range(len(args))]
    spaces += [pl.ANY] * len(after)
    count = len(args)
    total = sum(math.prod(a.shape) * a.dtype.itemsize for a in args + list(outs))
    return pl.pallas_call(
        lambda *refs: kernel(*refs[:count], *refs[count + len(after) :]),
        out_shape=outs,
        in_specs=[pl.BlockSpec(memory_space=space) for space in spaces],
        out_specs=[pl.BlockSpec(memory_space=pltpu.HBM if outs_outside else pltpu.VMEM)] * len(outs),
        scratch_shapes=scratch,
        compiler_params=pltpu.CompilerParams(vmem_limit_bytes=limit * 1024 * 1024),
        cost_estimate=pl.CostEstimate(flops=cost, bytes_accessed=total, transcendentals=0),
        name=getattr(kernel, "func", kernel).__name__,
    )(*args, *after)


def exchange(values, axis, size, mask):
    return lax.ppermute(values, axis, [(index, index ^ mask) for index in range(size)])


def gather_blocks(blocks, size, after):
    found = []
    for block, wait, cost in zip(blocks, after, PACK, strict=True):
        held = {0: block}
        bit = size // 2
        while bit > 1:
            for offset, array in list(held.items()):
                held[offset ^ (2 * bit - 2)] = exchange(array, "ens", size, 2 * bit - 2)
            bit //= 2
        shape = jax.ShapeDtypeStruct((len(held) * block.shape[0], block.shape[1]), block.dtype)
        (packed,) = call(pack_kernel, [shape], [], cost, list(held.values()), after=wait)
        found.append((tuple(held), packed, exchange(packed, "ens", size, 1)))
    return found


def on_device(axes, state, accum, base_flow):
    grid, rows, levels = state.shape[-1] // 2, state.shape[3], state.shape[2]
    size = axes["ens"]
    if axes["pen"] != PEN or levels != 4 or grid != 256 or size < 4 or size & (size - 1):
        return on_device_general(state, accum, base_flow)
    f32, bf16 = jnp.float32, jnp.bfloat16
    shape = functools.partial(jax.ShapeDtypeStruct, dtype=f32)
    fields, _, wide, tall = base_flow.shape
    lanes = 2 * wide
    table = jnp.asarray(np.concatenate([x_table(grid), y_forward_table(grid)]))
    y_table = y_inverse_table(grid)
    base_lanes = fields * lanes
    block, message = shape((tall, base_lanes)), shape((4 * HALF_ROWS + EXTRA, 2 * grid))
    own_base, swap_base = call(base_kernel, [block] * 2, [], 0, [jnp.swapaxes(base_flow, 2, 3)])
    (swap_base,) = call(lines_kernel, [shape((tall + EXTRA, base_lanes))], [], 0, [swap_base, state])
    came = exchange(swap_base, "pen", PEN, 1)
    (near_x,) = call(near_x_kernel, [message], [], 0, [state], after=[swap_base])
    near_x = exchange(near_x, "pen", PEN, 1)
    swap_base, near_y = call(relay_kernel, [block, message], [], 0, [came, state])
    near_y = exchange(near_y, "pen", PEN, 2)
    own_parts = call(
        functools.partial(own_rows_kernel, grid),
        [shape((2, fields, rows, lanes))] * 2,
        [],
        6 * fields * 4 * rows * grid * 256,
        [state, table],
    )
    own_fields, swap_fields = call(
        functools.partial(inverse_kernel, grid),
        [shape((grid, base_lanes))] * 2,
        [
            pltpu.VMEM((2, 4 * rows, lanes), f32),
            pltpu.VMEM((2, grid, base_lanes), bf16),
            pltpu.VMEM((2, grid, base_lanes), bf16),
            pltpu.VMEM(y_table.shape[1:], bf16),
            pltpu.SemaphoreType.DMA,
        ],
        INV * (6 * fields * 4 * (rows + EXTRA) * grid * 256 + 12 * grid * grid * base_lanes),
        [near_x, near_y, *own_parts, table, jnp.asarray(y_table)],
        outside=(5,),
    )
    blocks = gather_blocks((own_base, swap_base), size, ((), (own_fields,)))
    back = []
    for physical, (offsets, packed, partner) in zip((own_fields, swap_fields), blocks, strict=True):
        parts = call(
            functools.partial(advection_kernel, offsets, rows),
            [shape((2 * rows, 2 * lanes))] * PEN,
            [pltpu.VMEM((grid, 2 * lanes), bf16)] * 2,
            6 * 2 * grid * grid * 2 * lanes,
            [physical, packed, partner, table],
        )
        back.append([parts[0]] + [exchange(parts[step], "pen", PEN, step) for step in range(1, PEN)])
    gathered = [pltpu.VMEM((PEN, 2 * rows, 2 * lanes), f32)]
    flops = 6 * 8 * 2 * rows * 2 * rows * 2 * grid
    (part,) = call(
        functools.partial(first_kernel, grid),
        [shape(state.shape)],
        gathered,
        flops,
        back[0] + [state, accum, table],
    )
    state_next, accum_next = call(
        functools.partial(second_kernel, grid),
        [shape(state.shape), shape(state.shape)],
        gathered
        + [pltpu.VMEM(state.shape, f32)] * 2
        + [pltpu.SemaphoreType.DMA((2, 2, levels))],
        flops,
        back[1] + [state, part, table],
        outs_outside=True,
    )
    return state_next, accum_next


def solution(mesh):
    return jax.shard_map(
        functools.partial(on_device, dict(mesh.shape)),
        mesh=mesh,
        in_specs=(
            P(None, "ens", None, "pen", None),
            P(None, "ens", None, "pen", None),
            P(None, None, "pen", "ens"),
        ),
        out_specs=(P(None, "ens", None, "pen", None), P(None, "ens", None, "pen", None)),
        check_vma=False,
    )
```

```python
import functools
import math

import jax
import jax.numpy as jnp
import ml_dtypes
import numpy as np
from jax import lax
from jax.experimental import pallas as pl
from jax.experimental.pallas import tpu as pltpu
from jax.sharding import PartitionSpec as P

viscosity = 0.05
diffusivity = 0.05
vertical_mixing = 0.5
buoyancy_gain = 0.5
stratification = 0.5
memory_factor = -5.0 / 9.0
weight_factor = 15.0 / 16.0
time_step = 0.4


def wave_numbers(amount, offset, length):
    position = offset + jnp.arange(amount, dtype=jnp.int32)
    half_length = length // 2
    signed = jnp.where(position <= half_length, position, position - length)
    derivative = jnp.where(position == half_length, 0, signed)
    return (2.0 * math.pi / length * derivative.astype(jnp.float32), signed)


def times_i(real_part, imag_part, factor):
    return (-factor * imag_part, factor * real_part)


def vertical(quantity, level_axis):
    depth = quantity.shape[level_axis]
    lower = lax.slice_in_dim(quantity, 0, 1, axis=level_axis)
    upper = lax.slice_in_dim(quantity, depth - 1, depth, axis=level_axis)
    padded = jnp.concatenate([lower, quantity, upper], axis=level_axis)
    above = lax.slice_in_dim(padded, 2, depth + 2, axis=level_axis)
    below = lax.slice_in_dim(padded, 0, depth, axis=level_axis)
    return above + below - 2.0 * quantity


def tendency(vort, buoy, advect, across, kappa_x, square, level_axis):
    tend_vort_re = (
        -advect[0]
        + buoyancy_gain * (-kappa_x * buoy[1])
        - viscosity * square * vort[0]
        + vertical_mixing * vertical(vort[0], level_axis)
    )
    tend_vort_im = (
        -advect[1]
        + buoyancy_gain * (kappa_x * buoy[0])
        - viscosity * square * vort[1]
        + vertical_mixing * vertical(vort[1], level_axis)
    )
    tend_buoy_re = (
        -advect[2]
        - stratification * across[0]
        - diffusivity * square * buoy[0]
        + vertical_mixing * vertical(buoy[0], level_axis)
    )
    tend_buoy_im = (
        -advect[3]
        - stratification * across[1]
        - diffusivity * square * buoy[1]
        + vertical_mixing * vertical(buoy[1], level_axis)
    )
    return jnp.stack(
        [
            jnp.concatenate([tend_vort_re, tend_vort_im], axis=-1),
            jnp.concatenate([tend_buoy_re, tend_buoy_im], axis=-1),
        ]
    )


def dft_tables(length):
    position = jnp.arange(length, dtype=jnp.int32)
    product = position[:, None] * position[None, :] % length
    angle = 2.0 * math.pi / length * product.astype(jnp.float32)
    scale = 1.0 / math.sqrt(length)
    return (scale * jnp.cos(angle), scale * jnp.sin(angle))


def to_physical(spectral, x_table, y_table):
    mixed_space = jnp.einsum(
        "fplkj,jcx->fplcxk", spectral, x_table, precision=lax.Precision.HIGHEST
    )
    return jnp.einsum(
        "fplcxk,ckm->fplxm",
        lax.all_to_all(mixed_space, "pen", split_axis=4, concat_axis=5, tiled=True),
        y_table,
        precision=lax.Precision.HIGHEST,
    )


def on_device_general(state, accum, base_flow):
    grid_size = state.shape[-1] // 2
    row_count = state.shape[3]
    base_all = lax.all_gather(base_flow, "ens", axis=3, tiled=True)
    kappa_rows, signed_y = wave_numbers(row_count, lax.axis_index("pen") * row_count, grid_size)
    kappa_cols, signed_x = wave_numbers(grid_size, 0, grid_size)
    kappa_y = kappa_rows[:, None]
    kappa_x = kappa_cols[None, :]
    wave_square = signed_y[:, None] ** 2 + signed_x[None, :] ** 2
    factor = (2.0 * math.pi / grid_size) ** 2
    square = factor * wave_square.astype(jnp.float32)
    inverse = jnp.where(
        wave_square > 0, 1.0 / (factor * jnp.maximum(wave_square, 1).astype(jnp.float32)), 0.0
    )
    vort = (state[0][..., :grid_size], state[0][..., grid_size:])
    buoy = (state[1][..., :grid_size], state[1][..., grid_size:])
    potential_re = -vort[0] * inverse
    potential_im = -vort[1] * inverse
    flow_x = times_i(potential_re, potential_im, -kappa_y)
    flow_y = times_i(potential_re, potential_im, kappa_x)
    vort_x = times_i(vort[0], vort[1], kappa_x)
    vort_y = times_i(vort[0], vort[1], kappa_y)
    buoy_x = times_i(buoy[0], buoy[1], kappa_x)
    buoy_y = times_i(buoy[0], buoy[1], kappa_y)
    cosine_table, sine_table = dft_tables(grid_size)
    x_table = jnp.concatenate(
        [
            jnp.stack([cosine_table, sine_table], axis=1),
            jnp.stack([-sine_table, cosine_table], axis=1),
        ],
        axis=0,
    )
    y_table = jnp.stack([cosine_table, -sine_table])
    components = [flow_x, flow_y, vort_x, vort_y, buoy_x, buoy_y]
    spectral = jnp.stack([jnp.concatenate(component, axis=-1) for component in components])
    physical = to_physical(spectral, x_table, y_table)
    flow_x_p, flow_y_p = (physical[0], physical[1])
    vort_x_p, vort_y_p = (physical[2], physical[3])
    buoy_x_p, buoy_y_p = (physical[4], physical[5])
    advect_vort = (
        base_all[0] * vort_x_p
        + base_all[1] * vort_y_p
        + flow_x_p * base_all[2]
        + flow_y_p * base_all[3]
    )
    advect_buoy = (
        base_all[0] * buoy_x_p
        + base_all[1] * buoy_y_p
        + flow_x_p * base_all[4]
        + flow_y_p * base_all[5]
    )
    advect_both = jnp.stack([advect_vort, advect_buoy])
    y_forward = jnp.stack([cosine_table, -sine_table], axis=1)
    x_forward = jnp.stack(
        [
            jnp.concatenate([cosine_table, -sine_table], axis=1),
            jnp.concatenate([sine_table, cosine_table], axis=1),
        ]
    )
    spread = jnp.einsum(
        "fplxy,yck->fplckx", advect_both, y_forward, precision=lax.Precision.HIGHEST
    )
    spectra = jnp.einsum(
        "fplckx,cxm->fplkm",
        lax.all_to_all(spread, "pen", split_axis=4, concat_axis=5, tiled=True),
        x_forward,
        precision=lax.Precision.HIGHEST,
    )
    advect = (
        spectra[0][..., :grid_size],
        spectra[0][..., grid_size:],
        spectra[1][..., :grid_size],
        spectra[1][..., grid_size:],
    )
    tend = tendency(vort, buoy, advect, flow_y, kappa_x, square, 1)
    accum_next = memory_factor * accum + tend
    state_next = state + weight_factor * time_step * accum_next
    return (state_next, accum_next)


PEN = 4
EXTRA = 8
HINT = dict(own=0, inverse=10**10, forward=10**10, pack=0, advect=(0, 0), final=0)


def split(values):
    high = values.astype(jnp.bfloat16)
    return high, (values - high.astype(jnp.float32)).astype(jnp.bfloat16)


def split_table(values):
    high = values.astype(ml_dtypes.bfloat16)
    low = (values - high.astype(np.float64)).astype(ml_dtypes.bfloat16)
    return np.stack([high, low], axis=-3)


def cosine(grid, left, right):
    return np.cos(2.0 * np.pi / grid * (left * right % grid)) / math.sqrt(grid)


def sine(grid, left, right):
    return np.sin(2.0 * np.pi / grid * (left * right % grid)) / math.sqrt(grid)


def x_table(grid):
    kx = np.arange(grid)
    x = kx[:, None]
    return split_table(np.concatenate([cosine(grid, x, kx), sine(grid, x, kx)], axis=1))


def y_inverse_table(grid):
    rows = grid // PEN
    y = np.arange(grid)[:, None]
    tables = []
    for device in range(PEN):
        ky = np.concatenate([block * rows + np.arange(rows) for block in (device, device ^ 2)])
        real = np.where(ky % (grid // 2) == 0, 1.0, 2.0) * cosine(grid, y, ky)
        imag = -2.0 * sine(grid, y, ky)
        near, far = (device ^ 1) * rows, (device ^ 3) * rows
        if device % 2 == 0:
            imag[:, 0] = 2.0 * cosine(grid, y[:, 0], near)
            imag[:, rows] = -2.0 * sine(grid, y[:, 0], near)
        else:
            real[:, rows] = cosine(grid, y[:, 0], near)
            imag[:, rows] = cosine(grid, y[:, 0], far)
        tables.append(np.concatenate([real, imag], axis=1))
    return split_table(np.stack(tables))


def y_forward_table(grid):
    rows = grid // PEN
    parts = []
    for device in range(PEN):
        ky = device * rows + np.arange(rows)[:, None]
        y = np.arange(grid)[None, :]
        parts += [cosine(grid, ky, y), -sine(grid, ky, y)]
    return split_table(np.concatenate([np.concatenate(parts[:4]), np.concatenate(parts[4:])], axis=1))


def dot(left, right):
    return jnp.dot(left, right, preferred_element_type=jnp.float32)


def dot_split(left, right):
    return dot(left[0], right[0]) + (dot(left[1], right[0]) + dot(left[0], right[1]))


def waves(position, grid):
    signed = jnp.where(position <= grid // 2, position, position - grid)
    derivative = jnp.where(position == grid // 2, 0, signed)
    return (2.0 * math.pi / grid) * derivative.astype(jnp.float32), signed


def wave_arrays(row_position, grid):
    kappa_y, signed_y = waves(row_position, grid)
    kappa_x, signed_x = waves(lax.broadcasted_iota(jnp.int32, (1, grid), 1), grid)
    wave_square = signed_y * signed_y + signed_x * signed_x
    factor = (2.0 * math.pi / grid) ** 2
    square = factor * wave_square.astype(jnp.float32)
    inverse = jnp.where(wave_square > 0, 1.0 / jnp.where(wave_square > 0, square, 1.0), 0.0)
    return kappa_y, kappa_x, square, inverse


def interleave(even, odd):
    low_lanes = lax.broadcasted_iota(jnp.int32, (1, 128), 1) < 64
    return (
        jnp.where(low_lanes, even, pltpu.roll(odd, 64, 1)),
        jnp.where(low_lanes, pltpu.roll(even, 64, 1), odd),
    )


def base_kernel(base_ref, own_ref, swap_ref):
    mine = (lax.axis_index("pen") % 2) * 2
    for out_ref, first in ((own_ref, mine), (swap_ref, 2 - mine)):
        for field in range(base_ref.shape[0]):
            out_ref[:, 128 * field : 128 * field + 128] = jnp.concatenate(
                [base_ref[field, first], base_ref[field, first + 1]], axis=1
            )


def near_kernel(block_ref, state_ref, swap_ref, near_ref, far_ref):
    mine = (lax.axis_index("pen") % 2) * 2
    tall = block_ref.shape[0]
    swap_ref[:tall, :] = block_ref[...]
    swap_ref[tall:, :] = jnp.zeros((EXTRA, swap_ref.shape[1]), jnp.float32)
    far_ref[...] = jnp.zeros_like(far_ref)
    for index in range(4):
        field, level = index // 2, index % 2
        line = state_ref[field, 0, 2 - mine + level, 0:1, :]
        near_ref[index] = state_ref[field, 0, mine + level]
        far_ref[index : index + 1, :] = line
        swap_ref[tall + index : tall + index + 1, : far_ref.shape[1]] = line


def x_stage(grid, table, ky, held):
    count = held[0].shape[0]
    kappa_y, kappa_x, _, inverse = wave_arrays(ky, grid)
    fields = [
        (0, inverse, kappa_y),
        (0, -kappa_x * inverse, None),
        (0, kappa_x, None),
        (0, None, kappa_y),
        (1, kappa_x, None),
        (1, None, kappa_y),
    ]
    for field, before, after in fields:
        stacked = []
        for level in range(2):
            for columns in (slice(0, grid), slice(grid, 2 * grid)):
                values = held[2 * field + level][:, columns]
                stacked.append(values if before is None else values * before)
        product = dot_split(split(jnp.concatenate(stacked, axis=0)), table)
        results = []
        for level in range(2):
            top = product[2 * level * count : (2 * level + 1) * count]
            bottom = product[(2 * level + 1) * count : (2 * level + 2) * count]
            real = -(bottom[:, :128] + top[:, 128:])
            imag = top[:, :128] - bottom[:, 128:]
            results.append((real, imag) if after is None else (after * real, after * imag))
        yield results


def x_columns(grid, x_ref):
    start = pl.multiple_of((lax.axis_index("pen") // 2) * 128, 128)
    return [
        jnp.concatenate(
            [x_ref[part, :, pl.ds(start, 128)], x_ref[part, :, pl.ds(grid + start, 128)]], axis=1
        )
        for part in range(2)
    ]


def own_rows_kernel(grid, state_ref, x_ref, real_ref, imag_ref):
    rows = state_ref.shape[3]
    pen = lax.axis_index("pen")
    mine = (pen % 2) * 2
    held = [state_ref[field, 0, mine + level] for field in range(2) for level in range(2)]
    ky = pen * rows + lax.broadcasted_iota(jnp.int32, (rows, 1), 0)
    for number, results in enumerate(x_stage(grid, x_columns(grid, x_ref), ky, held)):
        for level, (real, imag) in enumerate(results):
            real_ref[level, number] = real
            imag_ref[level, number] = imag


def inverse_kernel(
    grid, near_ref, far_ref, came_ref, own_real, own_imag, x_ref, y_ref, own_ref, swap_ref, mixed, high_ref, low_ref, y_held, sem
):
    y_copy = pltpu.make_async_copy(y_ref.at[lax.axis_index("pen")], y_held, sem)
    y_copy.start()
    rows = own_real.shape[2]
    pen = lax.axis_index("pen")
    odd = pen % 2 == 1
    count = rows + EXTRA
    tall = came_ref.shape[0] - EXTRA
    held = [
        jnp.concatenate(
            [
                near_ref[index],
                came_ref[tall + index : tall + index + 1, : 2 * grid],
                far_ref[index : index + 1, :],
                jnp.zeros((EXTRA - 2, 2 * grid), jnp.float32),
            ],
            axis=0,
        )
        for index in range(4)
    ]
    row = lax.broadcasted_iota(jnp.int32, (count, 1), 0)
    ky = jnp.where(row < rows, (pen ^ 2) * rows + row, (pen ^ 1) * rows)
    ky = jnp.where(row > rows, (pen ^ 3) * rows, ky)
    for number, results in enumerate(x_stage(grid, x_columns(grid, x_ref), ky, held)):
        for level, (real, imag) in enumerate(results):
            first_imag = own_imag[level, number, 0:1, :]
            mixed[level, :rows, :] = own_real[level, number]
            mixed[level, rows : 2 * rows, :] = real[:rows]
            mixed[level, 2 * rows : 3 * rows, :] = own_imag[level, number]
            mixed[level, 3 * rows :, :] = imag[:rows]
            near_real, near_imag = real[rows : rows + 1], imag[rows : rows + 1]
            far_real = real[rows + 1 : rows + 2]
            mixed[level, rows : rows + 1, :] = jnp.where(odd, near_real, real[0:1])
            mixed[level, 2 * rows : 2 * rows + 1, :] = jnp.where(odd, first_imag, near_real)
            mixed[level, 3 * rows : 3 * rows + 1, :] = jnp.where(odd, far_real, near_imag)
        for block, values in enumerate(interleave(mixed[0], mixed[1])):
            high, low = split(values)
            high_ref[block ^ (pen % 2), :, 128 * number : 128 * number + 128] = high
            low_ref[block ^ (pen % 2), :, 128 * number : 128 * number + 128] = low
    y_copy.wait()
    left = (y_held[0], y_held[1])
    own_ref[...] = dot_split(left, (high_ref[0], low_ref[0]))
    swap_ref[...] = dot_split(left, (high_ref[1], low_ref[1]))


def advection_kernel(places, field, own_ref, swap_ref, *refs):
    packs, (table_ref, *outs, high_ref, low_ref) = refs[:2], refs[2:]
    ens = lax.axis_index("ens")
    tall = packs[0].shape[0] // len(places)
    for which in range(2):
        for slot, (offset, chunk) in enumerate(places):
            place = pl.ds(pl.multiple_of((ens ^ offset ^ which) * tall, tall), tall)
            along_ref = (own_ref, swap_ref)[chunk]

            def base(index, which=which, slot=slot):
                return packs[which][tall * slot : tall * (slot + 1), 128 * index : 128 * index + 128]

            def along(index, place=place, along_ref=along_ref):
                return along_ref[place, 128 * index : 128 * index + 128]

            first = 2 + 2 * field
            total = (
                base(0) * along(first)
                + base(1) * along(first + 1)
                + along(0) * base(first)
                + along(1) * base(first + 1)
            )
            lanes = slice(128 * chunk, 128 * chunk + 128)
            high_ref[place, lanes], low_ref[place, lanes] = split(total)
    pen = lax.axis_index("pen")
    grid = table_ref.shape[1]
    rows = grid // PEN
    for step in range(PEN):
        target = pen ^ step
        place = pl.ds(pl.multiple_of((target % 2) * 2 * rows, 2 * rows), 2 * rows)
        lanes = pl.ds(pl.multiple_of((target // 2) * grid, grid), grid)
        outs[step][...] = dot_split(
            (table_ref[2, place, lanes], table_ref[3, place, lanes]), (high_ref[...], low_ref[...])
        )


def final_kernel(grid, field, *refs):
    messages, (state_ref, accum_ref, table_ref) = refs[:PEN], refs[PEN : PEN + 3]
    state_out, accum_out, gathered, state_next, accum_next, sems = refs[-6:]
    rows, levels = state_ref.shape[3], state_ref.shape[2]
    pen = lax.axis_index("pen")
    for step in range(PEN):
        gathered[pen ^ step] = messages[step][...]
    row = lax.broadcasted_iota(jnp.int32, (rows, 1), 0)
    _, kappa_x, square, inverse = wave_arrays(pen * rows + row, grid)
    table = (table_ref[0], table_ref[1])
    real, imag = slice(0, grid), slice(grid, 2 * grid)
    copies = []
    for pair in range(levels // 2):
        first, second = [slice(128 * chunk, 128 * chunk + 128) for chunk in (pair, 1 - pair)]
        halves = [
            interleave(gathered[pair + 2 * block, :, first], gathered[pair + 2 * block, :, second])
            for block in range(2)
        ]
        left = jnp.concatenate(
            [jnp.concatenate([half[level] for half in halves], axis=1) for level in range(2)], axis=0
        )
        product = dot_split(split(left), table)
        for level in (2 * pair, 2 * pair + 1):
            start = 2 * rows * (level - 2 * pair)
            top, bottom = product[start : start + rows], product[start + rows : start + 2 * rows]
            for columns, other, sign, advect in (
                (real, imag, 1.0, top[:, :grid] + bottom[:, grid:]),
                (imag, real, -1.0, bottom[:, :grid] - top[:, grid:]),
            ):
                here = state_ref[field, 0, level, :, columns]
                above = state_ref[field, 0, min(level + 1, levels - 1), :, columns]
                below = state_ref[field, 0, max(level - 1, 0), :, columns]
                cross = state_ref[1 - field, 0, level, :, other]
                if field == 0:
                    coupling = (-sign * buoyancy_gain) * (kappa_x * cross)
                else:
                    coupling = (-sign * stratification) * (kappa_x * inverse * cross)
                damping = viscosity if field == 0 else diffusivity
                memory = (
                    memory_factor * accum_ref[field, 0, level, :, columns]
                    - advect
                    + coupling
                    - damping * square * here
                    + vertical_mixing * (above + below - 2.0 * here)
                )
                accum_next[level, :, columns] = memory
                state_next[level, :, columns] = here + weight_factor * time_step * memory
            for which, (held, out) in enumerate(((state_next, state_out), (accum_next, accum_out))):
                copy = pltpu.make_async_copy(
                    held.at[level], out.at[field, 0, level], sems.at[which, level]
                )
                copy.start()
                copies.append(copy)
    for copy in copies:
        copy.wait()


def pack_kernel(*refs):
    start, total = 0, refs[-1].shape[0]
    for ref in refs[:-1]:
        count = min(ref.shape[0], total - start)
        refs[-1][start : start + count, :] = ref[:count, :]
        start += count


def call(kernel, outs, scratch, cost, args, after=(), into=None, outside=()):
    args, after = list(args), list(after) + list(into or ())
    count, total = len(args), len(args) + len(after)
    size = sum(math.prod(a.shape) * a.dtype.itemsize for a in args + list(outs))
    first = total - len(into or ())
    return pl.pallas_call(
        lambda *refs: kernel(*refs[:count], *refs[total:]),
        out_shape=outs,
        in_specs=[
            pl.BlockSpec(memory_space=pl.ANY if index in outside else pltpu.VMEM) for index in range(count)
        ]
        + [pl.BlockSpec(memory_space=pl.ANY)] * len(after),
        out_specs=[pl.BlockSpec(memory_space=pltpu.VMEM if into is None else pl.ANY)] * len(outs),
        scratch_shapes=scratch,
        input_output_aliases={first + index: index for index in range(total - first)},
        compiler_params=pltpu.CompilerParams(vmem_limit_bytes=24 * 1024 * 1024),
        cost_estimate=pl.CostEstimate(flops=cost, bytes_accessed=size, transcendentals=0),
        name=getattr(kernel, "func", kernel).__name__,
    )(*args, *after)


def exchange(values, axis, size, mask):
    return lax.ppermute(values, axis, [(index, index ^ mask) for index in range(size)])


def pack(arrays, cost=0, after=(), drop=0):
    total = sum(array.shape[0] for array in arrays) - drop
    shape = jax.ShapeDtypeStruct((total, arrays[0].shape[1]), arrays[0].dtype)
    return call(pack_kernel, [shape], [], cost, arrays, after=after)[0]


def on_device(axes, state, accum, base_flow):
    grid, rows, levels = state.shape[-1] // 2, state.shape[3], state.shape[2]
    size = axes["ens"]
    if axes["pen"] != PEN or levels != 4 or grid != 256 or size != 8:
        return on_device_general(state, accum, base_flow)
    f32, bf16 = jnp.float32, jnp.bfloat16
    shape = functools.partial(jax.ShapeDtypeStruct, dtype=f32)
    fields, _, wide, tall = base_flow.shape
    lanes = 2 * wide
    base_lanes = fields * lanes
    table = jnp.asarray(np.concatenate([x_table(grid), y_forward_table(grid)]))
    y_table = y_inverse_table(grid)

    def near(values, mask):
        return exchange(values, "ens", size, mask)

    def across(values, mask):
        return exchange(values, ("ens", "pen"), size * PEN, mask * PEN + 1)

    own_base, swap_base = call(
        base_kernel, [shape((tall, base_lanes))] * 2, [], 0, [jnp.swapaxes(base_flow, 2, 3)]
    )
    own_far, swap_far = near(own_base, 6), across(swap_base, 6)
    swap_message, rows_message, far_message = call(
        near_kernel,
        [shape((tall + EXTRA, base_lanes)), shape((4, rows, 2 * grid)), shape((EXTRA, 2 * grid))],
        [],
        0,
        [swap_base, state],
        after=[own_base],
    )
    near_rows = exchange(rows_message, "pen", PEN, 2)
    own_near = near(pack([own_base], after=[rows_message]), 2)
    swap_near = across(pack([swap_base], after=[rows_message]), 2)
    came = exchange(swap_message, "pen", PEN, 1)
    far_rows = exchange(far_message, "pen", PEN, 3)
    swap_forward, own_forward = [near(pack([far], HINT["forward"]), 2) for far in (swap_far, own_far)]
    own_parts = call(
        functools.partial(own_rows_kernel, grid),
        [shape((2, fields, rows, lanes))] * 2,
        [],
        HINT["own"],
        [state, table],
            )
    own_fields, swap_fields = call(
        functools.partial(inverse_kernel, grid),
        [shape((grid, base_lanes))] * 2,
        [
            pltpu.VMEM((2, 4 * rows, lanes), f32),
            pltpu.VMEM((2, grid, base_lanes), bf16),
            pltpu.VMEM((2, grid, base_lanes), bf16),
            pltpu.VMEM(y_table.shape[1:], bf16),
            pltpu.SemaphoreType.DMA,
        ],
        HINT["inverse"],
        [near_rows, far_rows, came, *own_parts, table, jnp.asarray(y_table)],
        outside=(6,),
    )
    places = ((0, 0), (6, 0), (6, 1), (2, 0), (2, 1), (4, 0), (4, 1), (0, 1))
    packed = pack(
        [own_base, own_far, swap_far, own_near, swap_near, own_forward, swap_forward, came], HINT["pack"], (), EXTRA
    )
    partner = near(packed, 1)
    result = ()
    returns = []
    for field in range(2):
        messages = call(
            functools.partial(advection_kernel, places, field),
            [shape((2 * rows, 2 * lanes))] * PEN,
            [pltpu.VMEM((grid, 2 * lanes), bf16)] * 2,
            HINT["advect"][field],
            [own_fields, swap_fields, packed, partner, table],
        )
        returns.append(
            [messages[0]] + [exchange(messages[step], "pen", PEN, step) for step in range(1, PEN)]
        )
    for field, back in enumerate(returns):
        result = call(
            functools.partial(final_kernel, grid, field),
            [shape(state.shape)] * 2,
            [
                pltpu.VMEM((PEN, 2 * rows, 2 * lanes), f32),
                pltpu.VMEM((levels, rows, 2 * grid), f32),
                pltpu.VMEM((levels, rows, 2 * grid), f32),
                pltpu.SemaphoreType.DMA((2, levels)),
            ],
            HINT["final"] if field == 0 else 0,
            [*back, state, accum, table],
            into=result,
        )
    return tuple(result)


def solution(mesh):
    return jax.shard_map(
        functools.partial(on_device, dict(mesh.shape)),
        mesh=mesh,
        in_specs=(
            P(None, "ens", None, "pen", None),
            P(None, "ens", None, "pen", None),
            P(None, None, "pen", "ens"),
        ),
        out_specs=(P(None, "ens", None, "pen", None), P(None, "ens", None, "pen", None)),
        check_vma=False,
    )
```

```python
import functools
import math

import jax
import jax.numpy as jnp
import ml_dtypes
import numpy as np
from jax import lax
from jax.experimental import pallas as pl
from jax.experimental.pallas import tpu as pltpu
from jax.sharding import PartitionSpec as P

viscosity = 0.05
diffusivity = 0.05
vertical_mixing = 0.5
buoyancy_gain = 0.5
stratification = 0.5
memory_factor = -5.0 / 9.0
weight_factor = 15.0 / 16.0
time_step = 0.4


def wave_numbers(amount, offset, length):
    position = offset + jnp.arange(amount, dtype=jnp.int32)
    half_length = length // 2
    signed = jnp.where(position <= half_length, position, position - length)
    derivative = jnp.where(position == half_length, 0, signed)
    return (2.0 * math.pi / length * derivative.astype(jnp.float32), signed)


def times_i(real_part, imag_part, factor):
    return (-factor * imag_part, factor * real_part)


def vertical(quantity, level_axis):
    depth = quantity.shape[level_axis]
    lower = lax.slice_in_dim(quantity, 0, 1, axis=level_axis)
    upper = lax.slice_in_dim(quantity, depth - 1, depth, axis=level_axis)
    padded = jnp.concatenate([lower, quantity, upper], axis=level_axis)
    above = lax.slice_in_dim(padded, 2, depth + 2, axis=level_axis)
    below = lax.slice_in_dim(padded, 0, depth, axis=level_axis)
    return above + below - 2.0 * quantity


def tendency(vort, buoy, advect, across, kappa_x, square, level_axis):
    tend_vort_re = (
        -advect[0]
        + buoyancy_gain * (-kappa_x * buoy[1])
        - viscosity * square * vort[0]
        + vertical_mixing * vertical(vort[0], level_axis)
    )
    tend_vort_im = (
        -advect[1]
        + buoyancy_gain * (kappa_x * buoy[0])
        - viscosity * square * vort[1]
        + vertical_mixing * vertical(vort[1], level_axis)
    )
    tend_buoy_re = (
        -advect[2]
        - stratification * across[0]
        - diffusivity * square * buoy[0]
        + vertical_mixing * vertical(buoy[0], level_axis)
    )
    tend_buoy_im = (
        -advect[3]
        - stratification * across[1]
        - diffusivity * square * buoy[1]
        + vertical_mixing * vertical(buoy[1], level_axis)
    )
    return jnp.stack(
        [
            jnp.concatenate([tend_vort_re, tend_vort_im], axis=-1),
            jnp.concatenate([tend_buoy_re, tend_buoy_im], axis=-1),
        ]
    )


def dft_tables(length):
    position = jnp.arange(length, dtype=jnp.int32)
    product = position[:, None] * position[None, :] % length
    angle = 2.0 * math.pi / length * product.astype(jnp.float32)
    scale = 1.0 / math.sqrt(length)
    return (scale * jnp.cos(angle), scale * jnp.sin(angle))


def to_physical(spectral, x_table, y_table):
    mixed_space = jnp.einsum(
        "fplkj,jcx->fplcxk", spectral, x_table, precision=lax.Precision.HIGHEST
    )
    return jnp.einsum(
        "fplcxk,ckm->fplxm",
        lax.all_to_all(mixed_space, "pen", split_axis=4, concat_axis=5, tiled=True),
        y_table,
        precision=lax.Precision.HIGHEST,
    )


def on_device_general(state, accum, base_flow):
    grid_size = state.shape[-1] // 2
    row_count = state.shape[3]
    base_all = lax.all_gather(base_flow, "ens", axis=3, tiled=True)
    kappa_rows, signed_y = wave_numbers(row_count, lax.axis_index("pen") * row_count, grid_size)
    kappa_cols, signed_x = wave_numbers(grid_size, 0, grid_size)
    kappa_y = kappa_rows[:, None]
    kappa_x = kappa_cols[None, :]
    wave_square = signed_y[:, None] ** 2 + signed_x[None, :] ** 2
    factor = (2.0 * math.pi / grid_size) ** 2
    square = factor * wave_square.astype(jnp.float32)
    inverse = jnp.where(
        wave_square > 0, 1.0 / (factor * jnp.maximum(wave_square, 1).astype(jnp.float32)), 0.0
    )
    vort = (state[0][..., :grid_size], state[0][..., grid_size:])
    buoy = (state[1][..., :grid_size], state[1][..., grid_size:])
    potential_re = -vort[0] * inverse
    potential_im = -vort[1] * inverse
    flow_x = times_i(potential_re, potential_im, -kappa_y)
    flow_y = times_i(potential_re, potential_im, kappa_x)
    vort_x = times_i(vort[0], vort[1], kappa_x)
    vort_y = times_i(vort[0], vort[1], kappa_y)
    buoy_x = times_i(buoy[0], buoy[1], kappa_x)
    buoy_y = times_i(buoy[0], buoy[1], kappa_y)
    cosine_table, sine_table = dft_tables(grid_size)
    x_table = jnp.concatenate(
        [
            jnp.stack([cosine_table, sine_table], axis=1),
            jnp.stack([-sine_table, cosine_table], axis=1),
        ],
        axis=0,
    )
    y_table = jnp.stack([cosine_table, -sine_table])
    components = [flow_x, flow_y, vort_x, vort_y, buoy_x, buoy_y]
    spectral = jnp.stack([jnp.concatenate(component, axis=-1) for component in components])
    physical = to_physical(spectral, x_table, y_table)
    flow_x_p, flow_y_p = (physical[0], physical[1])
    vort_x_p, vort_y_p = (physical[2], physical[3])
    buoy_x_p, buoy_y_p = (physical[4], physical[5])
    advect_vort = (
        base_all[0] * vort_x_p
        + base_all[1] * vort_y_p
        + flow_x_p * base_all[2]
        + flow_y_p * base_all[3]
    )
    advect_buoy = (
        base_all[0] * buoy_x_p
        + base_all[1] * buoy_y_p
        + flow_x_p * base_all[4]
        + flow_y_p * base_all[5]
    )
    advect_both = jnp.stack([advect_vort, advect_buoy])
    y_forward = jnp.stack([cosine_table, -sine_table], axis=1)
    x_forward = jnp.stack(
        [
            jnp.concatenate([cosine_table, -sine_table], axis=1),
            jnp.concatenate([sine_table, cosine_table], axis=1),
        ]
    )
    spread = jnp.einsum(
        "fplxy,yck->fplckx", advect_both, y_forward, precision=lax.Precision.HIGHEST
    )
    spectra = jnp.einsum(
        "fplckx,cxm->fplkm",
        lax.all_to_all(spread, "pen", split_axis=4, concat_axis=5, tiled=True),
        x_forward,
        precision=lax.Precision.HIGHEST,
    )
    advect = (
        spectra[0][..., :grid_size],
        spectra[0][..., grid_size:],
        spectra[1][..., :grid_size],
        spectra[1][..., grid_size:],
    )
    tend = tendency(vort, buoy, advect, flow_y, kappa_x, square, 1)
    accum_next = memory_factor * accum + tend
    state_next = state + weight_factor * time_step * accum_next
    return (state_next, accum_next)


PEN = 4
EXTRA = 8
NEAR_X = 16
HINT = dict(own=0, inverse=10**10, forward=5 * 10**9, early=0, pack=0, advect=(0, 0), linear=0)


def split(values):
    high = values.astype(jnp.bfloat16)
    return high, (values - high.astype(jnp.float32)).astype(jnp.bfloat16)


def split_table(values):
    high = values.astype(ml_dtypes.bfloat16)
    low = (values - high.astype(np.float64)).astype(ml_dtypes.bfloat16)
    return np.stack([high, low], axis=-3)


def cosine(grid, left, right):
    return np.cos(2.0 * np.pi / grid * (left * right % grid)) / math.sqrt(grid)


def sine(grid, left, right):
    return np.sin(2.0 * np.pi / grid * (left * right % grid)) / math.sqrt(grid)


def x_table(grid):
    kx = np.arange(grid)
    x = kx[:, None]
    return split_table(np.concatenate([cosine(grid, x, kx), sine(grid, x, kx)], axis=1))


def row_numbers(device, rows):
    own = device * rows + np.arange(rows)
    near = [(device ^ step) * rows + np.arange(count) for step, count in ((1, NEAR_X), (2, rows - NEAR_X))]
    return np.concatenate([own] + near)


def y_inverse_table(grid):
    rows = grid // PEN
    y = np.arange(grid)[:, None]
    tables = []
    for device in range(PEN):
        ky = row_numbers(device, rows)
        real = np.where(ky % (grid // 2) == 0, 1.0, 2.0) * cosine(grid, y, ky)
        imag = -2.0 * sine(grid, y, ky)
        extra = (device ^ 1) * rows + NEAR_X
        far = (device ^ 3) * rows
        from_y = rows + NEAR_X
        extra_real, extra_imag = 2.0 * cosine(grid, y[:, 0], extra), -2.0 * sine(grid, y[:, 0], extra)
        imag[:, from_y] = extra_imag
        if device % 2 == 0:
            imag[:, 0] = extra_real
        else:
            real[:, from_y] = extra_real
            imag[:, rows] = cosine(grid, y[:, 0], far)
        tables.append(np.concatenate([real, imag], axis=1))
    return split_table(np.stack(tables))


def y_forward_table(grid):
    rows = grid // PEN
    parts = []
    for device in range(PEN):
        ky = device * rows + np.arange(rows)[:, None]
        y = np.arange(grid)[None, :]
        parts += [cosine(grid, ky, y), -sine(grid, ky, y)]
    return split_table(np.concatenate([np.concatenate(parts[:4]), np.concatenate(parts[4:])], axis=1))


def dot(left, right):
    return jnp.dot(left, right, preferred_element_type=jnp.float32)


def dot_split(left, right):
    return dot(left[0], right[0]) + (dot(left[1], right[0]) + dot(left[0], right[1]))


def waves(position, grid):
    signed = jnp.where(position <= grid // 2, position, position - grid)
    derivative = jnp.where(position == grid // 2, 0, signed)
    return (2.0 * math.pi / grid) * derivative.astype(jnp.float32), signed


def wave_arrays(row_position, grid):
    kappa_y, signed_y = waves(row_position, grid)
    kappa_x, signed_x = waves(lax.broadcasted_iota(jnp.int32, (1, grid), 1), grid)
    wave_square = signed_y * signed_y + signed_x * signed_x
    factor = (2.0 * math.pi / grid) ** 2
    square = factor * wave_square.astype(jnp.float32)
    inverse = jnp.where(wave_square > 0, 1.0 / jnp.where(wave_square > 0, square, 1.0), 0.0)
    return kappa_y, kappa_x, square, inverse


def interleave(even, odd):
    low_lanes = lax.broadcasted_iota(jnp.int32, (1, 128), 1) < 64
    return (
        jnp.where(low_lanes, even, pltpu.roll(odd, 64, 1)),
        jnp.where(low_lanes, pltpu.roll(even, 64, 1), odd),
    )


def base_kernel(base_ref, own_ref, swap_ref):
    mine = (lax.axis_index("pen") % 2) * 2
    for out_ref, first in ((own_ref, mine), (swap_ref, 2 - mine)):
        for field in range(base_ref.shape[0]):
            out_ref[:, 128 * field : 128 * field + 128] = jnp.concatenate(
                [base_ref[field, first], base_ref[field, first + 1]], axis=1
            )


def near_kernel(block_ref, state_ref, swap_ref, near_ref, far_ref):
    mine = (lax.axis_index("pen") % 2) * 2
    width = swap_ref.shape[1]
    tall, lanes = block_ref.shape
    swap_ref[:tall, :] = block_ref[:, :width]
    half = tall // 2
    swap_ref[tall : tall + half, : lanes - width] = block_ref[:half, width:]
    swap_ref[tall : tall + half, lanes - width :] = block_ref[half:, width:]
    start = tall + half
    swap_ref[start + 4 * NEAR_X :, :] = jnp.zeros((EXTRA, width), jnp.float32)
    far_ref[...] = jnp.zeros_like(far_ref)
    for index in range(4):
        field, level = index // 2, index % 2
        rows = state_ref[field, 0, 2 - mine + level, : NEAR_X + EXTRA, :]
        swap_ref[start + NEAR_X * index : start + NEAR_X * (index + 1), :] = rows[:NEAR_X]
        line = start + 4 * NEAR_X + index
        swap_ref[line : line + 1, :] = rows[NEAR_X : NEAR_X + 1]
        far_ref[index : index + 1, :] = rows[:1]
        near_ref[index] = state_ref[field, 0, mine + level, : near_ref.shape[1], :]


def x_stage(grid, table, ky, held):
    count = held[0].shape[0]
    kappa_y, kappa_x, _, inverse = wave_arrays(ky, grid)
    fields = [
        (0, inverse, kappa_y),
        (0, -kappa_x * inverse, None),
        (0, kappa_x, None),
        (0, None, kappa_y),
        (1, kappa_x, None),
        (1, None, kappa_y),
    ]
    for field, before, after in fields:
        stacked = []
        for level in range(2):
            for columns in (slice(0, grid), slice(grid, 2 * grid)):
                values = held[2 * field + level][:, columns]
                stacked.append(values if before is None else values * before)
        product = dot_split(split(jnp.concatenate(stacked, axis=0)), table)
        results = []
        for level in range(2):
            top = product[2 * level * count : (2 * level + 1) * count]
            bottom = product[(2 * level + 1) * count : (2 * level + 2) * count]
            real = -(bottom[:, :128] + top[:, 128:])
            imag = top[:, :128] - bottom[:, 128:]
            results.append((real, imag) if after is None else (after * real, after * imag))
        yield results


def x_columns(grid, x_ref):
    start = pl.multiple_of((lax.axis_index("pen") // 2) * 128, 128)
    return [
        jnp.concatenate(
            [x_ref[part, :, pl.ds(start, 128)], x_ref[part, :, pl.ds(grid + start, 128)]], axis=1
        )
        for part in range(2)
    ]


def own_rows_kernel(grid, state_ref, x_ref, real_ref, imag_ref):
    rows = state_ref.shape[3]
    pen = lax.axis_index("pen")
    mine = (pen % 2) * 2
    held = [state_ref[field, 0, mine + level] for field in range(2) for level in range(2)]
    ky = pen * rows + lax.broadcasted_iota(jnp.int32, (rows, 1), 0)
    for number, results in enumerate(x_stage(grid, x_columns(grid, x_ref), ky, held)):
        for level, (real, imag) in enumerate(results):
            real_ref[level, number] = real
            imag_ref[level, number] = imag


def inverse_kernel(
    grid, near_ref, far_ref, came_ref, own_real, own_imag, x_ref, y_ref, own_ref, swap_ref, mixed, high_ref, low_ref, y_held, sem
):
    y_copy = pltpu.make_async_copy(y_ref.at[lax.axis_index("pen")], y_held, sem)
    y_copy.start()
    rows = own_real.shape[2]
    pen = lax.axis_index("pen")
    odd = pen % 2 == 1
    count = rows + EXTRA
    start = came_ref.shape[0] - 4 * NEAR_X - EXTRA
    held = [
        jnp.concatenate(
            [
                came_ref[start + NEAR_X * index : start + NEAR_X * (index + 1), :],
                near_ref[index],
                came_ref[start + 4 * NEAR_X + index : start + 4 * NEAR_X + index + 1, :],
                far_ref[index : index + 1, :],
                jnp.zeros((EXTRA - 2, 2 * grid), jnp.float32),
            ],
            axis=0,
        )
        for index in range(4)
    ]
    row = lax.broadcasted_iota(jnp.int32, (count, 1), 0)
    ky = jnp.where(row < NEAR_X, (pen ^ 1) * rows + row, (pen ^ 2) * rows + row - NEAR_X)
    ky = jnp.where(row == rows, (pen ^ 1) * rows + NEAR_X, ky)
    ky = jnp.where(row > rows, (pen ^ 3) * rows, ky)
    from_y = rows + NEAR_X
    for number, results in enumerate(x_stage(grid, x_columns(grid, x_ref), ky, held)):
        for level, (real, imag) in enumerate(results):
            first_imag = own_imag[level, number, 0:1, :]
            mixed[level, :rows, :] = own_real[level, number]
            mixed[level, rows : 2 * rows, :] = real[:rows]
            mixed[level, 2 * rows : 3 * rows, :] = own_imag[level, number]
            mixed[level, 3 * rows :, :] = imag[:rows]
            extra_real, extra_imag = real[rows : rows + 1], imag[rows : rows + 1]
            far_real = real[rows + 1 : rows + 2]
            mixed[level, from_y : from_y + 1, :] = jnp.where(
                odd, extra_real, real[NEAR_X : NEAR_X + 1]
            )
            mixed[level, 2 * rows : 2 * rows + 1, :] = jnp.where(odd, first_imag, extra_real)
            mixed[level, 3 * rows : 3 * rows + 1, :] = jnp.where(odd, far_real, imag[0:1])
            mixed[level, 2 * rows + from_y : 2 * rows + from_y + 1, :] = extra_imag
        for block, values in enumerate(interleave(mixed[0], mixed[1])):
            high, low = split(values)
            high_ref[block ^ (pen % 2), :, 128 * number : 128 * number + 128] = high
            low_ref[block ^ (pen % 2), :, 128 * number : 128 * number + 128] = low
    y_copy.wait()
    left = (y_held[0], y_held[1])
    own_ref[...] = dot_split(left, (high_ref[0], low_ref[0]))
    swap_ref[...] = dot_split(left, (high_ref[1], low_ref[1]))


def advection_kernel(places, field, own_ref, swap_ref, *refs):
    packs, (table_ref, *outs, high_ref, low_ref) = refs[:4], refs[4:]
    ens = lax.axis_index("ens")
    for group, which in [(group, which) for group in range(2) for which in range(2)]:
        pack_ref = packs[2 * group + which]
        tall = pack_ref.shape[0] // len(places[group])
        for slot, (offset, chunk) in enumerate(places[group]):
            place = pl.ds(pl.multiple_of((ens ^ offset ^ which) * tall, tall), tall)
            along_ref = (own_ref, swap_ref)[chunk]

            def base(index, pack_ref=pack_ref, slot=slot, tall=tall):
                return pack_ref[tall * slot : tall * (slot + 1), 128 * index : 128 * index + 128]

            def along(index, place=place, along_ref=along_ref):
                return along_ref[place, 128 * index : 128 * index + 128]

            first = 2 + 2 * field
            total = (
                base(0) * along(first)
                + base(1) * along(first + 1)
                + along(0) * base(first)
                + along(1) * base(first + 1)
            )
            lanes = slice(128 * chunk, 128 * chunk + 128)
            high_ref[place, lanes], low_ref[place, lanes] = split(total)
    pen = lax.axis_index("pen")
    grid = table_ref.shape[1]
    rows = grid // PEN
    for step in range(PEN):
        target = pen ^ step
        place = pl.ds(pl.multiple_of((target % 2) * 2 * rows, 2 * rows), 2 * rows)
        lanes = pl.ds(pl.multiple_of((target // 2) * grid, grid), grid)
        outs[step][...] = dot_split(
            (table_ref[2, place, lanes], table_ref[3, place, lanes]), (high_ref[...], low_ref[...])
        )


def linear_kernel(grid, state_ref, accum_ref, out_ref):
    rows, levels = state_ref.shape[3], state_ref.shape[2]
    row = lax.broadcasted_iota(jnp.int32, (rows, 1), 0)
    _, kappa_x, square, inverse = wave_arrays(lax.axis_index("pen") * rows + row, grid)
    real, imag = slice(0, grid), slice(grid, 2 * grid)
    for field in range(2):
        factor = kappa_x * buoyancy_gain if field == 0 else kappa_x * inverse * stratification
        damping = (viscosity if field == 0 else diffusivity) * square
        for level in range(levels):
            for columns, other, sign in ((real, imag, 1.0), (imag, real, -1.0)):
                here = state_ref[field, 0, level, :, columns]
                above = state_ref[field, 0, min(level + 1, levels - 1), :, columns]
                below = state_ref[field, 0, max(level - 1, 0), :, columns]
                out_ref[field, 0, level, :, columns] = (
                    memory_factor * accum_ref[field, 0, level, :, columns]
                    - sign * factor * state_ref[1 - field, 0, level, :, other]
                    - damping * here
                    + vertical_mixing * (above + below - 2.0 * here)
                )


def final_kernel(grid, field, *refs):
    messages, (state_ref, part_ref, table_ref) = refs[:PEN], refs[PEN : PEN + 3]
    state_out, accum_out, gathered, state_next, accum_next, sems = refs[-6:]
    rows, levels = state_ref.shape[3], state_ref.shape[2]
    pen = lax.axis_index("pen")
    for step in range(PEN):
        gathered[pen ^ step] = messages[step][...]
    table = (table_ref[0], table_ref[1])
    real, imag = slice(0, grid), slice(grid, 2 * grid)
    copies = []
    for pair in range(levels // 2):
        first, second = [slice(128 * chunk, 128 * chunk + 128) for chunk in (pair, 1 - pair)]
        halves = [
            interleave(gathered[pair + 2 * block, :, first], gathered[pair + 2 * block, :, second])
            for block in range(2)
        ]
        left = jnp.concatenate(
            [jnp.concatenate([half[level] for half in halves], axis=1) for level in range(2)], axis=0
        )
        product = dot_split(split(left), table)
        for level in (2 * pair, 2 * pair + 1):
            start = 2 * rows * (level - 2 * pair)
            top, bottom = product[start : start + rows], product[start + rows : start + 2 * rows]
            for columns, advect in (
                (real, top[:, :grid] + bottom[:, grid:]),
                (imag, bottom[:, :grid] - top[:, grid:]),
            ):
                memory = part_ref[field, 0, level, :, columns] - advect
                accum_next[level, :, columns] = memory
                state_next[level, :, columns] = (
                    state_ref[field, 0, level, :, columns] + weight_factor * time_step * memory
                )
            for which, (held, out) in enumerate(((state_next, state_out), (accum_next, accum_out))):
                copy = pltpu.make_async_copy(
                    held.at[level], out.at[field, 0, level], sems.at[which, level]
                )
                copy.start()
                copies.append(copy)
    for copy in copies:
        copy.wait()


def pack_kernel(*refs):
    start, packed = 0, refs[-1]
    lanes = packed.shape[1]
    for ref in refs[:-1]:
        count, width = ref.shape
        if width == lanes:
            packed[start : start + count, :] = ref[...]
            start += count
        else:
            tall = packed.shape[0] - start
            half = tall // 2
            packed[start:, :width] = ref[:tall, :]
            packed[start : start + half, width:] = ref[tall : tall + half, : lanes - width]
            packed[start + half :, width:] = ref[tall : tall + half, lanes - width :]


def call(kernel, outs, scratch, cost, args, after=(), into=None, outside=()):
    args, after = list(args), list(after) + list(into or ())
    count, total = len(args), len(args) + len(after)
    size = sum(math.prod(a.shape) * a.dtype.itemsize for a in args + list(outs))
    first = total - len(into or ())
    return pl.pallas_call(
        lambda *refs: kernel(*refs[:count], *refs[total:]),
        out_shape=outs,
        in_specs=[
            pl.BlockSpec(memory_space=pl.ANY if index in outside else pltpu.VMEM) for index in range(count)
        ]
        + [pl.BlockSpec(memory_space=pl.ANY)] * len(after),
        out_specs=[pl.BlockSpec(memory_space=pltpu.VMEM if into is None else pl.ANY)] * len(outs),
        scratch_shapes=scratch,
        input_output_aliases={first + index: index for index in range(total - first)},
        compiler_params=pltpu.CompilerParams(vmem_limit_bytes=24 * 1024 * 1024),
        cost_estimate=pl.CostEstimate(flops=cost, bytes_accessed=size, transcendentals=0),
        name=getattr(kernel, "func", kernel).__name__,
    )(*args, *after)


def exchange(values, axis, size, mask):
    return lax.ppermute(values, axis, [(index, index ^ mask) for index in range(size)])


def pack(arrays, cost=0, after=(), rows=None):
    rows = rows or sum(array.shape[0] for array in arrays)
    shape = jax.ShapeDtypeStruct((rows, arrays[0].shape[1]), arrays[0].dtype)
    return call(pack_kernel, [shape], [], cost, arrays, after=after)[0]


def on_device(axes, state, accum, base_flow):
    grid, rows, levels = state.shape[-1] // 2, state.shape[3], state.shape[2]
    size = axes["ens"]
    if axes["pen"] != PEN or levels != 4 or grid != 256 or size != 8:
        return on_device_general(state, accum, base_flow)
    f32, bf16 = jnp.float32, jnp.bfloat16
    shape = functools.partial(jax.ShapeDtypeStruct, dtype=f32)
    fields, _, wide, tall = base_flow.shape
    lanes = 2 * wide
    base_lanes = fields * lanes
    table = jnp.asarray(np.concatenate([x_table(grid), y_forward_table(grid)]))
    y_table = y_inverse_table(grid)

    def near(values, mask):
        return exchange(values, "ens", size, mask)

    def across(values, mask):
        return exchange(values, ("ens", "pen"), size * PEN, mask * PEN + 1)

    own_base, swap_base = call(
        base_kernel, [shape((tall, base_lanes))] * 2, [], 0, [jnp.swapaxes(base_flow, 2, 3)]
    )
    own_far, swap_far = near(own_base, 6), across(swap_base, 6)
    message = tall + tall // 2 + 4 * NEAR_X + EXTRA
    swap_message, rows_message, far_message = call(
        near_kernel,
        [shape((message, 2 * grid)), shape((4, rows - NEAR_X, 2 * grid)), shape((EXTRA, 2 * grid))],
        [],
        0,
        [swap_base, state],
        after=[own_base],
    )
    near_rows = exchange(rows_message, "pen", PEN, 2)
    swap_near = across(pack([swap_base], after=[rows_message]), 2)
    came = exchange(swap_message, "pen", PEN, 1)
    far_rows = exchange(far_message, "pen", PEN, 3)
    swap_forward = near(pack([swap_far], HINT["forward"]), 2)
    own_forward = near(pack([own_far, own_base], HINT["forward"]), 2)
    own_parts = call(
        functools.partial(own_rows_kernel, grid),
        [shape((2, fields, rows, lanes))] * 2,
        [],
        HINT["own"],
        [state, table],
        after=[swap_far],
            )
    own_fields, swap_fields = call(
        functools.partial(inverse_kernel, grid),
        [shape((grid, base_lanes))] * 2,
        [
            pltpu.VMEM((2, 4 * rows, lanes), f32),
            pltpu.VMEM((2, grid, base_lanes), bf16),
            pltpu.VMEM((2, grid, base_lanes), bf16),
            pltpu.VMEM(y_table.shape[1:], bf16),
            pltpu.SemaphoreType.DMA,
        ],
        HINT["inverse"],
        [near_rows, far_rows, came, *own_parts, table, jnp.asarray(y_table)],
        outside=(6,),
    )
    places = (((0, 0), (6, 0), (6, 1), (2, 1)), ((4, 0), (2, 0), (4, 1), (0, 1)))
    packs = []
    for (blocks, cost, after), group in zip(
        (
            ([own_base, own_far, swap_far, swap_near], HINT["early"], ()),
            ([own_forward, swap_forward, came], HINT["pack"], ()),
        ),
        places,
        strict=True,
    ):
        packed = pack(blocks, cost, after, len(group) * tall)
        packs += [packed, near(packed, 1)]
    returns, made = [], []
    for field in range(2):
        messages = call(
            functools.partial(advection_kernel, places, field),
            [shape((2 * rows, 2 * lanes))] * PEN,
            [pltpu.VMEM((grid, 2 * lanes), bf16)] * 2,
            HINT["advect"][field],
            [own_fields, swap_fields, *packs, table],
        )
        made.append(messages[0])
        returns.append(
            [messages[0]] + [exchange(messages[step], "pen", PEN, step) for step in range(1, PEN)]
        )
    (part,) = call(
        functools.partial(linear_kernel, grid),
        [shape(state.shape)],
        [],
        HINT["linear"],
        [state, accum],
        after=made[1:],
    )
    result = ()
    for field, back in enumerate(returns):
        result = call(
            functools.partial(final_kernel, grid, field),
            [shape(state.shape)] * 2,
            [
                pltpu.VMEM((PEN, 2 * rows, 2 * lanes), f32),
                pltpu.VMEM((levels, rows, 2 * grid), f32),
                pltpu.VMEM((levels, rows, 2 * grid), f32),
                pltpu.SemaphoreType.DMA((2, levels)),
            ],
            0,
            [*back, state, part, table],
            into=result,
        )
    return tuple(result)


def solution(mesh):
    return jax.shard_map(
        functools.partial(on_device, dict(mesh.shape)),
        mesh=mesh,
        in_specs=(
            P(None, "ens", None, "pen", None),
            P(None, "ens", None, "pen", None),
            P(None, None, "pen", "ens"),
        ),
        out_specs=(P(None, "ens", None, "pen", None), P(None, "ens", None, "pen", None)),
        check_vma=False,
    )
```

```python
import functools
import math

import jax
import jax.numpy as jnp
import ml_dtypes
import numpy as np
from jax import lax
from jax.experimental import pallas as pl
from jax.experimental.pallas import tpu as pltpu
from jax.sharding import PartitionSpec as P

viscosity = 0.05
diffusivity = 0.05
vertical_mixing = 0.5
buoyancy_gain = 0.5
stratification = 0.5
memory_factor = -5.0 / 9.0
weight_factor = 15.0 / 16.0
time_step = 0.4


def wave_numbers(amount, offset, length):
    position = offset + jnp.arange(amount, dtype=jnp.int32)
    half_length = length // 2
    signed = jnp.where(position <= half_length, position, position - length)
    derivative = jnp.where(position == half_length, 0, signed)
    return (2.0 * math.pi / length * derivative.astype(jnp.float32), signed)


def times_i(real_part, imag_part, factor):
    return (-factor * imag_part, factor * real_part)


def vertical(quantity, level_axis):
    depth = quantity.shape[level_axis]
    lower = lax.slice_in_dim(quantity, 0, 1, axis=level_axis)
    upper = lax.slice_in_dim(quantity, depth - 1, depth, axis=level_axis)
    padded = jnp.concatenate([lower, quantity, upper], axis=level_axis)
    above = lax.slice_in_dim(padded, 2, depth + 2, axis=level_axis)
    below = lax.slice_in_dim(padded, 0, depth, axis=level_axis)
    return above + below - 2.0 * quantity


def tendency(vort, buoy, advect, across, kappa_x, square, level_axis):
    tend_vort_re = (
        -advect[0]
        + buoyancy_gain * (-kappa_x * buoy[1])
        - viscosity * square * vort[0]
        + vertical_mixing * vertical(vort[0], level_axis)
    )
    tend_vort_im = (
        -advect[1]
        + buoyancy_gain * (kappa_x * buoy[0])
        - viscosity * square * vort[1]
        + vertical_mixing * vertical(vort[1], level_axis)
    )
    tend_buoy_re = (
        -advect[2]
        - stratification * across[0]
        - diffusivity * square * buoy[0]
        + vertical_mixing * vertical(buoy[0], level_axis)
    )
    tend_buoy_im = (
        -advect[3]
        - stratification * across[1]
        - diffusivity * square * buoy[1]
        + vertical_mixing * vertical(buoy[1], level_axis)
    )
    return jnp.stack(
        [
            jnp.concatenate([tend_vort_re, tend_vort_im], axis=-1),
            jnp.concatenate([tend_buoy_re, tend_buoy_im], axis=-1),
        ]
    )


def dft_tables(length):
    position = jnp.arange(length, dtype=jnp.int32)
    product = position[:, None] * position[None, :] % length
    angle = 2.0 * math.pi / length * product.astype(jnp.float32)
    scale = 1.0 / math.sqrt(length)
    return (scale * jnp.cos(angle), scale * jnp.sin(angle))


def to_physical(spectral, x_table, y_table):
    mixed_space = jnp.einsum(
        "fplkj,jcx->fplcxk", spectral, x_table, precision=lax.Precision.HIGHEST
    )
    return jnp.einsum(
        "fplcxk,ckm->fplxm",
        lax.all_to_all(mixed_space, "pen", split_axis=4, concat_axis=5, tiled=True),
        y_table,
        precision=lax.Precision.HIGHEST,
    )


def on_device_general(state, accum, base_flow):
    grid_size = state.shape[-1] // 2
    row_count = state.shape[3]
    base_all = lax.all_gather(base_flow, "ens", axis=3, tiled=True)
    kappa_rows, signed_y = wave_numbers(row_count, lax.axis_index("pen") * row_count, grid_size)
    kappa_cols, signed_x = wave_numbers(grid_size, 0, grid_size)
    kappa_y = kappa_rows[:, None]
    kappa_x = kappa_cols[None, :]
    wave_square = signed_y[:, None] ** 2 + signed_x[None, :] ** 2
    factor = (2.0 * math.pi / grid_size) ** 2
    square = factor * wave_square.astype(jnp.float32)
    inverse = jnp.where(
        wave_square > 0, 1.0 / (factor * jnp.maximum(wave_square, 1).astype(jnp.float32)), 0.0
    )
    vort = (state[0][..., :grid_size], state[0][..., grid_size:])
    buoy = (state[1][..., :grid_size], state[1][..., grid_size:])
    potential_re = -vort[0] * inverse
    potential_im = -vort[1] * inverse
    flow_x = times_i(potential_re, potential_im, -kappa_y)
    flow_y = times_i(potential_re, potential_im, kappa_x)
    vort_x = times_i(vort[0], vort[1], kappa_x)
    vort_y = times_i(vort[0], vort[1], kappa_y)
    buoy_x = times_i(buoy[0], buoy[1], kappa_x)
    buoy_y = times_i(buoy[0], buoy[1], kappa_y)
    cosine_table, sine_table = dft_tables(grid_size)
    x_table = jnp.concatenate(
        [
            jnp.stack([cosine_table, sine_table], axis=1),
            jnp.stack([-sine_table, cosine_table], axis=1),
        ],
        axis=0,
    )
    y_table = jnp.stack([cosine_table, -sine_table])
    components = [flow_x, flow_y, vort_x, vort_y, buoy_x, buoy_y]
    spectral = jnp.stack([jnp.concatenate(component, axis=-1) for component in components])
    physical = to_physical(spectral, x_table, y_table)
    flow_x_p, flow_y_p = (physical[0], physical[1])
    vort_x_p, vort_y_p = (physical[2], physical[3])
    buoy_x_p, buoy_y_p = (physical[4], physical[5])
    advect_vort = (
        base_all[0] * vort_x_p
        + base_all[1] * vort_y_p
        + flow_x_p * base_all[2]
        + flow_y_p * base_all[3]
    )
    advect_buoy = (
        base_all[0] * buoy_x_p
        + base_all[1] * buoy_y_p
        + flow_x_p * base_all[4]
        + flow_y_p * base_all[5]
    )
    advect_both = jnp.stack([advect_vort, advect_buoy])
    y_forward = jnp.stack([cosine_table, -sine_table], axis=1)
    x_forward = jnp.stack(
        [
            jnp.concatenate([cosine_table, -sine_table], axis=1),
            jnp.concatenate([sine_table, cosine_table], axis=1),
        ]
    )
    spread = jnp.einsum(
        "fplxy,yck->fplckx", advect_both, y_forward, precision=lax.Precision.HIGHEST
    )
    spectra = jnp.einsum(
        "fplckx,cxm->fplkm",
        lax.all_to_all(spread, "pen", split_axis=4, concat_axis=5, tiled=True),
        x_forward,
        precision=lax.Precision.HIGHEST,
    )
    advect = (
        spectra[0][..., :grid_size],
        spectra[0][..., grid_size:],
        spectra[1][..., :grid_size],
        spectra[1][..., grid_size:],
    )
    tend = tendency(vort, buoy, advect, flow_y, kappa_x, square, 1)
    accum_next = memory_factor * accum + tend
    state_next = state + weight_factor * time_step * accum_next
    return (state_next, accum_next)


PEN = 4
EXTRA = 8
NEAR_X = 16
HINT = dict(inverse=10**10, forward=5 * 10**9)


def split(values):
    high = values.astype(jnp.bfloat16)
    return high, (values - high.astype(jnp.float32)).astype(jnp.bfloat16)


def split_table(values):
    high = values.astype(ml_dtypes.bfloat16)
    low = (values - high.astype(np.float64)).astype(ml_dtypes.bfloat16)
    return np.stack([high, low], axis=-3)


def cosine(grid, left, right):
    return np.cos(2.0 * np.pi / grid * (left * right % grid)) / math.sqrt(grid)


def sine(grid, left, right):
    return np.sin(2.0 * np.pi / grid * (left * right % grid)) / math.sqrt(grid)


def x_table(grid):
    kx = np.arange(grid)
    x = kx[:, None]
    return split_table(np.concatenate([cosine(grid, x, kx), sine(grid, x, kx)], axis=1))


def row_numbers(device, rows):
    own = device * rows + np.arange(rows)
    near = [(device ^ step) * rows + np.arange(count) for step, count in ((1, NEAR_X), (2, rows - NEAR_X))]
    return np.concatenate([own] + near)


def y_inverse_table(grid):
    rows = grid // PEN
    y = np.arange(grid)[:, None]
    tables = []
    for device in range(PEN):
        ky = row_numbers(device, rows)
        real = np.where(ky % (grid // 2) == 0, 1.0, 2.0) * cosine(grid, y, ky)
        imag = -2.0 * sine(grid, y, ky)
        extra = (device ^ 1) * rows + NEAR_X
        far = (device ^ 3) * rows
        from_y = rows + NEAR_X
        extra_real, extra_imag = 2.0 * cosine(grid, y[:, 0], extra), -2.0 * sine(grid, y[:, 0], extra)
        imag[:, from_y] = extra_imag
        if device % 2 == 0:
            imag[:, 0] = extra_real
        else:
            real[:, from_y] = extra_real
            imag[:, rows] = cosine(grid, y[:, 0], far)
        tables.append(np.concatenate([real, imag], axis=1))
    return split_table(np.stack(tables))


def y_forward_table(grid):
    rows = grid // PEN
    parts = []
    for device in range(PEN):
        ky = device * rows + np.arange(rows)[:, None]
        y = np.arange(grid)[None, :]
        parts += [cosine(grid, ky, y), -sine(grid, ky, y)]
    return split_table(np.concatenate([np.concatenate(parts[:4]), np.concatenate(parts[4:])], axis=1))


def dot(left, right):
    return jnp.dot(left, right, preferred_element_type=jnp.float32)


def dot_split(left, right):
    return dot(left[0], right[0]) + (dot(left[1], right[0]) + dot(left[0], right[1]))


def waves(position, grid):
    signed = jnp.where(position <= grid // 2, position, position - grid)
    derivative = jnp.where(position == grid // 2, 0, signed)
    return (2.0 * math.pi / grid) * derivative.astype(jnp.float32), signed


def wave_arrays(row_position, grid):
    kappa_y, signed_y = waves(row_position, grid)
    kappa_x, signed_x = waves(lax.broadcasted_iota(jnp.int32, (1, grid), 1), grid)
    wave_square = signed_y * signed_y + signed_x * signed_x
    factor = (2.0 * math.pi / grid) ** 2
    square = factor * wave_square.astype(jnp.float32)
    inverse = jnp.where(wave_square > 0, 1.0 / jnp.where(wave_square > 0, square, 1.0), 0.0)
    return kappa_y, kappa_x, square, inverse


def interleave(even, odd):
    low_lanes = lax.broadcasted_iota(jnp.int32, (1, 128), 1) < 64
    return (
        jnp.where(low_lanes, even, pltpu.roll(odd, 64, 1)),
        jnp.where(low_lanes, pltpu.roll(even, 64, 1), odd),
    )


def base_kernel(base_ref, own_ref, swap_ref):
    mine = (lax.axis_index("pen") % 2) * 2
    for out_ref, first in ((own_ref, mine), (swap_ref, 2 - mine)):
        for field in range(base_ref.shape[0]):
            out_ref[:, 128 * field : 128 * field + 128] = jnp.concatenate(
                [base_ref[field, first], base_ref[field, first + 1]], axis=1
            )


def near_kernel(block_ref, state_ref, swap_ref, near_ref, far_ref):
    mine = (lax.axis_index("pen") % 2) * 2
    width = swap_ref.shape[1]
    tall, lanes = block_ref.shape
    swap_ref[:tall, :] = block_ref[:, :width]
    half = tall // 2
    swap_ref[tall : tall + half, : lanes - width] = block_ref[:half, width:]
    swap_ref[tall : tall + half, lanes - width :] = block_ref[half:, width:]
    start = tall + half
    swap_ref[start + 4 * NEAR_X :, :] = jnp.zeros((EXTRA, width), jnp.float32)
    far_ref[...] = jnp.zeros_like(far_ref)
    for index in range(4):
        field, level = index // 2, index % 2
        rows = state_ref[field, 0, 2 - mine + level, : NEAR_X + EXTRA, :]
        swap_ref[start + NEAR_X * index : start + NEAR_X * (index + 1), :] = rows[:NEAR_X]
        line = start + 4 * NEAR_X + index
        swap_ref[line : line + 1, :] = rows[NEAR_X : NEAR_X + 1]
        far_ref[index : index + 1, :] = rows[:1]
        near_ref[index] = state_ref[field, 0, mine + level, : near_ref.shape[1], :]


def x_stage(grid, table, ky, held):
    count = held[0].shape[0]
    kappa_y, kappa_x, _, inverse = wave_arrays(ky, grid)
    fields = [
        (0, inverse, kappa_y),
        (0, -kappa_x * inverse, None),
        (0, kappa_x, None),
        (0, None, kappa_y),
        (1, kappa_x, None),
        (1, None, kappa_y),
    ]
    for field, before, after in fields:
        stacked = []
        for level in range(2):
            for columns in (slice(0, grid), slice(grid, 2 * grid)):
                values = held[2 * field + level][:, columns]
                stacked.append(values if before is None else values * before)
        product = dot_split(split(jnp.concatenate(stacked, axis=0)), table)
        results = []
        for level in range(2):
            top = product[2 * level * count : (2 * level + 1) * count]
            bottom = product[(2 * level + 1) * count : (2 * level + 2) * count]
            real = -(bottom[:, :128] + top[:, 128:])
            imag = top[:, :128] - bottom[:, 128:]
            results.append((real, imag) if after is None else (after * real, after * imag))
        yield results


def x_columns(grid, x_ref):
    start = pl.multiple_of((lax.axis_index("pen") // 2) * 128, 128)
    return [
        jnp.concatenate(
            [x_ref[part, :, pl.ds(start, 128)], x_ref[part, :, pl.ds(grid + start, 128)]], axis=1
        )
        for part in range(2)
    ]


def own_rows_kernel(grid, state_ref, x_ref, real_ref, imag_ref):
    rows = state_ref.shape[3]
    pen = lax.axis_index("pen")
    mine = (pen % 2) * 2
    held = [state_ref[field, 0, mine + level] for field in range(2) for level in range(2)]
    ky = pen * rows + lax.broadcasted_iota(jnp.int32, (rows, 1), 0)
    for number, results in enumerate(x_stage(grid, x_columns(grid, x_ref), ky, held)):
        for level, (real, imag) in enumerate(results):
            real_ref[level, number] = real
            imag_ref[level, number] = imag


def inverse_kernel(
    grid, near_ref, far_ref, came_ref, own_real, own_imag, x_ref, y_ref, own_ref, swap_ref, mixed, high_ref, low_ref, y_held, sem
):
    y_copy = pltpu.make_async_copy(y_ref.at[lax.axis_index("pen")], y_held, sem)
    y_copy.start()
    rows = own_real.shape[2]
    pen = lax.axis_index("pen")
    odd = pen % 2 == 1
    count = rows + EXTRA
    start = came_ref.shape[0] - 4 * NEAR_X - EXTRA
    held = [
        jnp.concatenate(
            [
                came_ref[start + NEAR_X * index : start + NEAR_X * (index + 1), :],
                near_ref[index],
                came_ref[start + 4 * NEAR_X + index : start + 4 * NEAR_X + index + 1, :],
                far_ref[index : index + 1, :],
                jnp.zeros((EXTRA - 2, 2 * grid), jnp.float32),
            ],
            axis=0,
        )
        for index in range(4)
    ]
    row = lax.broadcasted_iota(jnp.int32, (count, 1), 0)
    ky = jnp.where(row < NEAR_X, (pen ^ 1) * rows + row, (pen ^ 2) * rows + row - NEAR_X)
    ky = jnp.where(row == rows, (pen ^ 1) * rows + NEAR_X, ky)
    ky = jnp.where(row > rows, (pen ^ 3) * rows, ky)
    from_y = rows + NEAR_X
    for number, results in enumerate(x_stage(grid, x_columns(grid, x_ref), ky, held)):
        for level, (real, imag) in enumerate(results):
            first_imag = own_imag[level, number, 0:1, :]
            mixed[level, :rows, :] = own_real[level, number]
            mixed[level, rows : 2 * rows, :] = real[:rows]
            mixed[level, 2 * rows : 3 * rows, :] = own_imag[level, number]
            mixed[level, 3 * rows :, :] = imag[:rows]
            extra_real, extra_imag = real[rows : rows + 1], imag[rows : rows + 1]
            far_real = real[rows + 1 : rows + 2]
            mixed[level, from_y : from_y + 1, :] = jnp.where(
                odd, extra_real, real[NEAR_X : NEAR_X + 1]
            )
            mixed[level, 2 * rows : 2 * rows + 1, :] = jnp.where(odd, first_imag, extra_real)
            mixed[level, 3 * rows : 3 * rows + 1, :] = jnp.where(odd, far_real, imag[0:1])
            mixed[level, 2 * rows + from_y : 2 * rows + from_y + 1, :] = extra_imag
        for block, values in enumerate(interleave(mixed[0], mixed[1])):
            high, low = split(values)
            high_ref[block ^ (pen % 2), :, 128 * number : 128 * number + 128] = high
            low_ref[block ^ (pen % 2), :, 128 * number : 128 * number + 128] = low
    y_copy.wait()
    left = (y_held[0], y_held[1])
    own_ref[...] = dot_split(left, (high_ref[0], low_ref[0]))
    swap_ref[...] = dot_split(left, (high_ref[1], low_ref[1]))


def advection_kernel(places, field, own_ref, swap_ref, *refs):
    packs, (table_ref, *outs, high_ref, low_ref) = refs[:4], refs[4:]
    ens = lax.axis_index("ens")
    for group, which in [(group, which) for group in range(2) for which in range(2)]:
        pack_ref = packs[2 * group + which]
        tall = pack_ref.shape[0] // len(places[group])
        for slot, (offset, chunk) in enumerate(places[group]):
            place = pl.ds(pl.multiple_of((ens ^ offset ^ which) * tall, tall), tall)
            along_ref = (own_ref, swap_ref)[chunk]

            def base(index, pack_ref=pack_ref, slot=slot, tall=tall):
                return pack_ref[tall * slot : tall * (slot + 1), 128 * index : 128 * index + 128]

            def along(index, place=place, along_ref=along_ref):
                return along_ref[place, 128 * index : 128 * index + 128]

            first = 2 + 2 * field
            total = (
                base(0) * along(first)
                + base(1) * along(first + 1)
                + along(0) * base(first)
                + along(1) * base(first + 1)
            )
            lanes = slice(128 * chunk, 128 * chunk + 128)
            high_ref[place, lanes], low_ref[place, lanes] = split(total)
    pen = lax.axis_index("pen")
    grid = table_ref.shape[1]
    rows = grid // PEN
    for step in range(PEN):
        target = pen ^ step
        place = pl.ds(pl.multiple_of((target % 2) * 2 * rows, 2 * rows), 2 * rows)
        lanes = pl.ds(pl.multiple_of((target // 2) * grid, grid), grid)
        outs[step][...] = dot_split(
            (table_ref[2, place, lanes], table_ref[3, place, lanes]), (high_ref[...], low_ref[...])
        )


def linear_kernel(grid, state_ref, accum_ref, out_ref):
    rows, levels = state_ref.shape[3], state_ref.shape[2]
    row = lax.broadcasted_iota(jnp.int32, (rows, 1), 0)
    _, kappa_x, square, inverse = wave_arrays(lax.axis_index("pen") * rows + row, grid)
    real, imag = slice(0, grid), slice(grid, 2 * grid)
    for field in range(2):
        factor = kappa_x * buoyancy_gain if field == 0 else kappa_x * inverse * stratification
        damping = (viscosity if field == 0 else diffusivity) * square
        for level in range(levels):
            for columns, other, sign in ((real, imag, 1.0), (imag, real, -1.0)):
                here = state_ref[field, 0, level, :, columns]
                above = state_ref[field, 0, min(level + 1, levels - 1), :, columns]
                below = state_ref[field, 0, max(level - 1, 0), :, columns]
                out_ref[field, 0, level, :, columns] = (
                    memory_factor * accum_ref[field, 0, level, :, columns]
                    - sign * factor * state_ref[1 - field, 0, level, :, other]
                    - damping * here
                    + vertical_mixing * (above + below - 2.0 * here)
                )


def final_kernel(grid, field, *refs):
    messages, (state_ref, part_ref, table_ref) = refs[:PEN], refs[PEN : PEN + 3]
    state_out, accum_out, gathered, state_next, accum_next, sems = refs[-6:]
    rows, levels = state_ref.shape[3], state_ref.shape[2]
    pen = lax.axis_index("pen")
    for step in range(PEN):
        gathered[pen ^ step] = messages[step][...]
    table = (table_ref[0], table_ref[1])
    real, imag = slice(0, grid), slice(grid, 2 * grid)
    copies = []
    for pair in range(levels // 2):
        first, second = [slice(128 * chunk, 128 * chunk + 128) for chunk in (pair, 1 - pair)]
        halves = [
            interleave(gathered[pair + 2 * block, :, first], gathered[pair + 2 * block, :, second])
            for block in range(2)
        ]
        left = jnp.concatenate(
            [jnp.concatenate([half[level] for half in halves], axis=1) for level in range(2)], axis=0
        )
        product = dot_split(split(left), table)
        for level in (2 * pair, 2 * pair + 1):
            start = 2 * rows * (level - 2 * pair)
            top, bottom = product[start : start + rows], product[start + rows : start + 2 * rows]
            for columns, advect in (
                (real, top[:, :grid] + bottom[:, grid:]),
                (imag, bottom[:, :grid] - top[:, grid:]),
            ):
                memory = part_ref[field, 0, level, :, columns] - advect
                accum_next[level, :, columns] = memory
                state_next[level, :, columns] = (
                    state_ref[field, 0, level, :, columns] + weight_factor * time_step * memory
                )
            for which, (held, out) in enumerate(((state_next, state_out), (accum_next, accum_out))):
                copy = pltpu.make_async_copy(
                    held.at[level], out.at[field, 0, level], sems.at[which, level]
                )
                copy.start()
                copies.append(copy)
    for copy in copies:
        copy.wait()


def pack_kernel(*refs):
    start, packed = 0, refs[-1]
    lanes = packed.shape[1]
    for ref in refs[:-1]:
        count, width = ref.shape
        if width == lanes:
            packed[start : start + count, :] = ref[...]
            start += count
        else:
            tall = packed.shape[0] - start
            half = tall // 2
            packed[start:, :width] = ref[:tall, :]
            packed[start : start + half, width:] = ref[tall : tall + half, : lanes - width]
            packed[start + half :, width:] = ref[tall : tall + half, lanes - width :]


def call(kernel, outs, scratch, cost, args, after=(), into=None, outside=()):
    args, after = list(args), list(after) + list(into or ())
    count, total = len(args), len(args) + len(after)
    size = sum(math.prod(a.shape) * a.dtype.itemsize for a in args + list(outs))
    first = total - len(into or ())
    return pl.pallas_call(
        lambda *refs: kernel(*refs[:count], *refs[total:]),
        out_shape=outs,
        in_specs=[
            pl.BlockSpec(memory_space=pl.ANY if index in outside else pltpu.VMEM) for index in range(count)
        ]
        + [pl.BlockSpec(memory_space=pl.ANY)] * len(after),
        out_specs=[pl.BlockSpec(memory_space=pltpu.VMEM if into is None else pl.ANY)] * len(outs),
        scratch_shapes=scratch,
        input_output_aliases={first + index: index for index in range(total - first)},
        compiler_params=pltpu.CompilerParams(vmem_limit_bytes=24 * 1024 * 1024),
        cost_estimate=pl.CostEstimate(flops=cost, bytes_accessed=size, transcendentals=0),
        name=getattr(kernel, "func", kernel).__name__,
    )(*args, *after)


def exchange(values, axis, size, mask):
    return lax.ppermute(values, axis, [(index, index ^ mask) for index in range(size)])


def pack(arrays, cost=0, after=(), rows=None):
    rows = rows or sum(array.shape[0] for array in arrays)
    shape = jax.ShapeDtypeStruct((rows, arrays[0].shape[1]), arrays[0].dtype)
    return call(pack_kernel, [shape], [], cost, arrays, after=after)[0]


def on_device(axes, state, accum, base_flow):
    grid, rows, levels = state.shape[-1] // 2, state.shape[3], state.shape[2]
    size = axes["ens"]
    if axes["pen"] != PEN or levels != 4 or grid != 256 or size != 8:
        return on_device_general(state, accum, base_flow)
    f32, bf16 = jnp.float32, jnp.bfloat16
    shape = functools.partial(jax.ShapeDtypeStruct, dtype=f32)
    fields, _, wide, tall = base_flow.shape
    lanes = 2 * wide
    base_lanes = fields * lanes
    table = jnp.asarray(np.concatenate([x_table(grid), y_forward_table(grid)]))
    y_table = y_inverse_table(grid)

    def near(values, mask):
        return exchange(values, "ens", size, mask)

    def across(values, mask):
        return exchange(values, ("ens", "pen"), size * PEN, mask * PEN + 1)

    own_base, swap_base = call(
        base_kernel, [shape((tall, base_lanes))] * 2, [], 0, [jnp.swapaxes(base_flow, 2, 3)]
    )
    own_far, swap_far = near(own_base, 6), across(swap_base, 6)
    message = tall + tall // 2 + 4 * NEAR_X + EXTRA
    swap_message, rows_message, far_message = call(
        near_kernel,
        [shape((message, 2 * grid)), shape((4, rows - NEAR_X, 2 * grid)), shape((EXTRA, 2 * grid))],
        [],
        0,
        [swap_base, state],
        after=[own_base],
    )
    near_rows = exchange(rows_message, "pen", PEN, 2)
    swap_near = across(pack([swap_base], after=[rows_message]), 2)
    came = exchange(swap_message, "pen", PEN, 1)
    far_rows = exchange(far_message, "pen", PEN, 3)
    swap_forward = near(pack([swap_far], HINT["forward"]), 2)
    own_forward = near(pack([own_far, own_base], HINT["forward"]), 2)
    own_parts = call(
        functools.partial(own_rows_kernel, grid),
        [shape((2, fields, rows, lanes))] * 2,
        [],
        0,
        [state, table],
        after=[swap_far],
    )
    own_fields, swap_fields = call(
        functools.partial(inverse_kernel, grid),
        [shape((grid, base_lanes))] * 2,
        [
            pltpu.VMEM((2, 4 * rows, lanes), f32),
            pltpu.VMEM((2, grid, base_lanes), bf16),
            pltpu.VMEM((2, grid, base_lanes), bf16),
            pltpu.VMEM(y_table.shape[1:], bf16),
            pltpu.SemaphoreType.DMA,
        ],
        HINT["inverse"],
        [near_rows, far_rows, came, *own_parts, table, jnp.asarray(y_table)],
        outside=(6,),
    )
    places = (((0, 0), (6, 0), (6, 1), (2, 1)), ((4, 0), (2, 0), (4, 1), (0, 1)))
    packs = []
    for (blocks, cost, after), group in zip(
        (
            ([own_base, own_far, swap_far, swap_near], 0, ()),
            ([own_forward, swap_forward, came], 0, ()),
        ),
        places,
        strict=True,
    ):
        packed = pack(blocks, cost, after, len(group) * tall)
        packs += [packed, near(packed, 1)]
    returns, made = [], []
    for field in range(2):
        messages = call(
            functools.partial(advection_kernel, places, field),
            [shape((2 * rows, 2 * lanes))] * PEN,
            [pltpu.VMEM((grid, 2 * lanes), bf16)] * 2,
            0,
            [own_fields, swap_fields, *packs, table],
        )
        made.append(messages[0])
        returns.append(
            [messages[0]] + [exchange(messages[step], "pen", PEN, step) for step in range(1, PEN)]
        )
    (part,) = call(
        functools.partial(linear_kernel, grid),
        [shape(state.shape)],
        [],
        0,
        [state, accum],
        after=made[1:],
    )
    result = ()
    for field, back in enumerate(returns):
        result = call(
            functools.partial(final_kernel, grid, field),
            [shape(state.shape)] * 2,
            [
                pltpu.VMEM((PEN, 2 * rows, 2 * lanes), f32),
                pltpu.VMEM((levels, rows, 2 * grid), f32),
                pltpu.VMEM((levels, rows, 2 * grid), f32),
                pltpu.SemaphoreType.DMA((2, levels)),
            ],
            0,
            [*back, state, part, table],
            into=result,
        )
    return tuple(result)


def solution(mesh):
    return jax.shard_map(
        functools.partial(on_device, dict(mesh.shape)),
        mesh=mesh,
        in_specs=(
            P(None, "ens", None, "pen", None),
            P(None, "ens", None, "pen", None),
            P(None, None, "pen", "ens"),
        ),
        out_specs=(P(None, "ens", None, "pen", None), P(None, "ens", None, "pen", None)),
        check_vma=False,
    )
```

```python
import functools
import math

import jax
import jax.numpy as jnp
import ml_dtypes
import numpy as np
from jax import lax
from jax.experimental import pallas as pl
from jax.experimental.pallas import tpu as pltpu
from jax.sharding import PartitionSpec as P

viscosity = 0.05
diffusivity = 0.05
vertical_mixing = 0.5
buoyancy_gain = 0.5
stratification = 0.5
memory_factor = -5.0 / 9.0
weight_factor = 15.0 / 16.0
time_step = 0.4


def wave_numbers(amount, offset, length):
    position = offset + jnp.arange(amount, dtype=jnp.int32)
    half_length = length // 2
    signed = jnp.where(position <= half_length, position, position - length)
    derivative = jnp.where(position == half_length, 0, signed)
    return (2.0 * math.pi / length * derivative.astype(jnp.float32), signed)


def times_i(real_part, imag_part, factor):
    return (-factor * imag_part, factor * real_part)


def vertical(quantity, level_axis):
    depth = quantity.shape[level_axis]
    lower = lax.slice_in_dim(quantity, 0, 1, axis=level_axis)
    upper = lax.slice_in_dim(quantity, depth - 1, depth, axis=level_axis)
    padded = jnp.concatenate([lower, quantity, upper], axis=level_axis)
    above = lax.slice_in_dim(padded, 2, depth + 2, axis=level_axis)
    below = lax.slice_in_dim(padded, 0, depth, axis=level_axis)
    return above + below - 2.0 * quantity


def tendency(vort, buoy, advect, across, kappa_x, square, level_axis):
    tend_vort_re = (
        -advect[0]
        + buoyancy_gain * (-kappa_x * buoy[1])
        - viscosity * square * vort[0]
        + vertical_mixing * vertical(vort[0], level_axis)
    )
    tend_vort_im = (
        -advect[1]
        + buoyancy_gain * (kappa_x * buoy[0])
        - viscosity * square * vort[1]
        + vertical_mixing * vertical(vort[1], level_axis)
    )
    tend_buoy_re = (
        -advect[2]
        - stratification * across[0]
        - diffusivity * square * buoy[0]
        + vertical_mixing * vertical(buoy[0], level_axis)
    )
    tend_buoy_im = (
        -advect[3]
        - stratification * across[1]
        - diffusivity * square * buoy[1]
        + vertical_mixing * vertical(buoy[1], level_axis)
    )
    return jnp.stack(
        [
            jnp.concatenate([tend_vort_re, tend_vort_im], axis=-1),
            jnp.concatenate([tend_buoy_re, tend_buoy_im], axis=-1),
        ]
    )


def dft_tables(length):
    position = jnp.arange(length, dtype=jnp.int32)
    product = position[:, None] * position[None, :] % length
    angle = 2.0 * math.pi / length * product.astype(jnp.float32)
    scale = 1.0 / math.sqrt(length)
    return (scale * jnp.cos(angle), scale * jnp.sin(angle))


def to_physical(spectral, x_table, y_table):
    mixed_space = jnp.einsum(
        "fplkj,jcx->fplcxk", spectral, x_table, precision=lax.Precision.HIGHEST
    )
    return jnp.einsum(
        "fplcxk,ckm->fplxm",
        lax.all_to_all(mixed_space, "pen", split_axis=4, concat_axis=5, tiled=True),
        y_table,
        precision=lax.Precision.HIGHEST,
    )


def on_device_general(state, accum, base_flow):
    grid_size = state.shape[-1] // 2
    row_count = state.shape[3]
    base_all = lax.all_gather(base_flow, "ens", axis=3, tiled=True)
    kappa_rows, signed_y = wave_numbers(row_count, lax.axis_index("pen") * row_count, grid_size)
    kappa_cols, signed_x = wave_numbers(grid_size, 0, grid_size)
    kappa_y = kappa_rows[:, None]
    kappa_x = kappa_cols[None, :]
    wave_square = signed_y[:, None] ** 2 + signed_x[None, :] ** 2
    factor = (2.0 * math.pi / grid_size) ** 2
    square = factor * wave_square.astype(jnp.float32)
    inverse = jnp.where(
        wave_square > 0, 1.0 / (factor * jnp.maximum(wave_square, 1).astype(jnp.float32)), 0.0
    )
    vort = (state[0][..., :grid_size], state[0][..., grid_size:])
    buoy = (state[1][..., :grid_size], state[1][..., grid_size:])
    potential_re = -vort[0] * inverse
    potential_im = -vort[1] * inverse
    flow_x = times_i(potential_re, potential_im, -kappa_y)
    flow_y = times_i(potential_re, potential_im, kappa_x)
    vort_x = times_i(vort[0], vort[1], kappa_x)
    vort_y = times_i(vort[0], vort[1], kappa_y)
    buoy_x = times_i(buoy[0], buoy[1], kappa_x)
    buoy_y = times_i(buoy[0], buoy[1], kappa_y)
    cosine_table, sine_table = dft_tables(grid_size)
    x_table = jnp.concatenate(
        [
            jnp.stack([cosine_table, sine_table], axis=1),
            jnp.stack([-sine_table, cosine_table], axis=1),
        ],
        axis=0,
    )
    y_table = jnp.stack([cosine_table, -sine_table])
    components = [flow_x, flow_y, vort_x, vort_y, buoy_x, buoy_y]
    spectral = jnp.stack([jnp.concatenate(component, axis=-1) for component in components])
    physical = to_physical(spectral, x_table, y_table)
    flow_x_p, flow_y_p = (physical[0], physical[1])
    vort_x_p, vort_y_p = (physical[2], physical[3])
    buoy_x_p, buoy_y_p = (physical[4], physical[5])
    advect_vort = (
        base_all[0] * vort_x_p
        + base_all[1] * vort_y_p
        + flow_x_p * base_all[2]
        + flow_y_p * base_all[3]
    )
    advect_buoy = (
        base_all[0] * buoy_x_p
        + base_all[1] * buoy_y_p
        + flow_x_p * base_all[4]
        + flow_y_p * base_all[5]
    )
    advect_both = jnp.stack([advect_vort, advect_buoy])
    y_forward = jnp.stack([cosine_table, -sine_table], axis=1)
    x_forward = jnp.stack(
        [
            jnp.concatenate([cosine_table, -sine_table], axis=1),
            jnp.concatenate([sine_table, cosine_table], axis=1),
        ]
    )
    spread = jnp.einsum(
        "fplxy,yck->fplckx", advect_both, y_forward, precision=lax.Precision.HIGHEST
    )
    spectra = jnp.einsum(
        "fplckx,cxm->fplkm",
        lax.all_to_all(spread, "pen", split_axis=4, concat_axis=5, tiled=True),
        x_forward,
        precision=lax.Precision.HIGHEST,
    )
    advect = (
        spectra[0][..., :grid_size],
        spectra[0][..., grid_size:],
        spectra[1][..., :grid_size],
        spectra[1][..., grid_size:],
    )
    tend = tendency(vort, buoy, advect, flow_y, kappa_x, square, 1)
    accum_next = memory_factor * accum + tend
    state_next = state + weight_factor * time_step * accum_next
    return (state_next, accum_next)


PEN = 4
EXTRA = 8
NEAR_X = 8
HINT = dict(inverse=10**10, forward=5 * 10**9)


def split(values):
    high = values.astype(jnp.bfloat16)
    return high, (values - high.astype(jnp.float32)).astype(jnp.bfloat16)


def split_table(values):
    high = values.astype(ml_dtypes.bfloat16)
    low = (values - high.astype(np.float64)).astype(ml_dtypes.bfloat16)
    return np.stack([high, low], axis=-3)


def cosine(grid, left, right):
    return np.cos(2.0 * np.pi / grid * (left * right % grid)) / math.sqrt(grid)


def sine(grid, left, right):
    return np.sin(2.0 * np.pi / grid * (left * right % grid)) / math.sqrt(grid)


def x_table(grid):
    kx = np.arange(grid)
    x = kx[:, None]
    return split_table(np.concatenate([cosine(grid, x, kx), sine(grid, x, kx)], axis=1))


def row_numbers(device, rows):
    own = device * rows + np.arange(rows)
    near = [(device ^ step) * rows + np.arange(count) for step, count in ((1, NEAR_X), (2, rows - NEAR_X))]
    return np.concatenate([own] + near)


def y_inverse_table(grid):
    rows = grid // PEN
    y = np.arange(grid)[:, None]
    tables = []
    for device in range(PEN):
        ky = row_numbers(device, rows)
        real = np.where(ky % (grid // 2) == 0, 1.0, 2.0) * cosine(grid, y, ky)
        imag = -2.0 * sine(grid, y, ky)
        extra = (device ^ 1) * rows + NEAR_X
        far = (device ^ 3) * rows
        from_y = rows + NEAR_X
        extra_real, extra_imag = 2.0 * cosine(grid, y[:, 0], extra), -2.0 * sine(grid, y[:, 0], extra)
        imag[:, from_y] = extra_imag
        if device % 2 == 0:
            imag[:, 0] = extra_real
        else:
            real[:, from_y] = extra_real
            imag[:, rows] = cosine(grid, y[:, 0], far)
        tables.append(np.concatenate([real, imag], axis=1))
    return split_table(np.stack(tables))


def y_forward_table(grid):
    rows = grid // PEN
    parts = []
    for device in range(PEN):
        ky = device * rows + np.arange(rows)[:, None]
        y = np.arange(grid)[None, :]
        parts += [cosine(grid, ky, y), -sine(grid, ky, y)]
    return split_table(np.concatenate([np.concatenate(parts[:4]), np.concatenate(parts[4:])], axis=1))


def dot(left, right):
    return jnp.dot(left, right, preferred_element_type=jnp.float32)


def dot_split(left, right):
    return dot(left[0], right[0]) + (dot(left[1], right[0]) + dot(left[0], right[1]))


def waves(position, grid):
    signed = jnp.where(position <= grid // 2, position, position - grid)
    derivative = jnp.where(position == grid // 2, 0, signed)
    return (2.0 * math.pi / grid) * derivative.astype(jnp.float32), signed


def wave_arrays(row_position, grid):
    kappa_y, signed_y = waves(row_position, grid)
    kappa_x, signed_x = waves(lax.broadcasted_iota(jnp.int32, (1, grid), 1), grid)
    wave_square = signed_y * signed_y + signed_x * signed_x
    factor = (2.0 * math.pi / grid) ** 2
    square = factor * wave_square.astype(jnp.float32)
    inverse = jnp.where(wave_square > 0, 1.0 / jnp.where(wave_square > 0, square, 1.0), 0.0)
    return kappa_y, kappa_x, square, inverse


def interleave(even, odd):
    low_lanes = lax.broadcasted_iota(jnp.int32, (1, 128), 1) < 64
    return (
        jnp.where(low_lanes, even, pltpu.roll(odd, 64, 1)),
        jnp.where(low_lanes, pltpu.roll(even, 64, 1), odd),
    )


def base_kernel(base_ref, own_ref, swap_ref):
    mine = (lax.axis_index("pen") % 2) * 2
    for out_ref, first in ((own_ref, mine), (swap_ref, 2 - mine)):
        for field in range(base_ref.shape[0]):
            out_ref[:, 128 * field : 128 * field + 128] = jnp.concatenate(
                [base_ref[field, first], base_ref[field, first + 1]], axis=1
            )


def near_kernel(block_ref, state_ref, swap_ref, near_ref, far_ref):
    mine = (lax.axis_index("pen") % 2) * 2
    width = swap_ref.shape[1]
    tall, lanes = block_ref.shape
    swap_ref[:tall, :] = block_ref[:, :width]
    half = tall // 2
    swap_ref[tall : tall + half, : lanes - width] = block_ref[:half, width:]
    swap_ref[tall : tall + half, lanes - width :] = block_ref[half:, width:]
    start = tall + half
    swap_ref[start + 4 * NEAR_X :, :] = jnp.zeros((EXTRA, width), jnp.float32)
    far_ref[...] = jnp.zeros_like(far_ref)
    for index in range(4):
        field, level = index // 2, index % 2
        rows = state_ref[field, 0, 2 - mine + level, : NEAR_X + EXTRA, :]
        swap_ref[start + NEAR_X * index : start + NEAR_X * (index + 1), :] = rows[:NEAR_X]
        line = start + 4 * NEAR_X + index
        swap_ref[line : line + 1, :] = rows[NEAR_X : NEAR_X + 1]
        far_ref[index : index + 1, :] = rows[:1]
        near_ref[index] = state_ref[field, 0, mine + level, : near_ref.shape[1], :]


def x_stage(grid, table, ky, held):
    count = held[0].shape[0]
    kappa_y, kappa_x, _, inverse = wave_arrays(ky, grid)
    fields = [
        (0, inverse, kappa_y),
        (0, -kappa_x * inverse, None),
        (0, kappa_x, None),
        (0, None, kappa_y),
        (1, kappa_x, None),
        (1, None, kappa_y),
    ]
    for field, before, after in fields:
        stacked = []
        for level in range(2):
            for columns in (slice(0, grid), slice(grid, 2 * grid)):
                values = held[2 * field + level][:, columns]
                stacked.append(values if before is None else values * before)
        product = dot_split(split(jnp.concatenate(stacked, axis=0)), table)
        results = []
        for level in range(2):
            top = product[2 * level * count : (2 * level + 1) * count]
            bottom = product[(2 * level + 1) * count : (2 * level + 2) * count]
            real = -(bottom[:, :128] + top[:, 128:])
            imag = top[:, :128] - bottom[:, 128:]
            results.append((real, imag) if after is None else (after * real, after * imag))
        yield results


def x_columns(grid, x_ref):
    start = pl.multiple_of((lax.axis_index("pen") // 2) * 128, 128)
    return [
        jnp.concatenate(
            [x_ref[part, :, pl.ds(start, 128)], x_ref[part, :, pl.ds(grid + start, 128)]], axis=1
        )
        for part in range(2)
    ]


def own_rows_kernel(grid, state_ref, x_ref, real_ref, imag_ref):
    rows = state_ref.shape[3]
    pen = lax.axis_index("pen")
    mine = (pen % 2) * 2
    held = [state_ref[field, 0, mine + level] for field in range(2) for level in range(2)]
    ky = pen * rows + lax.broadcasted_iota(jnp.int32, (rows, 1), 0)
    for number, results in enumerate(x_stage(grid, x_columns(grid, x_ref), ky, held)):
        for level, (real, imag) in enumerate(results):
            real_ref[level, number] = real
            imag_ref[level, number] = imag


def inverse_kernel(
    grid, near_ref, far_ref, came_ref, own_real, own_imag, x_ref, y_ref, own_ref, swap_ref, mixed, high_ref, low_ref, y_held, sem
):
    y_copy = pltpu.make_async_copy(y_ref.at[lax.axis_index("pen")], y_held, sem)
    y_copy.start()
    rows = own_real.shape[2]
    pen = lax.axis_index("pen")
    odd = pen % 2 == 1
    count = rows + EXTRA
    start = came_ref.shape[0] - 4 * NEAR_X - EXTRA
    held = [
        jnp.concatenate(
            [
                came_ref[start + NEAR_X * index : start + NEAR_X * (index + 1), :],
                near_ref[index],
                came_ref[start + 4 * NEAR_X + index : start + 4 * NEAR_X + index + 1, :],
                far_ref[index : index + 1, :],
                jnp.zeros((EXTRA - 2, 2 * grid), jnp.float32),
            ],
            axis=0,
        )
        for index in range(4)
    ]
    row = lax.broadcasted_iota(jnp.int32, (count, 1), 0)
    ky = jnp.where(row < NEAR_X, (pen ^ 1) * rows + row, (pen ^ 2) * rows + row - NEAR_X)
    ky = jnp.where(row == rows, (pen ^ 1) * rows + NEAR_X, ky)
    ky = jnp.where(row > rows, (pen ^ 3) * rows, ky)
    from_y = rows + NEAR_X
    for number, results in enumerate(x_stage(grid, x_columns(grid, x_ref), ky, held)):
        for level, (real, imag) in enumerate(results):
            first_imag = own_imag[level, number, 0:1, :]
            mixed[level, :rows, :] = own_real[level, number]
            mixed[level, rows : 2 * rows, :] = real[:rows]
            mixed[level, 2 * rows : 3 * rows, :] = own_imag[level, number]
            mixed[level, 3 * rows :, :] = imag[:rows]
            extra_real, extra_imag = real[rows : rows + 1], imag[rows : rows + 1]
            far_real = real[rows + 1 : rows + 2]
            mixed[level, from_y : from_y + 1, :] = jnp.where(
                odd, extra_real, real[NEAR_X : NEAR_X + 1]
            )
            mixed[level, 2 * rows : 2 * rows + 1, :] = jnp.where(odd, first_imag, extra_real)
            mixed[level, 3 * rows : 3 * rows + 1, :] = jnp.where(odd, far_real, imag[0:1])
            mixed[level, 2 * rows + from_y : 2 * rows + from_y + 1, :] = extra_imag
        for block, values in enumerate(interleave(mixed[0], mixed[1])):
            high, low = split(values)
            high_ref[block ^ (pen % 2), :, 128 * number : 128 * number + 128] = high
            low_ref[block ^ (pen % 2), :, 128 * number : 128 * number + 128] = low
    y_copy.wait()
    left = (y_held[0], y_held[1])
    own_ref[...] = dot_split(left, (high_ref[0], low_ref[0]))
    swap_ref[...] = dot_split(left, (high_ref[1], low_ref[1]))


def advection_kernel(places, field, own_ref, swap_ref, *refs):
    packs, (table_ref, *outs, high_ref, low_ref) = refs[:4], refs[4:]
    ens = lax.axis_index("ens")
    for group, which in [(group, which) for group in range(2) for which in range(2)]:
        pack_ref = packs[2 * group + which]
        tall = pack_ref.shape[0] // len(places[group])
        for slot, (offset, chunk) in enumerate(places[group]):
            place = pl.ds(pl.multiple_of((ens ^ offset ^ which) * tall, tall), tall)
            along_ref = (own_ref, swap_ref)[chunk]

            def base(index, pack_ref=pack_ref, slot=slot, tall=tall):
                return pack_ref[tall * slot : tall * (slot + 1), 128 * index : 128 * index + 128]

            def along(index, place=place, along_ref=along_ref):
                return along_ref[place, 128 * index : 128 * index + 128]

            first = 2 + 2 * field
            total = (
                base(0) * along(first)
                + base(1) * along(first + 1)
                + along(0) * base(first)
                + along(1) * base(first + 1)
            )
            lanes = slice(128 * chunk, 128 * chunk + 128)
            high_ref[place, lanes], low_ref[place, lanes] = split(total)
    pen = lax.axis_index("pen")
    grid = table_ref.shape[1]
    rows = grid // PEN
    for step in range(PEN):
        target = pen ^ step
        place = pl.ds(pl.multiple_of((target % 2) * 2 * rows, 2 * rows), 2 * rows)
        lanes = pl.ds(pl.multiple_of((target // 2) * grid, grid), grid)
        outs[step][...] = dot_split(
            (table_ref[2, place, lanes], table_ref[3, place, lanes]), (high_ref[...], low_ref[...])
        )


def linear_kernel(grid, state_ref, accum_ref, out_ref):
    rows, levels = state_ref.shape[3], state_ref.shape[2]
    row = lax.broadcasted_iota(jnp.int32, (rows, 1), 0)
    _, kappa_x, square, inverse = wave_arrays(lax.axis_index("pen") * rows + row, grid)
    real, imag = slice(0, grid), slice(grid, 2 * grid)
    for field in range(2):
        factor = kappa_x * buoyancy_gain if field == 0 else kappa_x * inverse * stratification
        damping = (viscosity if field == 0 else diffusivity) * square
        for level in range(levels):
            for columns, other, sign in ((real, imag, 1.0), (imag, real, -1.0)):
                here = state_ref[field, 0, level, :, columns]
                above = state_ref[field, 0, min(level + 1, levels - 1), :, columns]
                below = state_ref[field, 0, max(level - 1, 0), :, columns]
                out_ref[field, 0, level, :, columns] = (
                    memory_factor * accum_ref[field, 0, level, :, columns]
                    - sign * factor * state_ref[1 - field, 0, level, :, other]
                    - damping * here
                    + vertical_mixing * (above + below - 2.0 * here)
                )


def final_kernel(grid, field, *refs):
    messages, (state_ref, part_ref, table_ref) = refs[:PEN], refs[PEN : PEN + 3]
    state_out, accum_out, gathered, state_next, accum_next, sems = refs[-6:]
    rows, levels = state_ref.shape[3], state_ref.shape[2]
    pen = lax.axis_index("pen")
    for step in range(PEN):
        gathered[pen ^ step] = messages[step][...]
    table = (table_ref[0], table_ref[1])
    real, imag = slice(0, grid), slice(grid, 2 * grid)
    copies = []
    for pair in range(levels // 2):
        first, second = [slice(128 * chunk, 128 * chunk + 128) for chunk in (pair, 1 - pair)]
        halves = [
            interleave(gathered[pair + 2 * block, :, first], gathered[pair + 2 * block, :, second])
            for block in range(2)
        ]
        left = jnp.concatenate(
            [jnp.concatenate([half[level] for half in halves], axis=1) for level in range(2)], axis=0
        )
        product = dot_split(split(left), table)
        for level in (2 * pair, 2 * pair + 1):
            start = 2 * rows * (level - 2 * pair)
            top, bottom = product[start : start + rows], product[start + rows : start + 2 * rows]
            for columns, advect in (
                (real, top[:, :grid] + bottom[:, grid:]),
                (imag, bottom[:, :grid] - top[:, grid:]),
            ):
                memory = part_ref[field, 0, level, :, columns] - advect
                accum_next[level, :, columns] = memory
                state_next[level, :, columns] = (
                    state_ref[field, 0, level, :, columns] + weight_factor * time_step * memory
                )
            for which, (held, out) in enumerate(((state_next, state_out), (accum_next, accum_out))):
                copy = pltpu.make_async_copy(
                    held.at[level], out.at[field, 0, level], sems.at[which, level]
                )
                copy.start()
                copies.append(copy)
    for copy in copies:
        copy.wait()


def pack_kernel(*refs):
    start, packed = 0, refs[-1]
    lanes = packed.shape[1]
    for ref in refs[:-1]:
        count, width = ref.shape
        if width == lanes:
            packed[start : start + count, :] = ref[...]
            start += count
        else:
            tall = packed.shape[0] - start
            half = tall // 2
            packed[start:, :width] = ref[:tall, :]
            packed[start : start + half, width:] = ref[tall : tall + half, : lanes - width]
            packed[start + half :, width:] = ref[tall : tall + half, lanes - width :]


def call(kernel, outs, scratch, cost, args, after=(), into=None, outside=()):
    args, after = list(args), list(after) + list(into or ())
    count, total = len(args), len(args) + len(after)
    size = sum(math.prod(a.shape) * a.dtype.itemsize for a in args + list(outs))
    first = total - len(into or ())
    return pl.pallas_call(
        lambda *refs: kernel(*refs[:count], *refs[total:]),
        out_shape=outs,
        in_specs=[
            pl.BlockSpec(memory_space=pl.ANY if index in outside else pltpu.VMEM) for index in range(count)
        ]
        + [pl.BlockSpec(memory_space=pl.ANY)] * len(after),
        out_specs=[pl.BlockSpec(memory_space=pltpu.VMEM if into is None else pl.ANY)] * len(outs),
        scratch_shapes=scratch,
        input_output_aliases={first + index: index for index in range(total - first)},
        compiler_params=pltpu.CompilerParams(vmem_limit_bytes=24 * 1024 * 1024),
        cost_estimate=pl.CostEstimate(flops=cost, bytes_accessed=size, transcendentals=0),
        name=getattr(kernel, "func", kernel).__name__,
    )(*args, *after)


def exchange(values, axis, size, mask):
    return lax.ppermute(values, axis, [(index, index ^ mask) for index in range(size)])


def pack(arrays, cost=0, after=(), rows=None):
    rows = rows or sum(array.shape[0] for array in arrays)
    shape = jax.ShapeDtypeStruct((rows, arrays[0].shape[1]), arrays[0].dtype)
    return call(pack_kernel, [shape], [], cost, arrays, after=after)[0]


def on_device(axes, state, accum, base_flow):
    grid, rows, levels = state.shape[-1] // 2, state.shape[3], state.shape[2]
    size = axes["ens"]
    if axes["pen"] != PEN or levels != 4 or grid != 256 or size != 8:
        return on_device_general(state, accum, base_flow)
    f32, bf16 = jnp.float32, jnp.bfloat16
    shape = functools.partial(jax.ShapeDtypeStruct, dtype=f32)
    fields, _, wide, tall = base_flow.shape
    lanes = 2 * wide
    base_lanes = fields * lanes
    table = jnp.asarray(np.concatenate([x_table(grid), y_forward_table(grid)]))
    y_table = y_inverse_table(grid)

    def near(values, mask):
        return exchange(values, "ens", size, mask)

    def across(values, mask):
        return exchange(values, ("ens", "pen"), size * PEN, mask * PEN + 1)

    own_base, swap_base = call(
        base_kernel, [shape((tall, base_lanes))] * 2, [], 0, [jnp.swapaxes(base_flow, 2, 3)]
    )
    own_far, swap_far = near(own_base, 6), across(swap_base, 6)
    message = tall + tall // 2 + 4 * NEAR_X + EXTRA
    swap_message, rows_message, far_message = call(
        near_kernel,
        [shape((message, 2 * grid)), shape((4, rows - NEAR_X, 2 * grid)), shape((EXTRA, 2 * grid))],
        [],
        0,
        [swap_base, state],
        after=[own_base],
    )
    near_rows = exchange(rows_message, "pen", PEN, 2)
    swap_near = across(pack([swap_base], after=[rows_message]), 2)
    came = exchange(swap_message, "pen", PEN, 1)
    far_rows = exchange(pack([far_message], after=[own_far]), "pen", PEN, 3)
    swap_forward = near(pack([swap_far], HINT["forward"]), 2)
    own_forward = near(pack([own_far, own_base], HINT["forward"]), 2)
    own_parts = call(
        functools.partial(own_rows_kernel, grid),
        [shape((2, fields, rows, lanes))] * 2,
        [],
        0,
        [state, table],
        after=[swap_far],
    )
    own_fields, swap_fields = call(
        functools.partial(inverse_kernel, grid),
        [shape((grid, base_lanes))] * 2,
        [
            pltpu.VMEM((2, 4 * rows, lanes), f32),
            pltpu.VMEM((2, grid, base_lanes), bf16),
            pltpu.VMEM((2, grid, base_lanes), bf16),
            pltpu.VMEM(y_table.shape[1:], bf16),
            pltpu.SemaphoreType.DMA,
        ],
        HINT["inverse"],
        [near_rows, far_rows, came, *own_parts, table, jnp.asarray(y_table)],
        outside=(6,),
    )
    places = (((0, 0), (6, 0), (6, 1), (2, 1)), ((4, 0), (2, 0), (4, 1), (0, 1)))
    packs = []
    for (blocks, cost, after), group in zip(
        (
            ([own_base, own_far, swap_far, swap_near], 0, ()),
            ([own_forward, swap_forward, came], 0, ()),
        ),
        places,
        strict=True,
    ):
        packed = pack(blocks, cost, after, len(group) * tall)
        packs += [packed, near(packed, 1)]
    returns, made = [], []
    for field in range(2):
        messages = call(
            functools.partial(advection_kernel, places, field),
            [shape((2 * rows, 2 * lanes))] * PEN,
            [pltpu.VMEM((grid, 2 * lanes), bf16)] * 2,
            0,
            [own_fields, swap_fields, *packs, table],
        )
        made.append(messages[0])
        returns.append(
            [messages[0]] + [exchange(messages[step], "pen", PEN, step) for step in range(1, PEN)]
        )
    (part,) = call(
        functools.partial(linear_kernel, grid),
        [shape(state.shape)],
        [],
        0,
        [state, accum],
        after=made[1:],
    )
    result = ()
    for field, back in enumerate(returns):
        result = call(
            functools.partial(final_kernel, grid, field),
            [shape(state.shape)] * 2,
            [
                pltpu.VMEM((PEN, 2 * rows, 2 * lanes), f32),
                pltpu.VMEM((levels, rows, 2 * grid), f32),
                pltpu.VMEM((levels, rows, 2 * grid), f32),
                pltpu.SemaphoreType.DMA((2, levels)),
            ],
            0,
            [*back, state, part, table],
            into=result,
        )
    return tuple(result)


def solution(mesh):
    return jax.shard_map(
        functools.partial(on_device, dict(mesh.shape)),
        mesh=mesh,
        in_specs=(
            P(None, "ens", None, "pen", None),
            P(None, "ens", None, "pen", None),
            P(None, None, "pen", "ens"),
        ),
        out_specs=(P(None, "ens", None, "pen", None), P(None, "ens", None, "pen", None)),
        check_vma=False,
    )
```

```python
import functools
import math

import jax
import jax.numpy as jnp
import ml_dtypes
import numpy as np
from jax import lax
from jax.experimental import pallas as pl
from jax.experimental.pallas import tpu as pltpu
from jax.sharding import PartitionSpec as P

viscosity = 0.05
diffusivity = 0.05
vertical_mixing = 0.5
buoyancy_gain = 0.5
stratification = 0.5
memory_factor = -5.0 / 9.0
weight_factor = 15.0 / 16.0
time_step = 0.4


def wave_numbers(amount, offset, length):
    position = offset + jnp.arange(amount, dtype=jnp.int32)
    half_length = length // 2
    signed = jnp.where(position <= half_length, position, position - length)
    derivative = jnp.where(position == half_length, 0, signed)
    return (2.0 * math.pi / length * derivative.astype(jnp.float32), signed)


def times_i(real_part, imag_part, factor):
    return (-factor * imag_part, factor * real_part)


def vertical(quantity, level_axis):
    depth = quantity.shape[level_axis]
    lower = lax.slice_in_dim(quantity, 0, 1, axis=level_axis)
    upper = lax.slice_in_dim(quantity, depth - 1, depth, axis=level_axis)
    padded = jnp.concatenate([lower, quantity, upper], axis=level_axis)
    above = lax.slice_in_dim(padded, 2, depth + 2, axis=level_axis)
    below = lax.slice_in_dim(padded, 0, depth, axis=level_axis)
    return above + below - 2.0 * quantity


def tendency(vort, buoy, advect, across, kappa_x, square, level_axis):
    tend_vort_re = (
        -advect[0]
        + buoyancy_gain * (-kappa_x * buoy[1])
        - viscosity * square * vort[0]
        + vertical_mixing * vertical(vort[0], level_axis)
    )
    tend_vort_im = (
        -advect[1]
        + buoyancy_gain * (kappa_x * buoy[0])
        - viscosity * square * vort[1]
        + vertical_mixing * vertical(vort[1], level_axis)
    )
    tend_buoy_re = (
        -advect[2]
        - stratification * across[0]
        - diffusivity * square * buoy[0]
        + vertical_mixing * vertical(buoy[0], level_axis)
    )
    tend_buoy_im = (
        -advect[3]
        - stratification * across[1]
        - diffusivity * square * buoy[1]
        + vertical_mixing * vertical(buoy[1], level_axis)
    )
    return jnp.stack(
        [
            jnp.concatenate([tend_vort_re, tend_vort_im], axis=-1),
            jnp.concatenate([tend_buoy_re, tend_buoy_im], axis=-1),
        ]
    )


def dft_tables(length):
    position = jnp.arange(length, dtype=jnp.int32)
    product = position[:, None] * position[None, :] % length
    angle = 2.0 * math.pi / length * product.astype(jnp.float32)
    scale = 1.0 / math.sqrt(length)
    return (scale * jnp.cos(angle), scale * jnp.sin(angle))


def to_physical(spectral, x_table, y_table):
    mixed_space = jnp.einsum(
        "fplkj,jcx->fplcxk", spectral, x_table, precision=lax.Precision.HIGHEST
    )
    return jnp.einsum(
        "fplcxk,ckm->fplxm",
        lax.all_to_all(mixed_space, "pen", split_axis=4, concat_axis=5, tiled=True),
        y_table,
        precision=lax.Precision.HIGHEST,
    )


def on_device_general(state, accum, base_flow):
    grid_size = state.shape[-1] // 2
    row_count = state.shape[3]
    base_all = lax.all_gather(base_flow, "ens", axis=3, tiled=True)
    kappa_rows, signed_y = wave_numbers(row_count, lax.axis_index("pen") * row_count, grid_size)
    kappa_cols, signed_x = wave_numbers(grid_size, 0, grid_size)
    kappa_y = kappa_rows[:, None]
    kappa_x = kappa_cols[None, :]
    wave_square = signed_y[:, None] ** 2 + signed_x[None, :] ** 2
    factor = (2.0 * math.pi / grid_size) ** 2
    square = factor * wave_square.astype(jnp.float32)
    inverse = jnp.where(
        wave_square > 0, 1.0 / (factor * jnp.maximum(wave_square, 1).astype(jnp.float32)), 0.0
    )
    vort = (state[0][..., :grid_size], state[0][..., grid_size:])
    buoy = (state[1][..., :grid_size], state[1][..., grid_size:])
    potential_re = -vort[0] * inverse
    potential_im = -vort[1] * inverse
    flow_x = times_i(potential_re, potential_im, -kappa_y)
    flow_y = times_i(potential_re, potential_im, kappa_x)
    vort_x = times_i(vort[0], vort[1], kappa_x)
    vort_y = times_i(vort[0], vort[1], kappa_y)
    buoy_x = times_i(buoy[0], buoy[1], kappa_x)
    buoy_y = times_i(buoy[0], buoy[1], kappa_y)
    cosine_table, sine_table = dft_tables(grid_size)
    x_table = jnp.concatenate(
        [
            jnp.stack([cosine_table, sine_table], axis=1),
            jnp.stack([-sine_table, cosine_table], axis=1),
        ],
        axis=0,
    )
    y_table = jnp.stack([cosine_table, -sine_table])
    components = [flow_x, flow_y, vort_x, vort_y, buoy_x, buoy_y]
    spectral = jnp.stack([jnp.concatenate(component, axis=-1) for component in components])
    physical = to_physical(spectral, x_table, y_table)
    flow_x_p, flow_y_p = (physical[0], physical[1])
    vort_x_p, vort_y_p = (physical[2], physical[3])
    buoy_x_p, buoy_y_p = (physical[4], physical[5])
    advect_vort = (
        base_all[0] * vort_x_p
        + base_all[1] * vort_y_p
        + flow_x_p * base_all[2]
        + flow_y_p * base_all[3]
    )
    advect_buoy = (
        base_all[0] * buoy_x_p
        + base_all[1] * buoy_y_p
        + flow_x_p * base_all[4]
        + flow_y_p * base_all[5]
    )
    advect_both = jnp.stack([advect_vort, advect_buoy])
    y_forward = jnp.stack([cosine_table, -sine_table], axis=1)
    x_forward = jnp.stack(
        [
            jnp.concatenate([cosine_table, -sine_table], axis=1),
            jnp.concatenate([sine_table, cosine_table], axis=1),
        ]
    )
    spread = jnp.einsum(
        "fplxy,yck->fplckx", advect_both, y_forward, precision=lax.Precision.HIGHEST
    )
    spectra = jnp.einsum(
        "fplckx,cxm->fplkm",
        lax.all_to_all(spread, "pen", split_axis=4, concat_axis=5, tiled=True),
        x_forward,
        precision=lax.Precision.HIGHEST,
    )
    advect = (
        spectra[0][..., :grid_size],
        spectra[0][..., grid_size:],
        spectra[1][..., :grid_size],
        spectra[1][..., grid_size:],
    )
    tend = tendency(vort, buoy, advect, flow_y, kappa_x, square, 1)
    accum_next = memory_factor * accum + tend
    state_next = state + weight_factor * time_step * accum_next
    return (state_next, accum_next)


PEN = 4
EXTRA = 8
NEAR_X = 8
HINT = dict(inverse=10**10, forward=5 * 10**9)


def split(values):
    high = values.astype(jnp.bfloat16)
    return high, (values - high.astype(jnp.float32)).astype(jnp.bfloat16)


def split_table(values):
    high = values.astype(ml_dtypes.bfloat16)
    low = (values - high.astype(np.float64)).astype(ml_dtypes.bfloat16)
    return np.stack([high, low], axis=-3)


def cosine(grid, left, right):
    return np.cos(2.0 * np.pi / grid * (left * right % grid)) / math.sqrt(grid)


def sine(grid, left, right):
    return np.sin(2.0 * np.pi / grid * (left * right % grid)) / math.sqrt(grid)


def x_table(grid):
    kx = np.arange(grid)
    x = kx[:, None]
    return split_table(np.concatenate([cosine(grid, x, kx), sine(grid, x, kx)], axis=1))


def row_numbers(device, rows):
    own = device * rows + np.arange(rows)
    near = [(device ^ step) * rows + np.arange(count) for step, count in ((1, NEAR_X), (2, rows - NEAR_X))]
    return np.concatenate([own] + near)


def y_inverse_table(grid):
    rows = grid // PEN
    y = np.arange(grid)[:, None]
    tables = []
    for device in range(PEN):
        ky = row_numbers(device, rows)
        real = np.where(ky % (grid // 2) == 0, 1.0, 2.0) * cosine(grid, y, ky)
        imag = -2.0 * sine(grid, y, ky)
        extra = (device ^ 1) * rows + NEAR_X
        far = (device ^ 3) * rows
        from_y = rows + NEAR_X
        extra_real, extra_imag = 2.0 * cosine(grid, y[:, 0], extra), -2.0 * sine(grid, y[:, 0], extra)
        imag[:, from_y] = extra_imag
        if device % 2 == 0:
            imag[:, 0] = extra_real
        else:
            real[:, from_y] = extra_real
            imag[:, rows] = cosine(grid, y[:, 0], far)
        tables.append(np.concatenate([real, imag], axis=1))
    return split_table(np.stack(tables))


def y_forward_table(grid):
    rows = grid // PEN
    parts = []
    for device in range(PEN):
        ky = device * rows + np.arange(rows)[:, None]
        y = np.arange(grid)[None, :]
        parts += [cosine(grid, ky, y), -sine(grid, ky, y)]
    return split_table(np.concatenate([np.concatenate(parts[:4]), np.concatenate(parts[4:])], axis=1))


def dot(left, right):
    return jnp.dot(left, right, preferred_element_type=jnp.float32)


def dot_split(left, right):
    return dot(left[0], right[0]) + (dot(left[1], right[0]) + dot(left[0], right[1]))


def waves(position, grid):
    signed = jnp.where(position <= grid // 2, position, position - grid)
    derivative = jnp.where(position == grid // 2, 0, signed)
    return (2.0 * math.pi / grid) * derivative.astype(jnp.float32), signed


def wave_arrays(row_position, grid):
    kappa_y, signed_y = waves(row_position, grid)
    kappa_x, signed_x = waves(lax.broadcasted_iota(jnp.int32, (1, grid), 1), grid)
    wave_square = signed_y * signed_y + signed_x * signed_x
    factor = (2.0 * math.pi / grid) ** 2
    square = factor * wave_square.astype(jnp.float32)
    inverse = jnp.where(wave_square > 0, 1.0 / jnp.where(wave_square > 0, square, 1.0), 0.0)
    return kappa_y, kappa_x, square, inverse


def interleave(even, odd):
    low_lanes = lax.broadcasted_iota(jnp.int32, (1, 128), 1) < 64
    return (
        jnp.where(low_lanes, even, pltpu.roll(odd, 64, 1)),
        jnp.where(low_lanes, pltpu.roll(even, 64, 1), odd),
    )


def base_kernel(base_ref, own_ref, swap_ref):
    mine = (lax.axis_index("pen") % 2) * 2
    for out_ref, first in ((own_ref, mine), (swap_ref, 2 - mine)):
        for field in range(base_ref.shape[0]):
            out_ref[:, 128 * field : 128 * field + 128] = jnp.concatenate(
                [base_ref[field, first], base_ref[field, first + 1]], axis=1
            )


def near_kernel(block_ref, state_ref, swap_ref, near_ref, far_ref):
    mine = (lax.axis_index("pen") % 2) * 2
    width = swap_ref.shape[1]
    tall, lanes = block_ref.shape
    swap_ref[:tall, :] = block_ref[:, :width]
    half = tall // 2
    swap_ref[tall : tall + half, : lanes - width] = block_ref[:half, width:]
    swap_ref[tall : tall + half, lanes - width :] = block_ref[half:, width:]
    start = tall + half
    swap_ref[start + 4 * NEAR_X :, :] = jnp.zeros((EXTRA, width), jnp.float32)
    far_ref[...] = jnp.zeros_like(far_ref)
    for index in range(4):
        field, level = index // 2, index % 2
        rows = state_ref[field, 0, 2 - mine + level, : NEAR_X + EXTRA, :]
        swap_ref[start + NEAR_X * index : start + NEAR_X * (index + 1), :] = rows[:NEAR_X]
        line = start + 4 * NEAR_X + index
        swap_ref[line : line + 1, :] = rows[NEAR_X : NEAR_X + 1]
        far_ref[index : index + 1, :] = rows[:1]
        near_ref[index] = state_ref[field, 0, mine + level, : near_ref.shape[1], :]


def x_stage(grid, table, ky, held):
    count = held[0].shape[0]
    kappa_y, kappa_x, _, inverse = wave_arrays(ky, grid)
    fields = [
        (0, inverse, kappa_y),
        (0, -kappa_x * inverse, None),
        (0, kappa_x, None),
        (0, None, kappa_y),
        (1, kappa_x, None),
        (1, None, kappa_y),
    ]
    for field, before, after in fields:
        stacked = []
        for level in range(2):
            for columns in (slice(0, grid), slice(grid, 2 * grid)):
                values = held[2 * field + level][:, columns]
                stacked.append(values if before is None else values * before)
        product = dot_split(split(jnp.concatenate(stacked, axis=0)), table)
        results = []
        for level in range(2):
            top = product[2 * level * count : (2 * level + 1) * count]
            bottom = product[(2 * level + 1) * count : (2 * level + 2) * count]
            real = -(bottom[:, :128] + top[:, 128:])
            imag = top[:, :128] - bottom[:, 128:]
            results.append((real, imag) if after is None else (after * real, after * imag))
        yield results


def x_columns(grid, x_ref):
    start = pl.multiple_of((lax.axis_index("pen") // 2) * 128, 128)
    return [
        jnp.concatenate(
            [x_ref[part, :, pl.ds(start, 128)], x_ref[part, :, pl.ds(grid + start, 128)]], axis=1
        )
        for part in range(2)
    ]


def own_rows_kernel(grid, state_ref, x_ref, real_ref, imag_ref):
    rows = state_ref.shape[3]
    pen = lax.axis_index("pen")
    mine = (pen % 2) * 2
    held = [state_ref[field, 0, mine + level] for field in range(2) for level in range(2)]
    ky = pen * rows + lax.broadcasted_iota(jnp.int32, (rows, 1), 0)
    for number, results in enumerate(x_stage(grid, x_columns(grid, x_ref), ky, held)):
        for level, (real, imag) in enumerate(results):
            real_ref[level, number] = real
            imag_ref[level, number] = imag


def inverse_kernel(
    grid, near_ref, far_ref, came_ref, own_real, own_imag, x_ref, y_ref, own_ref, swap_ref, mixed, high_ref, low_ref, y_held, sem
):
    y_copy = pltpu.make_async_copy(y_ref.at[lax.axis_index("pen")], y_held, sem)
    y_copy.start()
    rows = own_real.shape[2]
    pen = lax.axis_index("pen")
    odd = pen % 2 == 1
    count = rows + EXTRA
    start = came_ref.shape[0] - 4 * NEAR_X - EXTRA
    held = [
        jnp.concatenate(
            [
                came_ref[start + NEAR_X * index : start + NEAR_X * (index + 1), :],
                near_ref[index],
                came_ref[start + 4 * NEAR_X + index : start + 4 * NEAR_X + index + 1, :],
                far_ref[index : index + 1, :],
                jnp.zeros((EXTRA - 2, 2 * grid), jnp.float32),
            ],
            axis=0,
        )
        for index in range(4)
    ]
    row = lax.broadcasted_iota(jnp.int32, (count, 1), 0)
    ky = jnp.where(row < NEAR_X, (pen ^ 1) * rows + row, (pen ^ 2) * rows + row - NEAR_X)
    ky = jnp.where(row == rows, (pen ^ 1) * rows + NEAR_X, ky)
    ky = jnp.where(row > rows, (pen ^ 3) * rows, ky)
    from_y = rows + NEAR_X
    for number, results in enumerate(x_stage(grid, x_columns(grid, x_ref), ky, held)):
        for level, (real, imag) in enumerate(results):
            first_imag = own_imag[level, number, 0:1, :]
            mixed[level, :rows, :] = own_real[level, number]
            mixed[level, rows : 2 * rows, :] = real[:rows]
            mixed[level, 2 * rows : 3 * rows, :] = own_imag[level, number]
            mixed[level, 3 * rows :, :] = imag[:rows]
            extra_real, extra_imag = real[rows : rows + 1], imag[rows : rows + 1]
            far_real = real[rows + 1 : rows + 2]
            mixed[level, from_y : from_y + 1, :] = jnp.where(
                odd, extra_real, real[NEAR_X : NEAR_X + 1]
            )
            mixed[level, 2 * rows : 2 * rows + 1, :] = jnp.where(odd, first_imag, extra_real)
            mixed[level, 3 * rows : 3 * rows + 1, :] = jnp.where(odd, far_real, imag[0:1])
            mixed[level, 2 * rows + from_y : 2 * rows + from_y + 1, :] = extra_imag
        for block, values in enumerate(interleave(mixed[0], mixed[1])):
            high, low = split(values)
            high_ref[block ^ (pen % 2), :, 128 * number : 128 * number + 128] = high
            low_ref[block ^ (pen % 2), :, 128 * number : 128 * number + 128] = low
    y_copy.wait()
    left = (y_held[0], y_held[1])
    own_ref[...] = dot_split(left, (high_ref[0], low_ref[0]))
    swap_ref[...] = dot_split(left, (high_ref[1], low_ref[1]))


def advection_kernel(places, field, own_ref, swap_ref, *refs):
    packs, (table_ref, *outs, high_ref, low_ref) = refs[:4], refs[4:]
    ens = lax.axis_index("ens")
    for group, which in [(group, which) for group in range(2) for which in range(2)]:
        pack_ref = packs[2 * group + which]
        tall = pack_ref.shape[0] // len(places[group])
        for slot, (offset, chunk) in enumerate(places[group]):
            place = pl.ds(pl.multiple_of((ens ^ offset ^ which) * tall, tall), tall)
            along_ref = (own_ref, swap_ref)[chunk]

            def base(index, pack_ref=pack_ref, slot=slot, tall=tall):
                return pack_ref[tall * slot : tall * (slot + 1), 128 * index : 128 * index + 128]

            def along(index, place=place, along_ref=along_ref):
                return along_ref[place, 128 * index : 128 * index + 128]

            first = 2 + 2 * field
            total = (
                base(0) * along(first)
                + base(1) * along(first + 1)
                + along(0) * base(first)
                + along(1) * base(first + 1)
            )
            lanes = slice(128 * chunk, 128 * chunk + 128)
            high_ref[place, lanes], low_ref[place, lanes] = split(total)
    pen = lax.axis_index("pen")
    grid = table_ref.shape[1]
    rows = grid // PEN
    for step in range(PEN):
        target = pen ^ step
        place = pl.ds(pl.multiple_of((target % 2) * 2 * rows, 2 * rows), 2 * rows)
        lanes = pl.ds(pl.multiple_of((target // 2) * grid, grid), grid)
        outs[step][...] = dot_split(
            (table_ref[2, place, lanes], table_ref[3, place, lanes]), (high_ref[...], low_ref[...])
        )


def linear_kernel(grid, state_ref, accum_ref, out_ref):
    rows, levels = state_ref.shape[3], state_ref.shape[2]
    row = lax.broadcasted_iota(jnp.int32, (rows, 1), 0)
    _, kappa_x, square, inverse = wave_arrays(lax.axis_index("pen") * rows + row, grid)
    real, imag = slice(0, grid), slice(grid, 2 * grid)
    for field in range(2):
        factor = kappa_x * buoyancy_gain if field == 0 else kappa_x * inverse * stratification
        damping = (viscosity if field == 0 else diffusivity) * square
        for level in range(levels):
            for columns, other, sign in ((real, imag, 1.0), (imag, real, -1.0)):
                here = state_ref[field, 0, level, :, columns]
                above = state_ref[field, 0, min(level + 1, levels - 1), :, columns]
                below = state_ref[field, 0, max(level - 1, 0), :, columns]
                out_ref[field, 0, level, :, columns] = (
                    memory_factor * accum_ref[field, 0, level, :, columns]
                    - sign * factor * state_ref[1 - field, 0, level, :, other]
                    - damping * here
                    + vertical_mixing * (above + below - 2.0 * here)
                )


def final_kernel(grid, field, *refs):
    messages, (state_ref, part_ref, table_ref) = refs[:PEN], refs[PEN : PEN + 3]
    state_out, accum_out, gathered, state_next, accum_next, sems = refs[-6:]
    rows, levels = state_ref.shape[3], state_ref.shape[2]
    pen = lax.axis_index("pen")
    for step in range(PEN):
        gathered[pen ^ step] = messages[step][...]
    table = (table_ref[0], table_ref[1])
    real, imag = slice(0, grid), slice(grid, 2 * grid)
    copies = []
    for pair in range(levels // 2):
        first, second = [slice(128 * chunk, 128 * chunk + 128) for chunk in (pair, 1 - pair)]
        halves = [
            interleave(gathered[pair + 2 * block, :, first], gathered[pair + 2 * block, :, second])
            for block in range(2)
        ]
        for level in (2 * pair, 2 * pair + 1):
            left = jnp.concatenate([half[level - 2 * pair] for half in halves], axis=1)
            product, start = dot_split(split(left), table), 0
            top, bottom = product[start : start + rows], product[start + rows : start + 2 * rows]
            for columns, advect in (
                (real, top[:, :grid] + bottom[:, grid:]),
                (imag, bottom[:, :grid] - top[:, grid:]),
            ):
                memory = part_ref[field, 0, level, :, columns] - advect
                accum_next[level, :, columns] = memory
                state_next[level, :, columns] = (
                    state_ref[field, 0, level, :, columns] + weight_factor * time_step * memory
                )
            for which, (held, out) in enumerate(((state_next, state_out), (accum_next, accum_out))):
                copy = pltpu.make_async_copy(
                    held.at[level], out.at[field, 0, level], sems.at[which, level]
                )
                copy.start()
                copies.append(copy)
    for copy in copies:
        copy.wait()


def pack_kernel(*refs):
    start, packed = 0, refs[-1]
    lanes = packed.shape[1]
    for ref in refs[:-1]:
        count, width = ref.shape
        if width == lanes:
            packed[start : start + count, :] = ref[...]
            start += count
        else:
            tall = packed.shape[0] - start
            half = tall // 2
            packed[start:, :width] = ref[:tall, :]
            packed[start : start + half, width:] = ref[tall : tall + half, : lanes - width]
            packed[start + half :, width:] = ref[tall : tall + half, lanes - width :]


def call(kernel, outs, scratch, cost, args, after=(), into=None, outside=()):
    args, after = list(args), list(after) + list(into or ())
    count, total = len(args), len(args) + len(after)
    size = sum(math.prod(a.shape) * a.dtype.itemsize for a in args + list(outs))
    first = total - len(into or ())
    return pl.pallas_call(
        lambda *refs: kernel(*refs[:count], *refs[total:]),
        out_shape=outs,
        in_specs=[
            pl.BlockSpec(memory_space=pl.ANY if index in outside else pltpu.VMEM) for index in range(count)
        ]
        + [pl.BlockSpec(memory_space=pl.ANY)] * len(after),
        out_specs=[pl.BlockSpec(memory_space=pltpu.VMEM if into is None else pl.ANY)] * len(outs),
        scratch_shapes=scratch,
        input_output_aliases={first + index: index for index in range(total - first)},
        compiler_params=pltpu.CompilerParams(vmem_limit_bytes=24 * 1024 * 1024),
        cost_estimate=pl.CostEstimate(flops=cost, bytes_accessed=size, transcendentals=0),
        name=getattr(kernel, "func", kernel).__name__,
    )(*args, *after)


def exchange(values, axis, size, mask):
    return lax.ppermute(values, axis, [(index, index ^ mask) for index in range(size)])


def pack(arrays, cost=0, after=(), rows=None):
    rows = rows or sum(array.shape[0] for array in arrays)
    shape = jax.ShapeDtypeStruct((rows, arrays[0].shape[1]), arrays[0].dtype)
    return call(pack_kernel, [shape], [], cost, arrays, after=after)[0]


def on_device(axes, state, accum, base_flow):
    grid, rows, levels = state.shape[-1] // 2, state.shape[3], state.shape[2]
    size = axes["ens"]
    if axes["pen"] != PEN or levels != 4 or grid != 256 or size != 8:
        return on_device_general(state, accum, base_flow)
    f32, bf16 = jnp.float32, jnp.bfloat16
    shape = functools.partial(jax.ShapeDtypeStruct, dtype=f32)
    fields, _, wide, tall = base_flow.shape
    lanes = 2 * wide
    base_lanes = fields * lanes
    table = jnp.asarray(np.concatenate([x_table(grid), y_forward_table(grid)]))
    y_table = y_inverse_table(grid)

    def near(values, mask):
        return exchange(values, "ens", size, mask)

    def across(values, mask):
        return exchange(values, ("ens", "pen"), size * PEN, mask * PEN + 1)

    own_base, swap_base = call(
        base_kernel, [shape((tall, base_lanes))] * 2, [], 0, [jnp.swapaxes(base_flow, 2, 3)]
    )
    own_far, swap_far = near(own_base, 6), across(swap_base, 6)
    message = tall + tall // 2 + 4 * NEAR_X + EXTRA
    swap_message, rows_message, far_message = call(
        near_kernel,
        [shape((message, 2 * grid)), shape((4, rows - NEAR_X, 2 * grid)), shape((EXTRA, 2 * grid))],
        [],
        0,
        [swap_base, state],
        after=[own_base],
    )
    near_rows = exchange(rows_message, "pen", PEN, 2)
    swap_near = across(pack([swap_base], after=[rows_message]), 2)
    came = exchange(swap_message, "pen", PEN, 1)
    far_rows = exchange(pack([far_message], after=[own_far]), "pen", PEN, 3)
    swap_forward = near(pack([swap_far], HINT["forward"]), 2)
    own_forward = near(pack([own_far, own_base], HINT["forward"]), 2)
    own_parts = call(
        functools.partial(own_rows_kernel, grid),
        [shape((2, fields, rows, lanes))] * 2,
        [],
        0,
        [state, table],
        after=[swap_far],
    )
    own_fields, swap_fields = call(
        functools.partial(inverse_kernel, grid),
        [shape((grid, base_lanes))] * 2,
        [
            pltpu.VMEM((2, 4 * rows, lanes), f32),
            pltpu.VMEM((2, grid, base_lanes), bf16),
            pltpu.VMEM((2, grid, base_lanes), bf16),
            pltpu.VMEM(y_table.shape[1:], bf16),
            pltpu.SemaphoreType.DMA,
        ],
        HINT["inverse"],
        [near_rows, far_rows, came, *own_parts, table, jnp.asarray(y_table)],
        outside=(6,),
    )
    places = (((0, 0), (6, 0), (6, 1), (2, 1)), ((4, 0), (2, 0), (4, 1), (0, 1)))
    packs = []
    for (blocks, cost, after), group in zip(
        (
            ([own_base, own_far, swap_far, swap_near], 0, ()),
            ([own_forward, swap_forward, came], 0, ()),
        ),
        places,
        strict=True,
    ):
        packed = pack(blocks, cost, after, len(group) * tall)
        packs += [packed, near(packed, 1)]
    returns, made = [], []
    for field in range(2):
        messages = call(
            functools.partial(advection_kernel, places, field),
            [shape((2 * rows, 2 * lanes))] * PEN,
            [pltpu.VMEM((grid, 2 * lanes), bf16)] * 2,
            0,
            [own_fields, swap_fields, *packs, table],
        )
        made.append(messages[0])
        returns.append(
            [messages[0]] + [exchange(messages[step], "pen", PEN, step) for step in range(1, PEN)]
        )
    (part,) = call(
        functools.partial(linear_kernel, grid),
        [shape(state.shape)],
        [],
        0,
        [state, accum],
        after=made[1:],
    )
    result = ()
    for field, back in enumerate(returns):
        result = call(
            functools.partial(final_kernel, grid, field),
            [shape(state.shape)] * 2,
            [
                pltpu.VMEM((PEN, 2 * rows, 2 * lanes), f32),
                pltpu.VMEM((levels, rows, 2 * grid), f32),
                pltpu.VMEM((levels, rows, 2 * grid), f32),
                pltpu.SemaphoreType.DMA((2, levels)),
            ],
            0,
            [*back, state, part, table],
            into=result,
        )
    return tuple(result)


def solution(mesh):
    return jax.shard_map(
        functools.partial(on_device, dict(mesh.shape)),
        mesh=mesh,
        in_specs=(
            P(None, "ens", None, "pen", None),
            P(None, "ens", None, "pen", None),
            P(None, None, "pen", "ens"),
        ),
        out_specs=(P(None, "ens", None, "pen", None), P(None, "ens", None, "pen", None)),
        check_vma=False,
    )
```
